256 devices in a mesh: ctx: 16 (over y_lo, x, core), exp: 16 (over y_hi, z).
Axes of the slice: x: 4, y: 4 (y_hi: 2, y_lo: 2; y = y_hi * 2 + y_lo), z: 8, core: 2. Of those that a mesh axis runs over, the one named last changes fastest.
Arguments:
- query: bfloat16 [4096, 2048], P('ctx', 'exp'), may hold values from -8 to 8
- keys: bfloat16 [4096, 256], P('ctx'), may hold values from -8 to 8
- values: bfloat16 [4096, 256], P('ctx'), may hold values from -6 to 6
- out_proj: bfloat16 [2048, 2048], P('exp'), may hold values from -1.5 to 1.5
- residual: bfloat16 [4096, 2048], P(('ctx', 'exp')), may hold values from -4 to 4
- norm_gain: bfloat16 [2048], replicated, may hold values from 0.5 to 1.5
- expert_ids: int32 [4096, 8], P(('ctx', 'exp')), may hold values from 0 to 15, all different within a row; in each aligned block of 16 rows (0 to 15, 16 to 31, ...) at most 12 rows name the same one
- gate_values: bfloat16 [4096, 8], P(('ctx', 'exp')), may hold values from 0.049804688 to 0.44921875
- w_gate: bfloat16 [16, 2048, 768], P('exp'), may hold values from -0.125 to 0.125
- w_up: bfloat16 [16, 2048, 768], P('exp'), may hold values from -0.125 to 0.125
- w_down: bfloat16 [16, 768, 2048], P('exp'), may hold values from -0.21875 to 0.21875
Outputs:
- layer_out: bfloat16 [4096, 2048], P(('ctx', 'exp'))
The draws below stay inside these ranges and needn't reach their ends.
Inputs may be any that keep to these rules, and one draw needn't show every extreme that they name: `expert_ids`: each row names 8 different experts. Within each aligned block of 16 rows no expert is named by more than 12 rows, and in some blocks an expert is named by exactly 12 rows.
All inputs are finite; a program needn't handle non-finite values.
Results may differ from the reference program's by a relative error of at most 0.024.
Values may be sent and summed in bfloat16 or wider, within the bound.
No kernel may reach another device: no remote copies, remote signals or barrier semaphores. Data moves between devices by JAX's collectives and lax.ppermute only.
A program may use at most 64 MiB of HBM per device.

```python
import math
import jax
import jax.numpy as jnp
import numpy as np
from jax import lax

D = 2048
HEAD_DIM = 128
FF = 768
TOP = 8
HEADS = 16
KV_HEADS = 2
EXPERTS = 16
TOK_C = 256
TOK_DEV = 16
MOST_DEV = 12
SLOTS = 192
SEQ = 4096
N_CTX = 16


def draw_query(key, part):
    key = jax.random.fold_in(key, 1)
    shape = (SEQ, HEADS * HEAD_DIM)
    base = jnp.clip(jax.random.normal(key, shape, jnp.float32), -8.0, 8.0)
    return base.astype(jnp.bfloat16)


def draw_keys(key, part):
    key = jax.random.fold_in(key, 2)
    shape = (SEQ, KV_HEADS * HEAD_DIM)
    base = jnp.clip(jax.random.normal(key, shape, jnp.float32), -8.0, 8.0)
    return base.astype(jnp.bfloat16)


def block_levels(stream_key, extent, cuts, smallest, high):
    def one(axis_at, shards_of):
        heights = jax.random.uniform(jax.random.fold_in(jax.random.fold_in(stream_key, 6), axis_at), (shards_of,), jnp.float32, smallest / len(cuts), high / len(cuts))
        return jnp.repeat(jnp.exp(heights), extent[axis_at] // shards_of).reshape((-1,) + (1,) * (len(extent) - axis_at - 1))

    gain = one(*cuts[0])
    for cut in cuts[1:]:
        gain = gain * one(*cut)
    return gain


def routed_block(own_key, own, number, rows, amount, top, limit, lean):
    ranking = jax.random.permutation(own_key, amount)
    packed, ordinary = portions_of(amount, rows * top, limit, lean, True), portions_of(amount, rows * top, limit, lean, False)
    places = jnp.arange(amount)

    def named(tallies, rotation):
        used = int((tallies > 0).sum())
        fixed = max(1, used // 4)
        passed = fixed + (places - fixed + rotation * (used - fixed)) % max(1, amount - fixed)
        return jnp.zeros((amount,), jnp.int32).at[ranking[jnp.where(places < fixed, places, passed)]].set(jnp.asarray(tallies, jnp.int32))

    tallies = jnp.where(number % 4 == 0, named(packed, number // 4), named(ordinary, number - number // 4 - 1))
    mixed = jax.random.permutation(jax.random.fold_in(own, 3), amount)
    giver, taker = mixed[0:amount // 2 * 2:2], mixed[1:amount // 2 * 2:2]
    room = jnp.minimum(tallies[giver] - 1, limit - tallies[taker]) // 2
    room = jnp.where((giver == ranking[0]) | (taker == ranking[0]) | (tallies[taker] == 0), 0, jnp.maximum(room, 0))
    passed = jax.random.randint(jax.random.fold_in(own, 4), (amount // 2,), 0, 1 << 20) % (room + 1)
    tallies = tallies.at[giver].add(-passed).at[taker].add(passed)
    labels = jnp.searchsorted(jnp.cumsum(tallies), jnp.arange(rows * top), side="right").astype(jnp.int32)
    listing = labels.reshape(top, rows).T
    listing = listing[jax.random.permutation(jax.random.fold_in(own, 1), rows)]
    rotation = jax.random.randint(jax.random.fold_in(own, 2), (rows, 1), 0, top)
    return jnp.take_along_axis(listing, (jnp.arange(top)[None, :] + rotation) % top, axis=1)


def portions_of(number_of, total, limit, skew, full):
    loads = [(1 << 20) // math.isqrt(grade ** skew) + 1 for grade in range(1, number_of + 1)]
    largest = limit if full else min(limit, max(-(-total // number_of), total * loads[0] // sum(loads)))
    least = 1 if total - largest >= number_of - 1 else 0
    given, surplus = [largest] + [least] * (number_of - 1), total - largest - least * (number_of - 1)
    while surplus > 0:
        candidates = [i for i in range(1, number_of) if given[i] < largest] or [i for i in range(1, number_of) if given[i] < limit]
        whole, left = sum([loads[i] for i in candidates]), surplus
        for i in candidates:
            more = min(limit - given[i], max(1, left * loads[i] // whole), surplus)
            given[i] = given[i] + more
            surplus = surplus - more
    return np.array(given)


def scatter_about(stream_key, shape, scale, reach, pieces=(), kind=jnp.bfloat16):
    array = jax.random.normal(stream_key, shape, jnp.float32) * scale
    if len(pieces) > 0:
        array = block_levels(stream_key, shape, pieces, -0.22, 0.18) * array
    return jnp.clip(array, min=-reach, max=reach).astype(kind)


def setup_inputs(seed: int = 0) -> dict:
    streams_of = jax.random.split(jax.random.key(seed), 12)
    query = draw_query(jax.random.fold_in(streams_of[11], 71), 0)
    keys = draw_keys(jax.random.fold_in(streams_of[11], 71), 0)
    values = scatter_about(streams_of[2], (SEQ, KV_HEADS * HEAD_DIM), 1.0, 6.0, ((0, 16),))
    out_proj = scatter_about(streams_of[3], (HEADS * HEAD_DIM, D), (HEAD_DIM // 8) ** -0.5, 1.5, ((0, 16),))
    residual = scatter_about(streams_of[4], (SEQ, D), 0.5, 4.0, ((0, 256),))
    norm_gain = jnp.clip(1.0 + 0.1 * jax.random.normal(streams_of[5], (D,), jnp.float32), 0.5, 1.5).astype(jnp.bfloat16)
    expert_ids_keys = jax.random.split(jax.random.fold_in(streams_of[6], 1), SEQ // TOK_DEV)
    expert_ids_turns = jax.random.permutation(jax.random.fold_in(streams_of[6], 3), SEQ // TOK_DEV)
    expert_ids = jax.vmap(lambda own, number: routed_block(jax.random.fold_in(streams_of[6], 2), own, number, TOK_DEV, EXPERTS, TOP, MOST_DEV, 2))(expert_ids_keys, expert_ids_turns).reshape((SEQ, TOP))
    gate_values = jnp.clip(0.049804688 + 0.39941406 * jax.random.uniform(streams_of[7], (SEQ, TOP), jnp.float32) ** block_levels(streams_of[7], (SEQ, TOP), ((0, 256),), -0.2, 0.2), 0.049804688, 0.44921875).astype(jnp.bfloat16)
    w_gate = scatter_about(streams_of[8], (EXPERTS, D, FF), D ** -0.5, 0.125, ((0, 16),))
    w_up = scatter_about(streams_of[9], (EXPERTS, D, FF), D ** -0.5, 0.125, ((0, 16),))
    w_down = scatter_about(streams_of[10], (EXPERTS, FF, D), FF ** -0.5, 0.21875, ((0, 16),))
    return dict(query=query, keys=keys, values=values, out_proj=out_proj, residual=residual, norm_gain=norm_gain, expert_ids=expert_ids, gate_values=gate_values, w_gate=w_gate, w_up=w_up, w_down=w_down)


def slot_table(route_ids, route_gates, expert_list, capacity):
    row_count = route_ids.shape[0]
    expert_count = expert_list.shape[0]
    matches = route_ids[:, :, None] == expert_list[None, None, :]
    routed = jnp.any(matches, axis=1)
    weight = lax.optimization_barrier(jnp.sum(jnp.where(matches, route_gates[:, :, None].astype(jnp.float32), jnp.float32(0.0)), axis=1))
    position = jnp.cumsum(routed.astype(jnp.int32), axis=0) - 1
    offsets = jnp.arange(expert_count, dtype=jnp.int32)[None, :] * capacity
    target = jnp.where(routed, offsets + position, expert_count * capacity).astype(jnp.int32)
    row_numbers = jnp.broadcast_to(jnp.arange(row_count, dtype=jnp.int32)[:, None], (row_count, expert_count))
    slot_rows = jnp.zeros((expert_count * capacity,), jnp.int32).at[target.reshape(-1)].set(row_numbers.reshape(-1), mode='drop')
    slot_gates = jnp.zeros((expert_count * capacity,), jnp.float32).at[target.reshape(-1)].set(weight.reshape(-1), mode='drop')
    return (slot_rows.reshape(expert_count, capacity), slot_gates.reshape(expert_count, capacity))

def reference(query, keys, values, out_proj, residual, norm_gain, expert_ids, gate_values, w_gate, w_up, w_down):
    group = HEADS // KV_HEADS
    scale = 1.0 / math.sqrt(HEAD_DIM)
    queries = query.reshape(SEQ, HEADS, HEAD_DIM)
    key_heads = keys.reshape(SEQ, KV_HEADS, HEAD_DIM)
    value_heads = values.reshape(SEQ, KV_HEADS, HEAD_DIM)
    key_pos = jnp.arange(SEQ, dtype=jnp.int32)

    def one_head(head):
        head_queries = lax.dynamic_index_in_dim(queries, head, 1, keepdims=False)
        head_keys = lax.dynamic_index_in_dim(key_heads, head // group, 1, keepdims=False)
        head_values = lax.dynamic_index_in_dim(value_heads, head // group, 1, keepdims=False)

        def one_block(block):
            start = (block * TOK_C).astype(jnp.int32)
            block_queries = lax.dynamic_slice_in_dim(head_queries, start, TOK_C, 0)
            scores = jnp.dot(block_queries, head_keys.T, preferred_element_type=jnp.float32) * scale
            query_pos = start + jnp.arange(TOK_C, dtype=jnp.int32)
            allowed = key_pos[None, :] <= query_pos[:, None]
            scores = jnp.where(allowed, scores, jnp.float32(-1e+30))
            row_max = lax.optimization_barrier(jnp.max(scores, axis=1, keepdims=True))
            weights = jnp.where(allowed, jnp.exp(scores - row_max), jnp.float32(0.0))
            totals = lax.optimization_barrier(jnp.sum(weights, axis=1))
            mixed = jnp.dot(weights.astype(jnp.bfloat16), head_values, preferred_element_type=jnp.float32)
            return (mixed / totals[:, None]).astype(jnp.bfloat16)
        return lax.map(one_block, jnp.arange(N_CTX, dtype=jnp.int32))
    per_head = lax.map(one_head, jnp.arange(HEADS, dtype=jnp.int32))
    attn = per_head.reshape(HEADS, SEQ, HEAD_DIM).transpose(1, 0, 2).reshape(SEQ, HEADS * HEAD_DIM)
    projected = jnp.dot(attn, out_proj, preferred_element_type=jnp.float32)
    hidden_state = (residual.astype(jnp.float32) + projected).astype(jnp.bfloat16)
    hidden_wide = hidden_state.astype(jnp.float32)
    inverse = lax.rsqrt(lax.optimization_barrier(jnp.mean(hidden_wide * hidden_wide, axis=-1, keepdims=True)) + 1e-06)
    normed = (hidden_wide * inverse * norm_gain.astype(jnp.float32)).astype(jnp.bfloat16)
    gate_wide = w_gate.astype(jnp.float32)
    up_wide = w_up.astype(jnp.float32)
    down_wide = w_down.astype(jnp.float32)
    every_expert = jnp.arange(EXPERTS, dtype=jnp.int32)

    def moe_block(block):
        start = (block * TOK_C).astype(jnp.int32)
        rows = lax.dynamic_slice_in_dim(normed, start, TOK_C, 0)
        block_ids = lax.dynamic_slice_in_dim(expert_ids, start, TOK_C, 0)
        block_gates = lax.dynamic_slice_in_dim(gate_values, start, TOK_C, 0)
        slot_rows, slot_gates = slot_table(block_ids, block_gates, every_expert, SLOTS)
        picked = rows[slot_rows].astype(jnp.float32)
        gate_part = jnp.einsum('esd,edf->esf', picked, gate_wide)
        up_part = jnp.einsum('esd,edf->esf', picked, up_wide)
        inner = (jax.nn.silu(gate_part) * up_part).astype(jnp.bfloat16)
        outputs = jnp.einsum('esf,efd->esd', inner.astype(jnp.float32), down_wide).astype(jnp.bfloat16)
        weighted = slot_gates[:, :, None] * outputs.astype(jnp.float32)
        summed = jnp.zeros((TOK_C, D), jnp.float32).at[slot_rows.reshape(-1)].add(weighted.reshape(-1, D))
        return summed
    moe = lax.map(moe_block, jnp.arange(N_CTX, dtype=jnp.int32)).reshape(SEQ, D)
    return (hidden_wide + moe).astype(jnp.bfloat16)
```

```python
import math

import jax
import jax.numpy as jnp
from jax import lax
from jax.experimental import pallas as pl
from jax.experimental.pallas import tpu as pltpu
from jax.sharding import PartitionSpec as P

D = 2048
HEAD_DIM = 128
FF = 768
TOP = 8
HEADS = 16
KV_HEADS = 2
EXPERTS = 16
TOK_C = 256
TOK_DEV = 16
MOST_DEV = 12
N_CTX = 16
SLOTS = EXPERTS * MOST_DEV
NEGATIVE = -1e30

ROW_SWAP = [(i, i ^ 8) for i in range(16)]
CORE_SWAP = [(i, i ^ 1) for i in range(16)]


def x_shift(step):
    return [
        (y * 8 + x * 2 + c, y * 8 + (x + step) % 4 * 2 + c)
        for y in range(2)
        for x in range(4)
        for c in range(2)
    ]


def gather_blocks(block):
    me = lax.axis_index("ctx")
    row, x, core = me // 8, me // 2 % 4, me % 2
    other = lax.ppermute(block, "ctx", ROW_SWAP)
    pair = jnp.concatenate([block, other], axis=0)
    left = lax.ppermute(pair, "ctx", x_shift(1))
    right = lax.ppermute(pair, "ctx", x_shift(-1))
    half = block.shape[0]
    far_a = lax.ppermute(left[:half], "ctx", x_shift(1))
    far_b = lax.ppermute(right[half:], "ctx", x_shift(-1))
    mine = jnp.concatenate([pair, left, right, far_a, far_b], axis=0)
    theirs = lax.ppermute(mine, "ctx", CORE_SWAP)
    sources = []
    for c in (core, 1 - core):
        for dx in (0, -1, 1, 2):
            for r in (row, 1 - row):
                sources.append(r * 8 + (x + dx) % 4 * 2 + c)
    return jnp.concatenate([mine, theirs], axis=0), jnp.stack(sources)


def attention_kernel(query_ref, kv_ref, qpos_ref, kpos_ref, out_ref):
    scale = math.log2(math.e) / math.sqrt(HEAD_DIM)
    tile = 64

    def rows(i, _):
        at = pl.ds(pl.multiple_of(i * tile, tile), tile)
        scores = lax.dot_general(
            query_ref[at, :],
            kv_ref[:, :HEAD_DIM],
            (((1,), (1,)), ((), ())),
            preferred_element_type=jnp.float32,
        )
        allowed = kpos_ref[...] <= qpos_ref[at, :]
        scores = jnp.where(allowed, scores, jnp.float32(NEGATIVE))
        top = jnp.max(scores, axis=1, keepdims=True)
        weights = jnp.exp2((scores - top) * scale)
        total = jnp.sum(weights, axis=1, keepdims=True)
        mixed = jnp.dot(
            weights.astype(jnp.bfloat16), kv_ref[:, HEAD_DIM:], preferred_element_type=jnp.float32
        )
        out_ref[at, :] = (mixed / total).astype(jnp.bfloat16)
        return 0

    lax.fori_loop(0, query_ref.shape[0] // tile, rows, 0)


def attention(query, kv, query_pos, key_pos):
    rows, keys = query.shape[0], kv.shape[0]
    return pl.pallas_call(
        attention_kernel,
        out_shape=jax.ShapeDtypeStruct(query.shape, jnp.bfloat16),
        in_specs=[pl.BlockSpec(memory_space=pltpu.VMEM)] * 4,
        out_specs=pl.BlockSpec(memory_space=pltpu.VMEM),
        compiler_params=pltpu.CompilerParams(vmem_limit_bytes=32 * 1024 * 1024),
        cost_estimate=pl.CostEstimate(
            flops=4 * rows * keys * HEAD_DIM,
            bytes_accessed=keys * 2 * HEAD_DIM * 2,
            transcendentals=rows * keys,
        ),
    )(query, kv, query_pos.reshape(rows, 1), key_pos.reshape(1, keys))


def routing(ids, gates):
    named = ids[:, :, None] == jnp.arange(EXPERTS, dtype=jnp.int32)
    routed = jnp.any(named, axis=1)
    weight = jnp.sum(jnp.where(named, gates[:, :, None].astype(jnp.float32), 0.0), axis=1)
    position = jnp.cumsum(routed.astype(jnp.int32), axis=0) - 1
    place = position[:, :, None] == jnp.arange(MOST_DEV, dtype=jnp.int32)
    place = place & routed[:, :, None]
    pick = place.astype(jnp.bfloat16).reshape(ids.shape[0], SLOTS)
    mix = jnp.where(place, weight[:, :, None], 0.0).astype(jnp.bfloat16)
    return pick.T, mix.reshape(ids.shape[0], SLOTS)


def shards(
    query,
    keys,
    values,
    out_proj,
    residual,
    norm_gain,
    expert_ids,
    gate_values,
    w_gate,
    w_up,
    w_down,
):
    ctx_index = lax.axis_index("ctx")
    kv_index = lax.axis_index("exp") // (HEADS // KV_HEADS)
    block = jnp.concatenate(
        [
            lax.dynamic_slice_in_dim(keys, kv_index * HEAD_DIM, HEAD_DIM, 1),
            lax.dynamic_slice_in_dim(values, kv_index * HEAD_DIM, HEAD_DIM, 1),
        ],
        axis=1,
    )
    pick, mix = routing(expert_ids, gate_values)
    kv, sources = gather_blocks(block)
    offsets = jnp.arange(TOK_C, dtype=jnp.int32)
    key_pos = (sources[:, None] * TOK_C + offsets[None, :]).reshape(-1)
    attn = attention(query, kv, ctx_index * TOK_C + offsets, key_pos)
    partial = jnp.dot(attn, out_proj, preferred_element_type=jnp.float32).astype(jnp.bfloat16)
    parts = lax.all_to_all(partial, "exp", 0, 0, tiled=True)
    projected = jnp.sum(parts.reshape(16, TOK_DEV, D).astype(jnp.float32), axis=0)
    hidden_state = (residual.astype(jnp.float32) + projected).astype(jnp.bfloat16)
    hidden_wide = hidden_state.astype(jnp.float32)
    inverse = lax.rsqrt(jnp.mean(hidden_wide * hidden_wide, axis=-1, keepdims=True) + 1e-06)
    normed = (hidden_wide * inverse * norm_gain.astype(jnp.float32)).astype(jnp.bfloat16)
    sent = jnp.dot(pick, normed, preferred_element_type=jnp.float32).astype(jnp.bfloat16)
    rows = lax.all_to_all(sent, "exp", 0, 0, tiled=True)
    gate_part = jnp.dot(rows, w_gate[0], preferred_element_type=jnp.float32)
    up_part = jnp.dot(rows, w_up[0], preferred_element_type=jnp.float32)
    inner = (jax.nn.silu(gate_part) * up_part).astype(jnp.bfloat16)
    outputs = jnp.dot(inner, w_down[0], preferred_element_type=jnp.float32).astype(jnp.bfloat16)
    back = lax.all_to_all(outputs, "exp", 0, 0, tiled=True)
    moe = jnp.dot(mix, back, preferred_element_type=jnp.float32)
    return (hidden_wide + moe).astype(jnp.bfloat16)


def solution(mesh):
    return jax.shard_map(
        shards,
        mesh=mesh,
        in_specs=(
            P("ctx", "exp"),
            P("ctx", None),
            P("ctx", None),
            P("exp", None),
            P(("ctx", "exp"), None),
            P(),
            P(("ctx", "exp"), None),
            P(("ctx", "exp"), None),
            P("exp", None, None),
            P("exp", None, None),
            P("exp", None, None),
        ),
        out_specs=P(("ctx", "exp"), None),
        check_vma=False,
    )
```

```python
import math

import jax
import jax.numpy as jnp
from jax import lax
from jax.experimental import pallas as pl
from jax.experimental.pallas import tpu as pltpu
from jax.sharding import PartitionSpec as P

D = 2048
HEAD_DIM = 128
FF = 768
TOP = 8
HEADS = 16
KV_HEADS = 2
EXPERTS = 16
TOK_C = 256
TOK_DEV = 16
NEGATIVE = -1e30
SCALE = math.log2(math.e) / math.sqrt(HEAD_DIM)
F32 = jnp.float32
BF16 = jnp.bfloat16

ROW_SWAP = [(i, i ^ 8) for i in range(16)]
CORE_SWAP = [(i, i ^ 1) for i in range(16)]
Y_SWAP = [(i, i ^ 8) for i in range(16)]
Z_SWAP = [(i, i ^ 1) for i in range(16)]


def x_shift(step):
    return [
        (y * 8 + x * 2 + c, y * 8 + (x + step) % 4 * 2 + c)
        for y in range(2)
        for x in range(4)
        for c in range(2)
    ]


def z_shift(step):
    return [(y * 8 + z, y * 8 + (z + step) % 8) for y in range(2) for z in range(8)]


def on_ctx(block, route):
    return lax.ppermute(block, "ctx", route)


def on_exp(block, route):
    return lax.ppermute(block, "exp", route)


def kernel_call(body, ins, out_shapes, flops, transcendentals=0, scratch=(), scalars=0):
    size = sum(a.size * a.dtype.itemsize for a in ins)
    specs = [pl.BlockSpec(memory_space=pltpu.SMEM)] * scalars
    specs += [pl.BlockSpec(memory_space=pltpu.VMEM)] * (len(ins) - scalars)
    return pl.pallas_call(
        body,
        out_shape=out_shapes,
        in_specs=specs,
        out_specs=jax.tree.map(lambda _: pl.BlockSpec(memory_space=pltpu.VMEM), out_shapes),
        scratch_shapes=list(scratch),
        compiler_params=pltpu.CompilerParams(vmem_limit_bytes=32 * 1024 * 1024),
        cost_estimate=pl.CostEstimate(
            flops=flops, bytes_accessed=size, transcendentals=transcendentals
        ),
    )(*ins)


def struct(shape, dtype):
    return jax.ShapeDtypeStruct(shape, dtype)


def block_scores(queries, qpos, kv_refs, kpos_ref):
    parts = []
    for n, ref in enumerate(kv_refs):
        scores = lax.dot_general(
            queries, ref[:, :HEAD_DIM], (((1,), (1,)), ((), ())), preferred_element_type=F32
        )
        allowed = kpos_ref[:, n * TOK_C : (n + 1) * TOK_C] <= qpos
        parts.append(jnp.where(allowed, scores, F32(NEGATIVE)))
    return parts


def attend(queries, qpos, kv_refs, kpos_ref, state):
    parts = block_scores(queries, qpos, kv_refs, kpos_ref)
    top = jnp.max(parts[0], axis=1, keepdims=True)
    for part in parts[1:]:
        top = jnp.maximum(top, jnp.max(part, axis=1, keepdims=True))
    if state is not None:
        old_top = state[:, HEAD_DIM : HEAD_DIM + 1]
        old_total = state[:, HEAD_DIM + 64 : HEAD_DIM + 65]
        top = jnp.maximum(top, old_top)
        factor = jnp.exp2((old_top - top) * SCALE)
        total, mixed = old_total * factor, state[:, :HEAD_DIM] * factor
    else:
        total, mixed = 0.0, 0.0
    for part, ref in zip(parts, kv_refs):
        weights = jnp.exp2((part - top) * SCALE)
        total = total + jnp.sum(weights, axis=1, keepdims=True)
        mixed = mixed + jnp.dot(
            weights.astype(BF16), ref[:, HEAD_DIM:], preferred_element_type=F32
        )
    lane = lax.broadcasted_iota(jnp.int32, (queries.shape[0], HEAD_DIM), 1)
    return mixed, jnp.where(lane < 64, top, total)


ROWS_TILE = 64


def attend_first(mine_ref, theirs_ref, qpos_ref, kpos_ref, *refs):
    kv_refs, out_ref = refs[:4], refs[4]
    half = mine_ref.shape[0]
    for n, q_ref in enumerate((mine_ref, theirs_ref)):

        def rows(i, _, n=n, q_ref=q_ref):
            at = pl.ds(pl.multiple_of(i * ROWS_TILE, ROWS_TILE), ROWS_TILE)
            to = pl.ds(pl.multiple_of(n * half + i * ROWS_TILE, ROWS_TILE), ROWS_TILE)
            mixed, stats = attend(q_ref[at, :], qpos_ref[to, :], kv_refs, kpos_ref, None)
            out_ref[to, :HEAD_DIM] = mixed
            out_ref[to, HEAD_DIM:] = stats
            return 0

        lax.fori_loop(0, half // ROWS_TILE, rows, 0)


def attend_second(mine_ref, theirs_ref, qpos_ref, kpos_ref, state_ref, *refs):
    kv_refs, outs = refs[:4], refs[4:]
    half = mine_ref.shape[0]
    for n, q_ref in enumerate((mine_ref, theirs_ref)):

        def rows(i, _, n=n, q_ref=q_ref):
            at = pl.ds(pl.multiple_of(i * ROWS_TILE, ROWS_TILE), ROWS_TILE)
            to = pl.ds(pl.multiple_of(n * half + i * ROWS_TILE, ROWS_TILE), ROWS_TILE)
            mixed, stats = attend(
                q_ref[at, :], qpos_ref[to, :], kv_refs, kpos_ref, state_ref[to, :]
            )
            outs[n][at, :HEAD_DIM] = mixed
            outs[n][at, HEAD_DIM:] = stats
            return 0

        lax.fori_loop(0, half // ROWS_TILE, rows, 0)


def project(place_ref, own_ref, other_ref, w_own_ref, *refs):
    near, far = refs[:3], refs[3:6]
    keep_ref, send_ref = refs[6:8]
    core, parity = place_ref[0], place_ref[1]
    own_top = own_ref[:, HEAD_DIM : HEAD_DIM + 1]
    other_top = other_ref[:, HEAD_DIM : HEAD_DIM + 1]
    top = jnp.maximum(own_top, other_top)
    own_factor = jnp.exp2((own_top - top) * SCALE)
    other_factor = jnp.exp2((other_top - top) * SCALE)
    total = own_ref[:, HEAD_DIM + 64 : HEAD_DIM + 65] * own_factor
    total = total + other_ref[:, HEAD_DIM + 64 : HEAD_DIM + 65] * other_factor
    mixed = own_ref[:, :HEAD_DIM] * own_factor + other_ref[:, :HEAD_DIM] * other_factor
    attn = (mixed / total).astype(BF16)
    heads = [attn[n * 64 : (n + 1) * 64] for n in range(4)]
    width = D // 2
    for side, ws in ((core, near), (1 - core, far)):
        at = pl.ds(pl.multiple_of(side * width, width), width)
        sums = jnp.dot(heads[0], w_own_ref[:, at], preferred_element_type=F32)
        for n in range(3):
            sums = sums + jnp.dot(heads[n + 1], ws[n][...], preferred_element_type=F32)
        for y in range(2):
            low, high = sums[y * 32 : y * 32 + 16], sums[y * 32 + 16 : y * 32 + 32]
            rows = pl.ds(y * 16, 16)
            keep_ref[rows, at] = jnp.where(parity == 0, low, high)
            send_ref[rows, at] = jnp.where(parity == 0, high, low).astype(BF16)


def add_up(keep_ref, recv_ref, out_ref, send_ref):
    sums = keep_ref[...] + recv_ref[...].astype(F32)
    out_ref[...] = sums
    send_ref[...] = sums.astype(BF16)


def normalise(place_ref, sums_ref, recv_ref, own_ref, other_ref, gain_ref, hidden_ref, normed_ref):
    y = place_ref[2]
    for n in range(2):
        at = pl.ds(n * 16, 16)
        residual = jnp.where(y == n, own_ref[...].astype(F32), other_ref[...].astype(F32))
        projected = sums_ref[at, :] + recv_ref[at, :].astype(F32)
        hidden = (residual + projected).astype(BF16)
        wide = hidden.astype(F32)
        inverse = lax.rsqrt(jnp.mean(wide * wide, axis=-1, keepdims=True) + 1e-06)
        hidden_ref[at, :] = hidden
        normed_ref[at, :] = (wide * inverse * gain_ref[...].astype(F32)).astype(BF16)


def expert(*refs):
    count = (len(refs) - 3) // 2
    rows_refs, (gate_ref, up_ref, down_ref), outs = refs[:count], refs[count : count + 3], refs[count + 3 :]
    rows = jnp.concatenate([r[...] for r in rows_refs], axis=0)
    gate_part = jnp.dot(rows, gate_ref[...], preferred_element_type=F32)
    up_part = jnp.dot(rows, up_ref[...], preferred_element_type=F32)
    inner = (gate_part * jax.nn.sigmoid(gate_part) * up_part).astype(BF16)
    result = jnp.dot(inner, down_ref[...], preferred_element_type=F32).astype(BF16)
    start = 0
    for out in outs:
        out[...] = result[start : start + out.shape[0]]
        start += out.shape[0]


def run_expert(rows, w_gate, w_up, w_down):
    total = sum(r.shape[0] for r in rows)
    return kernel_call(
        expert,
        [*rows, w_gate, w_up, w_down],
        [struct(r.shape, BF16) for r in rows],
        6 * total * D * FF,
        total * FF,
    )


def weigh(place_ref, weights_ref, *refs):
    outs, (keep_ref, send_ref) = refs[:8], refs[8:]
    y = place_ref[2]
    sums = []
    for half in range(2):
        at = pl.ds(half * 16, 16)
        total = 0.0
        for n in range(8):
            total = total + weights_ref[at, n : n + 1] * outs[n][at, :].astype(F32)
        sums.append(total)
    keep_ref[...] = jnp.where(y == 0, sums[0], sums[1])
    send_ref[...] = jnp.where(y == 0, sums[1], sums[0]).astype(BF16)


def finish(place_ref, hidden_ref, keep_ref, recv_ref, out_ref):
    y = place_ref[2]
    hidden = jnp.where(y == 0, hidden_ref[:16, :].astype(F32), hidden_ref[16:, :].astype(F32))
    out_ref[...] = (hidden + (keep_ref[...] + recv_ref[...].astype(F32))).astype(BF16)


def router_weights(ids, gates):
    named = ids[:, :, None] == jnp.arange(EXPERTS, dtype=jnp.int32)
    weight = jnp.sum(jnp.where(named, gates[:, :, None].astype(F32), 0.0), axis=1)
    return jnp.pad(weight, ((0, 0), (0, 128 - EXPERTS)))


def shards(
    query,
    keys,
    values,
    out_proj,
    residual,
    norm_gain,
    expert_ids,
    gate_values,
    w_gate,
    w_up,
    w_down,
):
    ctx, exp = lax.axis_index("ctx"), lax.axis_index("exp")
    row, x, core = ctx // 8, ctx // 2 % 4, ctx % 2
    y, z = exp // 8, exp % 8
    place = jnp.stack([core, z % 2, y]).astype(jnp.int32)
    kv_index = exp // (HEADS // KV_HEADS)
    block = jnp.concatenate(
        [
            lax.dynamic_slice_in_dim(keys, kv_index * HEAD_DIM, HEAD_DIM, 1),
            lax.dynamic_slice_in_dim(values, kv_index * HEAD_DIM, HEAD_DIM, 1),
        ],
        axis=1,
    )

    other = on_ctx(block, ROW_SWAP)
    near = [block] + [on_ctx(block, x_shift(s)) for s in (1, -1, 2)]

    pairs = query.reshape(2, 4, 32, HEAD_DIM)

    def rows_for(step):
        to = (z + 2 * step) % 8 // 2
        return lax.dynamic_slice_in_dim(pairs, to, 1, 1).reshape(64, HEAD_DIM)

    mine = jnp.concatenate(
        [rows_for(0)] + [on_exp(rows_for(s), z_shift(2 * s)) for s in (1, 2, 3)], axis=0
    )
    theirs = on_ctx(mine, CORE_SWAP)

    far = [other] + [on_ctx(other, x_shift(s)) for s in (1, -1, 2)]

    w_half = lax.dynamic_slice_in_dim(out_proj, core * (D // 2), D // 2, 1)
    w_near = [on_exp(w_half, z_shift(2 * s)) for s in (1, 2, 3)]
    w_far = [on_ctx(w, CORE_SWAP) for w in w_near]
    res_other = on_exp(residual, Y_SWAP)
    own_weights = router_weights(expert_ids, gate_values)
    other_weights = on_exp(own_weights, Y_SWAP)

    offsets = jnp.arange(TOK_C, dtype=jnp.int32)
    token = jnp.arange(64, dtype=jnp.int32)
    token = token // 32 * 128 + z // 2 * 32 + token % 32
    local = jnp.tile(token, 4)
    query_pos = jnp.concatenate([ctx * TOK_C + local, (ctx ^ 1) * TOK_C + local]).reshape(512, 1)

    def key_pos(r):
        sources = jnp.stack([r * 8 + (x + s) % 4 * 2 + core for s in (0, -1, 1, 2)])
        return (sources[:, None] * TOK_C + offsets[None, :]).reshape(1, 4 * TOK_C)

    flops = 4 * 512 * 1024 * HEAD_DIM
    state = kernel_call(
        attend_first,
        [mine, theirs, query_pos, key_pos(row), *near],
        struct((512, 256), F32),
        flops,
        512 * 1024,
    )
    own, swap = kernel_call(
        attend_second,
        [mine, theirs, query_pos, key_pos(1 - row), state, *far],
        [struct((256, 256), F32)] * 2,
        flops,
        512 * 1024,
    )
    joined = on_ctx(swap, CORE_SWAP)
    keep, send = kernel_call(
        project,
        [place, own, joined, out_proj, *w_near, *w_far],
        [struct((32, D), F32), struct((32, D), BF16)],
        2 * 64 * 512 * D,
        scalars=1,
    )
    sums, send = kernel_call(
        add_up,
        [keep, on_exp(send, Z_SWAP)],
        [struct((32, D), F32), struct((32, D), BF16)],
        32 * D,
    )
    hidden, normed = kernel_call(
        normalise,
        [place, sums, on_exp(send, Y_SWAP), residual, res_other, norm_gain.reshape(1, D)],
        [struct((32, D), BF16)] * 2,
        8 * 32 * D,
        scalars=1,
    )

    w = (w_gate[0], w_up[0], w_down[0])
    up, down = [normed], [normed]
    for s in range(3):
        up.append(on_exp(up[-1], z_shift(1)))
        down.append(on_exp(down[-1], z_shift(-1)))
    last_up = on_exp(up[3][:16], z_shift(1))
    last_down = on_exp(down[3][16:], z_shift(-1))
    back = [None] * 8
    back[0] = run_expert([normed], *w)[0]
    for s in (1, 2, 3):
        from_up, from_down = run_expert([up[s], down[s]], *w)
        back[s] = on_exp(from_up, z_shift(-s))
        back[8 - s] = on_exp(from_down, z_shift(s))
    back[4] = on_exp(
        jnp.concatenate(run_expert([last_up, last_down], *w), axis=0), z_shift(4)
    )
    both = jnp.where(
        y == 0,
        jnp.concatenate([own_weights, other_weights], axis=0),
        jnp.concatenate([other_weights, own_weights], axis=0),
    )
    column = y * 8 + (z + jnp.arange(8)) % 8
    chosen = (jnp.arange(128)[:, None] == column[None, :]).astype(F32)
    weights = jnp.sum(both[:, :, None] * chosen[None], axis=1)
    keep, send = kernel_call(
        weigh,
        [place, weights, *back],
        [struct((16, D), F32), struct((16, D), BF16)],
        16 * 32 * D,
        scalars=1,
    )
    return kernel_call(
        finish,
        [place, hidden, keep, on_exp(send, Y_SWAP)],
        struct((16, D), BF16),
        3 * 16 * D,
        scalars=1,
    )


def solution(mesh):
    return jax.shard_map(
        shards,
        mesh=mesh,
        in_specs=(
            P("ctx", "exp"),
            P("ctx", None),
            P("ctx", None),
            P("exp", None),
            P(("ctx", "exp"), None),
            P(),
            P(("ctx", "exp"), None),
            P(("ctx", "exp"), None),
            P("exp", None, None),
            P("exp", None, None),
            P("exp", None, None),
        ),
        out_specs=P(("ctx", "exp"), None),
        check_vma=False,
    )
```

```python
import math

import jax
import jax.numpy as jnp
from jax import lax
from jax.experimental import pallas as pl
from jax.experimental.pallas import tpu as pltpu
from jax.sharding import PartitionSpec as P

D = 2048
HEAD_DIM = 128
FF = 768
TOP = 8
HEADS = 16
KV_HEADS = 2
EXPERTS = 16
TOK_C = 256
TOK_DEV = 16
NEGATIVE = -1e30
SCALE = math.log2(math.e) / math.sqrt(HEAD_DIM)
F32 = jnp.float32
BF16 = jnp.bfloat16

ROW_SWAP = [(i, i ^ 8) for i in range(16)]
CORE_SWAP = [(i, i ^ 1) for i in range(16)]
Y_SWAP = [(i, i ^ 8) for i in range(16)]
Z_SWAP = [(i, i ^ 1) for i in range(16)]


def x_shift(step):
    return [
        (y * 8 + x * 2 + c, y * 8 + (x + step) % 4 * 2 + c)
        for y in range(2)
        for x in range(4)
        for c in range(2)
    ]


def z_shift(step):
    return [(y * 8 + z, y * 8 + (z + step) % 8) for y in range(2) for z in range(8)]


def on_ctx(block, route):
    return lax.ppermute(block, "ctx", route)


def on_exp(block, route):
    return lax.ppermute(block, "exp", route)


def kernel_call(
    body, scalars, resident, fetched, out_shapes, flops, transcendentals=0, limit=16, idle=()
):
    ins = [*resident, *fetched, *idle]
    n_res, n_fetch = len(resident), len(fetched)
    n_out = len(jax.tree.leaves(out_shapes))

    def whole(*refs):
        place, refs = refs[0], refs[1:]
        sources = refs[n_res : n_res + n_fetch]
        outs = refs[len(ins) : len(ins) + n_out]
        buffers = refs[len(ins) + n_out : len(ins) + n_out + n_fetch]
        copies = []
        for n in range(n_fetch):
            copies.append(
                pltpu.make_async_copy(sources[n], buffers[n], refs[len(ins) + n_out + n_fetch + n])
            )
        for copy in copies:
            copy.start()
        body(place, refs[:n_res], buffers, outs, lambda n: copies[n].wait())

    size = sum(a.size * a.dtype.itemsize for a in [*resident, *fetched])
    vmem = pl.BlockSpec(memory_space=pltpu.VMEM)
    return pl.pallas_call(
        whole,
        out_shape=out_shapes,
        in_specs=[pl.BlockSpec(memory_space=pltpu.SMEM)]
        + [vmem] * n_res
        + [pl.BlockSpec(memory_space=pl.ANY)] * n_fetch
        + [vmem] * len(idle),
        out_specs=jax.tree.map(lambda _: vmem, out_shapes),
        scratch_shapes=[pltpu.VMEM(a.shape, a.dtype) for a in fetched]
        + [pltpu.SemaphoreType.DMA] * n_fetch,
        compiler_params=pltpu.CompilerParams(vmem_limit_bytes=limit * 1024 * 1024),
        cost_estimate=pl.CostEstimate(
            flops=flops, bytes_accessed=size, transcendentals=transcendentals
        ),
    )(scalars, *ins)


def struct(shape, dtype):
    return jax.ShapeDtypeStruct(shape, dtype)


def block_scores(queries, qpos, kv_refs, kpos_ref):
    parts = []
    for n, ref in enumerate(kv_refs):
        scores = lax.dot_general(
            queries, ref[:, :HEAD_DIM], (((1,), (1,)), ((), ())), preferred_element_type=F32
        )
        allowed = kpos_ref[:, n * TOK_C : (n + 1) * TOK_C] <= qpos
        parts.append(jnp.where(allowed, scores, F32(NEGATIVE)))
    return parts


def attend(queries, qpos, kv_refs, kpos_ref, state):
    parts = block_scores(queries, qpos, kv_refs, kpos_ref)
    top = jnp.max(parts[0], axis=1, keepdims=True)
    for part in parts[1:]:
        top = jnp.maximum(top, jnp.max(part, axis=1, keepdims=True))
    if state is not None:
        old_top = state[:, HEAD_DIM : HEAD_DIM + 1]
        old_total = state[:, HEAD_DIM + 64 : HEAD_DIM + 65]
        top = jnp.maximum(top, old_top)
        factor = jnp.exp2((old_top - top) * SCALE)
        total, mixed = old_total * factor, state[:, :HEAD_DIM] * factor
    else:
        total, mixed = 0.0, 0.0
    for part, ref in zip(parts, kv_refs):
        weights = jnp.exp2((part - top) * SCALE)
        total = total + jnp.sum(weights, axis=1, keepdims=True)
        mixed = mixed + jnp.dot(
            weights.astype(BF16), ref[:, HEAD_DIM:], preferred_element_type=F32
        )
    lane = lax.broadcasted_iota(jnp.int32, (queries.shape[0], HEAD_DIM), 1)
    return mixed, jnp.where(lane < 64, top, total)


ROWS_TILE = 64


def attend_all(place, resident, fetched, outs, wait):
    mine_ref, theirs_ref, qpos_ref, kpos_ref = resident[:4]
    state_ref = resident[4] if len(resident) > 4 else None
    half = mine_ref.shape[0]
    for n in range(4):
        wait(n)
    for n, q_ref in enumerate((mine_ref, theirs_ref)):

        def rows(i, _, n=n, q_ref=q_ref):
            at = pl.ds(pl.multiple_of(i * ROWS_TILE, ROWS_TILE), ROWS_TILE)
            to = pl.ds(pl.multiple_of(n * half + i * ROWS_TILE, ROWS_TILE), ROWS_TILE)
            state = None if state_ref is None else state_ref[to, :]
            mixed, stats = attend(q_ref[at, :], qpos_ref[to, :], fetched, kpos_ref, state)
            out_ref, into = (outs[0], to) if len(outs) == 1 else (outs[n], at)
            out_ref[into, :HEAD_DIM] = mixed
            out_ref[into, HEAD_DIM:] = stats
            return 0

        lax.fori_loop(0, half // ROWS_TILE, rows, 0)


def project(place, resident, fetched, outs, wait):
    own_ref, w_own_ref = resident
    other_ref, got_ref, swapped_ref, near_ref, far_ref = fetched
    keep_ref, keep_half_ref, send_ref = outs
    core, parity = place[0], place[1]
    wait(0)
    own_top = own_ref[:, HEAD_DIM : HEAD_DIM + 1]
    other_top = other_ref[:, HEAD_DIM : HEAD_DIM + 1]
    top = jnp.maximum(own_top, other_top)
    own_factor = jnp.exp2((own_top - top) * SCALE)
    other_factor = jnp.exp2((other_top - top) * SCALE)
    total = own_ref[:, HEAD_DIM + 64 : HEAD_DIM + 65] * own_factor
    total = total + other_ref[:, HEAD_DIM + 64 : HEAD_DIM + 65] * other_factor
    mixed = own_ref[:, :HEAD_DIM] * own_factor + other_ref[:, :HEAD_DIM] * other_factor
    attn = (mixed / total).astype(BF16)
    heads = [attn[n * 64 : (n + 1) * 64] for n in range(4)]
    got_head = jnp.where(core == 0, heads[1], heads[3])
    swapped_head = jnp.where(core == 0, heads[3], heads[1])
    for n in range(1, 5):
        wait(n)
    width = D // 2
    for side, quarter_ref in ((core, near_ref), (1 - core, far_ref)):
        at = pl.ds(pl.multiple_of(side * width, width), width)
        sums = jnp.dot(heads[0], w_own_ref[:, at], preferred_element_type=F32)
        sums = sums + jnp.dot(got_head, got_ref[:, at], preferred_element_type=F32)
        sums = sums + jnp.dot(swapped_head, swapped_ref[:, at], preferred_element_type=F32)
        sums = sums + jnp.dot(heads[2], quarter_ref[...], preferred_element_type=F32)
        for y in range(2):
            low, high = sums[y * 32 : y * 32 + 16], sums[y * 32 + 16 : y * 32 + 32]
            rows = pl.ds(y * 16, 16)
            keep = jnp.where(parity == 0, low, high)
            keep_ref[rows, at] = keep
            keep_half_ref[rows, at] = keep.astype(BF16)
            send_ref[rows, at] = jnp.where(parity == 0, high, low).astype(BF16)


def normalise(place, resident, fetched, outs, wait):
    own_ref, sums_ref, gain_ref = resident
    other_ref, *recv_refs = fetched
    hidden_ref, normed_ref, both_ref = outs
    y = place[2]
    for n in range(4):
        wait(n)
    for n in range(2):
        at = pl.ds(n * 16, 16)
        extended = jnp.where(y == n, own_ref[...].astype(F32), other_ref[...].astype(F32))
        projected = sums_ref[at, :]
        for ref in recv_refs:
            projected = projected + ref[at, :].astype(F32)
        hidden = (extended[:, :D] + projected).astype(BF16)
        wide = hidden.astype(F32)
        inverse = lax.rsqrt(jnp.mean(wide * wide, axis=-1, keepdims=True) + 1e-06)
        normed = (wide * inverse * gain_ref[...].astype(F32)).astype(BF16)
        hidden_ref[at, :] = hidden
        normed_ref[at, :] = normed
        both_ref[at, :D] = normed
        both_ref[at, D:] = extended[:, D:].astype(BF16)


def expert(place, resident, fetched, outs, wait):
    gate_ref, up_ref, down_ref = resident
    for n in range(len(fetched)):
        wait(n)
    rows = [ref[...] for ref in fetched]
    rows = rows[0] if len(rows) == 1 else jnp.concatenate(rows, axis=0)
    gate_part = jnp.dot(rows, gate_ref[...], preferred_element_type=F32)
    up_part = jnp.dot(rows, up_ref[...], preferred_element_type=F32)
    inner = (gate_part * jax.nn.sigmoid(gate_part) * up_part).astype(BF16)
    result = jnp.dot(inner, down_ref[...], preferred_element_type=F32).astype(BF16)
    start = 0
    for out in outs:
        out[...] = result[start : start + out.shape[0]]
        start += out.shape[0]


def run_expert(place, rows, weights):
    total = sum(r.shape[0] for r in rows)
    return kernel_call(
        expert,
        place,
        weights,
        rows,
        [struct(r.shape, BF16) for r in rows],
        6 * total * D * FF,
        total * FF,
    )


def weigh(place, resident, fetched, outs, wait):
    mine_ref, theirs_ref = resident
    far_ref, *near_refs, own_ref = fetched
    keep_ref, y_ref, core_ref, both_ref = outs
    core, y, z = place[0], place[2], place[3]
    lane = lax.broadcasted_iota(jnp.int32, (32, 128), 1)

    def column(ref, step):
        name = y * 8 + lax.rem(z + step, 8)
        return jnp.sum(jnp.where(lane == name, ref[...].astype(F32), 0.0), axis=1, keepdims=True)

    for n in range(5):
        wait(n)
    mine = column(mine_ref, 0) * own_ref[...].astype(F32)
    mine = mine + column(mine_ref, 4) * far_ref[...].astype(F32)
    theirs = 0.0
    for s in range(3):
        step = jnp.where(core == 0, s + 1, 7 - s)
        mine = mine + column(mine_ref, step) * near_refs[s][:32, :].astype(F32)
        theirs = theirs + column(theirs_ref, step) * near_refs[s][32:, :].astype(F32)
    keep_ref[...] = jnp.where(y == 0, mine[:16], mine[16:])
    y_ref[...] = jnp.where(y == 0, mine[16:], mine[:16]).astype(BF16)
    core_ref[...] = jnp.where(y == 0, theirs[:16], theirs[16:]).astype(BF16)
    both_ref[...] = jnp.where(y == 0, theirs[16:], theirs[:16]).astype(BF16)


def finish(place, resident, fetched, outs, wait):
    hidden_ref, keep_ref = resident
    hidden = jnp.where(
        place[2] == 0, hidden_ref[:16, :].astype(F32), hidden_ref[16:, :].astype(F32)
    )
    moe = keep_ref[...]
    for n in range(3):
        wait(n)
        moe = moe + fetched[n][...].astype(F32)
    outs[0][...] = (hidden + moe).astype(BF16)


def extend(place, resident, fetched, outs, wait):
    residual_ref, ids_ref, gates_ref = resident
    lane = lax.broadcasted_iota(jnp.int32, (TOK_DEV, 128), 1)
    weights = jnp.zeros((TOK_DEV, 128), F32)
    for k in range(TOP):
        gate = gates_ref[:, k : k + 1].astype(F32)
        weights = weights + jnp.where(lane == ids_ref[:, k : k + 1], gate, 0.0)
    outs[0][:, :D] = residual_ref[...]
    outs[0][:, D:] = weights.astype(BF16)


def by_core(step):
    route = []
    for c in range(16):
        way = step if c % 2 == 0 else -step
        for e in range(16):
            route.append((c * 16 + e, c * 16 + e // 8 * 8 + (e + way) % 8))
    return route


def on_both(block, route):
    return lax.ppermute(block, ("ctx", "exp"), route)


def two_swaps(ctx_bit, exp_bit):
    return [
        (c * 16 + e, (c ^ ctx_bit) * 16 + (e ^ exp_bit)) for c in range(16) for e in range(16)
    ]


def shards(
    query,
    keys,
    values,
    out_proj,
    residual,
    norm_gain,
    expert_ids,
    gate_values,
    w_gate,
    w_up,
    w_down,
):
    ctx, exp = lax.axis_index("ctx"), lax.axis_index("exp")
    row, x, core = ctx // 8, ctx // 2 % 4, ctx % 2
    y, z = exp // 8, exp % 8
    place = jnp.stack([core, z % 2, y, z]).astype(jnp.int32)
    kv_index = exp // (HEADS // KV_HEADS)
    block = jnp.concatenate(
        [
            lax.dynamic_slice_in_dim(keys, kv_index * HEAD_DIM, HEAD_DIM, 1),
            lax.dynamic_slice_in_dim(values, kv_index * HEAD_DIM, HEAD_DIM, 1),
        ],
        axis=1,
    )

    other = on_ctx(block, ROW_SWAP)
    near = [block] + [on_ctx(block, x_shift(s)) for s in (1, -1, 2)]

    pairs = query.reshape(2, 4, 32, HEAD_DIM)

    def rows_for(step):
        to = (z + 2 * step) % 8 // 2
        return lax.dynamic_slice_in_dim(pairs, to, 1, 1).reshape(64, HEAD_DIM)

    mine = jnp.concatenate(
        [rows_for(0)] + [on_exp(rows_for(s), z_shift(2 * s)) for s in (1, 2, 3)], axis=0
    )
    theirs = on_ctx(mine, CORE_SWAP)

    far = [other] + [on_ctx(other, x_shift(s)) for s in (1, -1, 2)]

    w_got = on_both(out_proj, by_core(2))
    w_swapped = on_ctx(w_got, CORE_SWAP)
    w_half = lax.dynamic_slice_in_dim(out_proj, core * (D // 2), D // 2, 1)
    w_near = on_exp(w_half, z_shift(4))
    w_far = on_ctx(w_near, CORE_SWAP)

    offsets = jnp.arange(TOK_C, dtype=jnp.int32)
    token = jnp.arange(64, dtype=jnp.int32)
    token = token // 32 * 128 + z // 2 * 32 + token % 32
    local = jnp.tile(token, 4)
    query_pos = jnp.concatenate([ctx * TOK_C + local, (ctx ^ 1) * TOK_C + local]).reshape(512, 1)

    def key_pos(r):
        sources = jnp.stack([r * 8 + (x + s) % 4 * 2 + core for s in (0, -1, 1, 2)])
        return (sources[:, None] * TOK_C + offsets[None, :]).reshape(1, 4 * TOK_C)

    flops = 4 * 512 * 1024 * HEAD_DIM
    (state,) = kernel_call(
        attend_all,
        place,
        [mine, theirs, query_pos, key_pos(row)],
        near,
        [struct((512, 256), F32)],
        flops,
        512 * 1024,
    )
    own, swap = kernel_call(
        attend_all,
        place,
        [mine, theirs, query_pos, key_pos(1 - row), state],
        far,
        [struct((256, 256), F32)] * 2,
        flops,
        512 * 1024,
    )
    joined = on_ctx(swap, CORE_SWAP)
    keep, keep_half, send = kernel_call(
        project,
        place,
        [own, out_proj],
        [joined, w_got, w_swapped, w_near, w_far],
        [struct((32, D), F32), struct((32, D), BF16), struct((32, D), BF16)],
        2 * 64 * 512 * D,
    )
    (extended,) = kernel_call(
        extend,
        place,
        [residual, expert_ids, gate_values],
        [],
        [struct((TOK_DEV, D + 128), BF16)],
        TOK_DEV * D,
    )
    extended, send = lax.optimization_barrier((extended, send))
    sums_y = on_exp(keep_half, Y_SWAP)
    sums_z = on_exp(send, Z_SWAP)
    sums_yz = on_exp(send, [(i, i ^ 9) for i in range(16)])
    extended_other = on_exp(extended, Y_SWAP)
    w = [w_gate[0], w_up[0], w_down[0]]
    hidden, normed, both = kernel_call(
        normalise,
        place,
        [extended, keep, norm_gain.reshape(1, D)],
        [extended_other, sums_z, sums_y, sums_yz],
        [struct((32, D), BF16), struct((32, D), BF16), struct((32, D + 128), BF16)],
        8 * 32 * D,
        idle=w,
    )

    opposite = on_exp(normed, z_shift(4))
    theirs_both = on_ctx(both, CORE_SWAP)
    ring = [jnp.concatenate([normed, theirs_both[:, :D]], axis=0)]
    for s in range(3):
        ring.append(on_both(ring[-1], by_core(1)))
    stay, opposite = run_expert(place, [normed, opposite], w)
    opposite = on_exp(opposite, z_shift(4))
    back = [
        on_both(run_expert(place, [ring[s]], w)[0], by_core(-s)) for s in (1, 2, 3)
    ]
    keep, to_y, to_core, to_both = kernel_call(
        weigh,
        place,
        [both[:, D:], theirs_both[:, D:]],
        [opposite, *back, stay],
        [struct((16, D), F32)] + [struct((16, D), BF16)] * 3,
        16 * 32 * D,
    )
    from_core = on_ctx(to_core, CORE_SWAP)
    from_y = on_exp(to_y, Y_SWAP)
    from_both = on_both(to_both, two_swaps(1, 8))
    return kernel_call(
        finish,
        place,
        [hidden, keep],
        [from_core, from_y, from_both],
        [struct((16, D), BF16)],
        3 * 16 * D,
    )[0]


def solution(mesh):
    return jax.shard_map(
        shards,
        mesh=mesh,
        in_specs=(
            P("ctx", "exp"),
            P("ctx", None),
            P("ctx", None),
            P("exp", None),
            P(("ctx", "exp"), None),
            P(),
            P(("ctx", "exp"), None),
            P(("ctx", "exp"), None),
            P("exp", None, None),
            P("exp", None, None),
            P("exp", None, None),
        ),
        out_specs=P(("ctx", "exp"), None),
        check_vma=False,
    )
```

```python
import math

import jax
import jax.numpy as jnp
from jax import lax
from jax.experimental import pallas as pl
from jax.experimental.pallas import tpu as pltpu
from jax.sharding import PartitionSpec as P

D = 2048
HEAD_DIM = 128
FF = 768
TOP = 8
HEADS = 16
KV_HEADS = 2
EXPERTS = 16
TOK_C = 256
TOK_DEV = 16
NEGATIVE = -1e30
SCALE = math.log2(math.e) / math.sqrt(HEAD_DIM)
F32 = jnp.float32
BF16 = jnp.bfloat16

CORE_SWAP = [(i, i ^ 1) for i in range(16)]
Y_SWAP = [(i, i ^ 8) for i in range(16)]


OTHER_ROW = [(i, i + 8) for i in range(8)]


def block_route(step):
    route = []
    for here in range(16):
        there = here // 8 * 8 + (here // 2 + step) % 4 * 2 + here % 2
        if here < there:
            route.append((here, there))
    return route


def relay_route(step):
    return [(8 + i, 8 + (i // 2 + step) % 4 * 2 + i % 2) for i in range(8)]


def z_shift(step):
    return [(y * 8 + z, y * 8 + (z + step) % 8) for y in range(2) for z in range(8)]


def on_ctx(block, route):
    return lax.ppermute(block, "ctx", route)


def on_exp(block, route):
    return lax.ppermute(block, "exp", route)


def kernel_call(
    body, scalars, resident, fetched, out_shapes, flops, transcendentals=0, limit=16, idle=(), scratch=()
):
    n_own = len(resident)
    resident, fetched = [*resident, *fetched], []
    ins = [*resident, *fetched, *idle]
    n_res, n_fetch = len(resident), len(fetched)
    n_out = len(jax.tree.leaves(out_shapes))

    def whole(*refs):
        place, refs = refs[0], refs[1:]
        sources = refs[n_res : n_res + n_fetch]
        outs = refs[len(ins) : len(ins) + n_out]
        buffers = refs[len(ins) + n_out : len(ins) + n_out + n_fetch]
        copies = []
        for n in range(n_fetch):
            copies.append(
                pltpu.make_async_copy(sources[n], buffers[n], refs[len(ins) + n_out + n_fetch + n])
            )
        for copy in copies:
            copy.start()
        extra = refs[len(ins) + n_out + 2 * n_fetch :]
        body(place, refs[:n_own], refs[n_own:n_res], (*outs, *extra), lambda n: None)

    size = sum(a.size * a.dtype.itemsize for a in [*resident, *fetched])
    vmem = pl.BlockSpec(memory_space=pltpu.VMEM)
    return pl.pallas_call(
        whole,
        out_shape=out_shapes,
        in_specs=[pl.BlockSpec(memory_space=pltpu.SMEM)]
        + [vmem] * n_res
        + [pl.BlockSpec(memory_space=pl.ANY)] * n_fetch
        + [vmem] * len(idle),
        out_specs=jax.tree.map(lambda _: vmem, out_shapes),
        scratch_shapes=[pltpu.VMEM(a.shape, a.dtype) for a in fetched]
        + [pltpu.SemaphoreType.DMA] * n_fetch
        + list(scratch),
        compiler_params=pltpu.CompilerParams(vmem_limit_bytes=limit * 1024 * 1024),
        cost_estimate=pl.CostEstimate(
            flops=flops, bytes_accessed=size, transcendentals=transcendentals
        ),
    )(scalars, *ins)


def after(value, *earlier):
    return lax.optimization_barrier((value, *earlier))


def struct(shape, dtype):
    return jax.ShapeDtypeStruct(shape, dtype)


ROWS_TILE = 256
PLACES = [(r, d) for r in (0, 1) for d in (0, -1, 1, 2)]


def attend_all(place, resident, fetched, outs, wait):
    core, y, z, ctx = place[0], place[1], place[2], place[3]
    row, x = ctx // 8, lax.rem(ctx // 2, 4)
    sources = [(row ^ r) * 8 + lax.rem(x + d + 4, 4) * 2 + core for r, d in PLACES]
    half = resident[0].shape[0]
    for n in range(8):
        wait(n)
    token = lax.broadcasted_iota(jnp.int32, (ROWS_TILE, 1), 0) & 127
    part = token >> 4
    key = lax.broadcasted_iota(jnp.int32, (1, TOK_C), 1)
    lane = lax.broadcasted_iota(jnp.int32, (ROWS_TILE, HEAD_DIM), 1)
    for n, q_ref in enumerate(resident):
        q_ctx = ctx ^ n
        first = z + 7 - (core ^ n)
        local = (part >> 2) * 128 + (((part & 3) + first) & 7) * 16 + (token & 15)

        def rows(i, _, n=n, q_ref=q_ref, q_ctx=q_ctx, local=local):
            at = pl.ds(pl.multiple_of(i * ROWS_TILE, ROWS_TILE), ROWS_TILE)
            ahead = key - local
            queries = q_ref[at, :]
            parts = []
            for source, ref in zip(sources, fetched):
                scores = lax.dot_general(
                    queries,
                    ref[:, :HEAD_DIM],
                    (((1,), (1,)), ((), ())),
                    preferred_element_type=F32,
                )
                parts.append(
                    jnp.where(ahead <= (q_ctx - source) * TOK_C, scores, F32(NEGATIVE))
                )
            top = parts[0]
            for part in parts[1:]:
                top = jnp.maximum(top, part)
            top = jnp.max(top, axis=1, keepdims=True)
            total, mixed = 0.0, 0.0
            for part, ref in zip(parts, fetched):
                weights = jnp.exp2((part - top) * SCALE)
                total = total + weights
                mixed = mixed + jnp.dot(
                    weights.astype(BF16), ref[:, HEAD_DIM:], preferred_element_type=F32
                )
            total = jnp.sum(total, axis=1, keepdims=True)
            outs[n][at, :HEAD_DIM] = mixed
            outs[n][at, HEAD_DIM:] = jnp.where(lane < 64, top, total)
            return 0

        lax.fori_loop(0, half // ROWS_TILE, rows, 0)


def project(place, resident, fetched, outs, wait):
    (own_ref,) = resident
    other_ref, near_ref, far_ref, w_own_ref = fetched
    keep_ref, *send_refs, attn_ref = outs
    core = place[0]
    wait(0)
    own_top = own_ref[:, HEAD_DIM : HEAD_DIM + 1]
    other_top = other_ref[:, HEAD_DIM : HEAD_DIM + 1]
    top = jnp.maximum(own_top, other_top)
    own_factor = jnp.exp2((own_top - top) * SCALE)
    other_factor = jnp.exp2((other_top - top) * SCALE)
    total = own_ref[:, HEAD_DIM + 64 : HEAD_DIM + 65] * own_factor
    total = total + other_ref[:, HEAD_DIM + 64 : HEAD_DIM + 65] * other_factor
    mixed = own_ref[:, :HEAD_DIM] * own_factor + other_ref[:, :HEAD_DIM] * other_factor
    attn_ref[...] = (mixed / total).astype(BF16)

    def ordered(head):
        pieces = []
        for low, high in ((1, 2), (0, 1), (2, 3), (3, 0)):
            for half in range(2):
                start = head * 128 + half * 64 + jnp.where(core == 0, low, high) * 16
                pieces.append(attn_ref[pl.ds(pl.multiple_of(start, 16), 16), :])
        return jnp.concatenate(pieces, axis=0)

    heads = [ordered(0), ordered(1)]
    width = D // 2
    for n in range(1, 4):
        wait(n)
    for side, w_ref in ((core, near_ref), (1 - core, far_ref)):
        at = pl.ds(pl.multiple_of(side * width, width), width)
        sums = jnp.dot(heads[0], w_own_ref[:, at], preferred_element_type=F32)
        sums = sums + jnp.dot(heads[1], w_ref[...], preferred_element_type=F32)
        keep_ref[:, at] = sums[:32]
        for s in range(3):
            send_refs[s][:, at] = sums[(s + 1) * 32 : (s + 2) * 32].astype(BF16)


def add_up(place, resident, fetched, outs, wait):
    sums = resident[0][...]
    for n in range(3):
        wait(n)
        sums = sums + fetched[n][...].astype(F32)
    outs[0][...] = sums
    outs[1][...] = sums.astype(BF16)


def normalise(place, resident, fetched, outs, wait):
    own_ref, sums_ref, gain_ref = resident
    y_ref, core_ref, both_ref, sums_y_ref, sums_core_ref, sums_both_ref = fetched
    hidden_ref, normed_ref = outs
    y = place[1]
    for n in range(6):
        wait(n)
    for n in range(4):
        at = pl.ds(n % 2 * 16, 16)
        to = pl.ds(n * 16, 16)
        here, there = (own_ref, y_ref) if n < 2 else (core_ref, both_ref)
        extended = jnp.where(y == n % 2, here[...].astype(F32), there[...].astype(F32))
        if n < 2:
            projected = sums_ref[at, :] + sums_y_ref[at, :].astype(F32)
        else:
            projected = sums_core_ref[at, :].astype(F32) + sums_both_ref[at, :].astype(F32)
        hidden = (extended[:, :D] + projected).astype(BF16)
        wide = hidden.astype(F32)
        inverse = lax.rsqrt(jnp.mean(wide * wide, axis=-1, keepdims=True) + 1e-06)
        normed = (wide * inverse * gain_ref[...].astype(F32)).astype(BF16)
        if n < 2:
            hidden_ref[at, :] = hidden
        normed_ref[to, :D] = normed
        normed_ref[to, D:] = extended[:, D:].astype(BF16)


def early(place, resident, fetched, outs, wait):
    outs[0][...] = resident[0][:8, :128]


def expert(place, resident, fetched, outs, wait):
    gate_ref, up_ref, down_ref = resident
    keep_ref, give_ref = outs
    y, z = place[1], place[2]
    for n in range(len(fetched)):
        wait(n)
    rows = [ref[:, :D] for ref in fetched]
    weights = [ref[:, D:] for ref in fetched]
    rows = rows[0] if len(rows) == 1 else jnp.concatenate(rows, axis=0)
    weights = weights[0] if len(weights) == 1 else jnp.concatenate(weights, axis=0)
    lane = lax.broadcasted_iota(jnp.int32, weights.shape, 1)
    weight = jnp.where(lane == y * 8 + z, weights.astype(F32), 0.0)
    weight = jnp.sum(weight, axis=1, keepdims=True)
    gate_part = jnp.dot(rows, gate_ref[...], preferred_element_type=F32)
    up_part = jnp.dot(rows, up_ref[...], preferred_element_type=F32)
    inner = (gate_part * jax.nn.sigmoid(gate_part) * up_part).astype(BF16)
    result = jnp.dot(inner, down_ref[...], preferred_element_type=F32).astype(BF16)
    result = result.astype(F32) * weight
    for n in range(rows.shape[0] // 32):
        at = pl.ds(n * 16, 16)
        low, high = result[n * 32 : n * 32 + 16], result[n * 32 + 16 : n * 32 + 32]
        keep_ref[at, :] = jnp.where(y == 0, low, high)
        give_ref[at, :] = jnp.where(y == 0, high, low).astype(BF16)


def run_expert(place, rows, weights, idle=()):
    total = sum(r.shape[0] for r in rows)
    keep, give = kernel_call(
        expert,
        place,
        weights,
        rows,
        [struct((total // 2, D), F32), struct((total // 2, D), BF16)],
        6 * total * D * FF,
        total * FF,
        idle=idle,
    )
    return keep, on_exp(give, Y_SWAP)


def join(place, resident, fetched, outs, wait):
    sums = resident[0][...] + resident[1][...].astype(F32)
    start = 0
    for out in outs:
        out[...] = sums[start : start + out.shape[0]].astype(out.dtype)
        start += out.shape[0]


def run_join(place, keep, got, outs):
    return kernel_call(join, place, [keep, got], [], outs, keep.size)


def gather_up(place, resident, fetched, outs, wait):
    own_ref, opposite_ref, *near_refs = resident
    mine = own_ref[...] + opposite_ref[...].astype(F32)
    theirs = 0.0
    for ref in near_refs:
        mine = mine + ref[:16, :].astype(F32)
        theirs = theirs + ref[16:, :].astype(F32)
    outs[0][...] = mine
    outs[1][...] = theirs.astype(BF16)


def finish(place, resident, fetched, outs, wait):
    hidden_ref, keep_ref = resident
    hidden = jnp.where(
        place[1] == 0, hidden_ref[:16, :].astype(F32), hidden_ref[16:, :].astype(F32)
    )
    wait(0)
    moe = keep_ref[...] + fetched[0][...].astype(F32)
    outs[0][...] = (hidden + moe).astype(BF16)


def extend(place, resident, fetched, outs, wait):
    residual_ref, ids_ref, gates_ref = resident
    lane = lax.broadcasted_iota(jnp.int32, (TOK_DEV, 128), 1)
    weights = jnp.zeros((TOK_DEV, 128), F32)
    for k in range(TOP):
        gate = gates_ref[:, k : k + 1].astype(F32)
        weights = weights + jnp.where(lane == ids_ref[:, k : k + 1], gate, 0.0)
    outs[0][:, :D] = residual_ref[...]
    outs[0][:, D:] = weights.astype(BF16)


def by_core(step):
    route = []
    for c in range(16):
        way = step if c % 2 == 0 else -step
        for e in range(16):
            route.append((c * 16 + e, c * 16 + e // 8 * 8 + (e + way) % 8))
    return route


def on_both(block, route):
    return lax.ppermute(block, ("ctx", "exp"), route)


def two_swaps(ctx_bit, exp_bit):
    return [
        (c * 16 + e, (c ^ ctx_bit) * 16 + (e ^ exp_bit)) for c in range(16) for e in range(16)
    ]


def to_three(to_y, to_core, to_both):
    return (
        on_exp(to_y, Y_SWAP),
        on_ctx(to_core, CORE_SWAP),
        on_both(to_both, two_swaps(1, 8)),
    )


def shards(
    query,
    keys,
    values,
    out_proj,
    residual,
    norm_gain,
    expert_ids,
    gate_values,
    w_gate,
    w_up,
    w_down,
):
    ctx, exp = lax.axis_index("ctx"), lax.axis_index("exp")
    core, y, z = ctx % 2, exp // 8, exp % 8
    place = jnp.stack([core, y, z, ctx]).astype(jnp.int32)
    kv_index = exp // (HEADS // KV_HEADS)
    block = jnp.concatenate(
        [
            lax.dynamic_slice_in_dim(keys, kv_index * HEAD_DIM, HEAD_DIM, 1),
            lax.dynamic_slice_in_dim(values, kv_index * HEAD_DIM, HEAD_DIM, 1),
        ],
        axis=1,
    )

    other = on_ctx(block, OTHER_ROW)
    blocks = [block] + [on_ctx(block, block_route(-d)) for _, d in PLACES[1:4]]
    blocks += [other] + [on_ctx(other, relay_route(-d)) for _, d in PLACES[5:]]

    by_holder = query.reshape(2, 8, TOK_DEV, HEAD_DIM)
    by_holder = jnp.concatenate([by_holder, by_holder], axis=1)

    def rows_of(first):
        return lax.dynamic_slice_in_dim(by_holder, first % 8, 4, 1).reshape(128, HEAD_DIM)

    first = z + 7 - core
    mine = jnp.concatenate([rows_of(first), on_exp(rows_of(first + 4), z_shift(4))], axis=0)
    theirs = on_ctx(mine, CORE_SWAP)

    w_out, blocks[4] = after(out_proj, blocks[4])
    w_half = lax.dynamic_slice_in_dim(w_out, core * (D // 2), D // 2, 1)
    w_near = on_exp(w_half, z_shift(4))
    w_far = on_ctx(w_near, CORE_SWAP)

    own, swap = kernel_call(
        attend_all,
        place,
        [mine, theirs],
        blocks,
        [struct((256, 256), F32)] * 2,
        4 * 512 * 2048 * HEAD_DIM,
        512 * 2048,
    )
    joined = on_ctx(swap, CORE_SWAP)
    keep, *sends = kernel_call(
        project,
        place,
        [own],
        [joined, w_near, w_far, out_proj],
        [struct((32, D), F32)] + [struct((32, D), BF16)] * 3,
        2 * 128 * 256 * D,
        scratch=[pltpu.VMEM((256, HEAD_DIM), BF16)],
    )
    recvs = [
        on_exp(sends[0], z_shift(-1)),
        on_exp(sends[1], z_shift(1)),
        on_both(sends[2], by_core(2)),
    ]
    rows, recvs[0] = after(residual, recvs[0])
    (extended,) = kernel_call(
        extend,
        place,
        [rows, expert_ids, gate_values],
        [],
        [struct((TOK_DEV, D + 128), BF16)],
        TOK_DEV * D,
    )
    extended_others = to_three(extended, extended, extended)
    sums, send = kernel_call(
        add_up,
        place,
        [keep],
        recvs,
        [struct((32, D), F32), struct((32, D), BF16)],
        3 * 32 * D,
    )
    hidden, round_0 = kernel_call(
        normalise,
        place,
        [extended, sums, norm_gain.reshape(1, D)],
        [*extended_others, *to_three(send, send, send)],
        [struct((32, D), BF16), struct((64, D + 128), BF16)],
        16 * 32 * D,
    )

    half = struct((32, D), BF16)
    w = [w_gate[0], w_up[0], w_down[0]]
    round_1 = on_both(round_0, by_core(1))
    round_2 = on_both(round_0, by_core(2))
    (seen,) = kernel_call(
        early, place, [round_0], [], [struct((8, 128), BF16)], 8 * 128, idle=w
    )
    round_2, seen = after(round_2, seen)
    round_3 = on_both(round_2, by_core(1))
    round_4 = on_both(round_2[:32], by_core(2))
    keep, got = run_expert(place, [round_1, round_2, round_0[:32]], w, [seen])
    keep_far, got_far = run_expert(place, [round_3, round_4], w)
    sum_1, sum_2, own_sum = run_join(place, keep, got, [half, half, struct((16, D), F32)])
    back_1 = on_both(sum_1, by_core(-1))
    back_2 = on_both(sum_2, by_core(-2))
    got_far, back_1, back_2 = after(got_far, back_1, back_2)
    sum_3, sum_4 = run_join(place, keep_far, got_far, [half, struct((16, D), BF16)])
    back_3 = on_both(sum_3, by_core(-3))
    back_4 = on_exp(sum_4, z_shift(4))
    keep, to_core = kernel_call(
        gather_up,
        place,
        [own_sum, back_4, back_1, back_2, back_3],
        [],
        [struct((16, D), F32), struct((16, D), BF16)],
        8 * 16 * D,
    )
    return kernel_call(
        finish,
        place,
        [hidden, keep],
        [on_ctx(to_core, CORE_SWAP)],
        [struct((16, D), BF16)],
        3 * 16 * D,
    )[0]


def solution(mesh):
    return jax.shard_map(
        shards,
        mesh=mesh,
        in_specs=(
            P("ctx", "exp"),
            P("ctx", None),
            P("ctx", None),
            P("exp", None),
            P(("ctx", "exp"), None),
            P(),
            P(("ctx", "exp"), None),
            P(("ctx", "exp"), None),
            P("exp", None, None),
            P("exp", None, None),
            P("exp", None, None),
        ),
        out_specs=P(("ctx", "exp"), None),
        check_vma=False,
    )
```

```python
import math

import jax
import jax.numpy as jnp
from jax import lax
from jax.experimental import pallas as pl
from jax.experimental.pallas import tpu as pltpu
from jax.sharding import PartitionSpec as P

D = 2048
HEAD_DIM = 128
FF = 768
TOP = 8
HEADS = 16
KV_HEADS = 2
EXPERTS = 16
TOK_C = 256
TOK_DEV = 16
NEGATIVE = -1e30
SCALE = math.log2(math.e) / math.sqrt(HEAD_DIM)
F32 = jnp.float32
BF16 = jnp.bfloat16

CORE_SWAP = [(i, i ^ 1) for i in range(16)]
Y_SWAP = [(i, i ^ 8) for i in range(16)]


ROW_SWAP = [(i, i ^ 8) for i in range(16)]


def x_shift(step):
    return [(i, i // 8 * 8 + (i // 2 + step) % 4 * 2 + i % 2) for i in range(16)]


def z_shift(step):
    return [(y * 8 + z, y * 8 + (z + step) % 8) for y in range(2) for z in range(8)]


def on_ctx(block, route):
    return lax.ppermute(block, "ctx", route)


def on_exp(block, route):
    return lax.ppermute(block, "exp", route)


def kernel_call(
    body, scalars, resident, fetched, out_shapes, flops, transcendentals=0, limit=10, idle=(), scratch=()
):
    n_own = len(resident)
    resident, fetched = [*resident, *fetched], []
    ins = [*resident, *fetched, *idle]
    n_res, n_fetch = len(resident), len(fetched)
    n_out = len(jax.tree.leaves(out_shapes))

    def whole(*refs):
        place, refs = refs[0], refs[1:]
        sources = refs[n_res : n_res + n_fetch]
        outs = refs[len(ins) : len(ins) + n_out]
        buffers = refs[len(ins) + n_out : len(ins) + n_out + n_fetch]
        copies = []
        for n in range(n_fetch):
            copies.append(
                pltpu.make_async_copy(sources[n], buffers[n], refs[len(ins) + n_out + n_fetch + n])
            )
        for copy in copies:
            copy.start()
        extra = refs[len(ins) + n_out + 2 * n_fetch :]
        body(place, refs[:n_own], refs[n_own:n_res], (*outs, *extra), lambda n: None)

    size = sum(a.size * a.dtype.itemsize for a in [*resident, *fetched])
    vmem = pl.BlockSpec(memory_space=pltpu.VMEM)
    return pl.pallas_call(
        whole,
        out_shape=out_shapes,
        in_specs=[pl.BlockSpec(memory_space=pltpu.SMEM)]
        + [vmem] * n_res
        + [pl.BlockSpec(memory_space=pl.ANY)] * n_fetch
        + [vmem] * len(idle),
        out_specs=jax.tree.map(lambda _: vmem, out_shapes),
        scratch_shapes=[pltpu.VMEM(a.shape, a.dtype) for a in fetched]
        + [pltpu.SemaphoreType.DMA] * n_fetch
        + list(scratch),
        compiler_params=pltpu.CompilerParams(vmem_limit_bytes=limit * 1024 * 1024),
        cost_estimate=pl.CostEstimate(
            flops=flops, bytes_accessed=size, transcendentals=transcendentals
        ),
    )(scalars, *ins)


def after(value, *earlier):
    return lax.optimization_barrier((value, *earlier))


def struct(shape, dtype):
    return jax.ShapeDtypeStruct(shape, dtype)


ROWS_TILE = 256
PLACES = [(r, d) for r in (0, 1) for d in (0, -1, 1, 2)]


def attend_all(place, resident, fetched, outs, wait):
    core, y, z, ctx = place[0], place[1], place[2], place[3]
    row, x = ctx // 8, lax.rem(ctx // 2, 4)
    sources = [(row ^ r) * 8 + lax.rem(x + d + 4, 4) * 2 + core for r, d in PLACES]
    half = resident[0].shape[0]
    for n in range(8):
        wait(n)
    token = lax.broadcasted_iota(jnp.int32, (ROWS_TILE, 1), 0) & 127
    part = token >> 4
    key = lax.broadcasted_iota(jnp.int32, (1, TOK_C), 1)
    lane = lax.broadcasted_iota(jnp.int32, (ROWS_TILE, HEAD_DIM), 1)
    for n, q_ref in enumerate(resident):
        q_ctx = ctx ^ n
        first = z + 7 - (core ^ n)
        local = (part >> 2) * 128 + (((part & 3) + first) & 7) * 16 + (token & 15)

        def rows(i, _, n=n, q_ref=q_ref, q_ctx=q_ctx, local=local):
            at = pl.ds(pl.multiple_of(i * ROWS_TILE, ROWS_TILE), ROWS_TILE)
            ahead = key - local
            queries = q_ref[at, :]
            parts = []
            for source, ref in zip(sources, fetched):
                scores = lax.dot_general(
                    queries,
                    ref[:, :HEAD_DIM],
                    (((1,), (1,)), ((), ())),
                    preferred_element_type=F32,
                )
                parts.append(
                    jnp.where(ahead <= (q_ctx - source) * TOK_C, scores, F32(NEGATIVE))
                )
            top = parts[0]
            for part in parts[1:]:
                top = jnp.maximum(top, part)
            top = jnp.max(top, axis=1, keepdims=True)
            total, mixed = 0.0, 0.0
            for part, ref in zip(parts, fetched):
                weights = jnp.exp2((part - top) * SCALE)
                total = total + weights
                mixed = mixed + jnp.dot(
                    weights.astype(BF16), ref[:, HEAD_DIM:], preferred_element_type=F32
                )
            total = jnp.sum(total, axis=1, keepdims=True)
            outs[n][at, :HEAD_DIM] = mixed
            outs[n][at, HEAD_DIM:] = jnp.where(lane < 64, top, total)
            return 0

        lax.fori_loop(0, half // ROWS_TILE, rows, 0)


def project(place, resident, fetched, outs, wait):
    (own_ref,) = resident
    other_ref, near_ref, far_ref, w_own_ref = fetched
    keep_ref, *send_refs, attn_ref = outs
    core = place[0]
    wait(0)
    own_top = own_ref[:, HEAD_DIM : HEAD_DIM + 1]
    other_top = other_ref[:, HEAD_DIM : HEAD_DIM + 1]
    top = jnp.maximum(own_top, other_top)
    own_factor = jnp.exp2((own_top - top) * SCALE)
    other_factor = jnp.exp2((other_top - top) * SCALE)
    total = own_ref[:, HEAD_DIM + 64 : HEAD_DIM + 65] * own_factor
    total = total + other_ref[:, HEAD_DIM + 64 : HEAD_DIM + 65] * other_factor
    mixed = own_ref[:, :HEAD_DIM] * own_factor + other_ref[:, :HEAD_DIM] * other_factor
    attn_ref[...] = (mixed / total).astype(BF16)

    def ordered(head):
        pieces = []
        for low, high in ((1, 2), (0, 1), (2, 3), (3, 0)):
            for half in range(2):
                start = head * 128 + half * 64 + jnp.where(core == 0, low, high) * 16
                pieces.append(attn_ref[pl.ds(pl.multiple_of(start, 16), 16), :])
        return jnp.concatenate(pieces, axis=0)

    heads = [ordered(0), ordered(1)]
    width = D // 2
    for n in range(1, 4):
        wait(n)
    for side, w_ref in ((core, near_ref), (1 - core, far_ref)):
        at = pl.ds(pl.multiple_of(side * width, width), width)
        sums = jnp.dot(heads[0], w_own_ref[:, at], preferred_element_type=F32)
        sums = sums + jnp.dot(heads[1], w_ref[...], preferred_element_type=F32)
        keep_ref[:, at] = sums[:32]
        for s in range(3):
            send_refs[s][:, at] = sums[(s + 1) * 32 : (s + 2) * 32].astype(BF16)


def add_up(place, resident, fetched, outs, wait):
    sums = resident[0][...]
    for n in range(3):
        wait(n)
        sums = sums + fetched[n][...].astype(F32)
    outs[0][...] = sums
    outs[1][...] = sums.astype(BF16)


def normalise(place, resident, fetched, outs, wait):
    own_ref, sums_ref, gain_ref = resident
    y_ref, core_ref, both_ref, sums_y_ref, sums_core_ref, sums_both_ref = fetched
    hidden_ref, normed_ref = outs
    y = place[1]
    for n in range(6):
        wait(n)
    for n in range(4):
        at = pl.ds(n % 2 * 16, 16)
        to = pl.ds(n * 16, 16)
        here, there = (own_ref, y_ref) if n < 2 else (core_ref, both_ref)
        extended = jnp.where(y == n % 2, here[...].astype(F32), there[...].astype(F32))
        if n < 2:
            projected = sums_ref[at, :] + sums_y_ref[at, :].astype(F32)
        else:
            projected = sums_core_ref[at, :].astype(F32) + sums_both_ref[at, :].astype(F32)
        hidden = (extended[:, :D] + projected).astype(BF16)
        wide = hidden.astype(F32)
        inverse = lax.rsqrt(jnp.mean(wide * wide, axis=-1, keepdims=True) + 1e-06)
        normed = (wide * inverse * gain_ref[:1, :]).astype(BF16)
        if n < 2:
            hidden_ref[at, :] = hidden
        normed_ref[to, :D] = normed
        normed_ref[to, D:] = extended[:, D:].astype(BF16)


def early(place, resident, fetched, outs, wait):
    outs[0][...] = resident[0][:8, :128]


def expert(place, resident, fetched, outs, wait):
    gate_ref, up_ref, down_ref = resident
    keep_ref, give_ref = outs
    y, z = place[1], place[2]
    for n in range(len(fetched)):
        wait(n)
    rows = [ref[:, :D] for ref in fetched]
    weights = [ref[:, D:] for ref in fetched]
    rows = rows[0] if len(rows) == 1 else jnp.concatenate(rows, axis=0)
    weights = weights[0] if len(weights) == 1 else jnp.concatenate(weights, axis=0)
    lane = lax.broadcasted_iota(jnp.int32, weights.shape, 1)
    weight = jnp.where(lane == y * 8 + z, weights.astype(F32), 0.0)
    weight = jnp.sum(weight, axis=1, keepdims=True)
    gate_part = jnp.dot(rows, gate_ref[...], preferred_element_type=F32)
    up_part = jnp.dot(rows, up_ref[...], preferred_element_type=F32)
    inner = (gate_part * jax.nn.sigmoid(gate_part) * up_part).astype(BF16)
    result = jnp.dot(inner, down_ref[...], preferred_element_type=F32).astype(BF16)
    result = result.astype(F32) * weight
    for n in range(rows.shape[0] // 32):
        at = pl.ds(n * 16, 16)
        low, high = result[n * 32 : n * 32 + 16], result[n * 32 + 16 : n * 32 + 32]
        keep_ref[at, :] = jnp.where(y == 0, low, high)
        give_ref[at, :] = jnp.where(y == 0, high, low).astype(BF16)


def run_expert(place, rows, weights, idle=()):
    total = sum(r.shape[0] for r in rows)
    keep, give = kernel_call(
        expert,
        place,
        weights,
        rows,
        [struct((total // 2, D), F32), struct((total // 2, D), BF16)],
        6 * total * D * FF,
        total * FF,
        idle=idle,
    )
    return keep, on_exp(give, Y_SWAP)


def join(place, resident, fetched, outs, wait):
    sums = resident[0][...] + resident[1][...].astype(F32)
    start = 0
    for out in outs:
        out[...] = sums[start : start + out.shape[0]].astype(out.dtype)
        start += out.shape[0]


def run_join(place, keep, got, outs):
    return kernel_call(join, place, [keep, got], [], outs, keep.size)


def gather_up(place, resident, fetched, outs, wait):
    own_ref, opposite_ref, *near_refs = resident
    mine = own_ref[...] + opposite_ref[...].astype(F32)
    theirs = 0.0
    for ref in near_refs:
        mine = mine + ref[:16, :].astype(F32)
        theirs = theirs + ref[16:, :].astype(F32)
    outs[0][...] = mine
    outs[1][...] = theirs.astype(BF16)


def finish(place, resident, fetched, outs, wait):
    hidden_ref, keep_ref = resident
    hidden = jnp.where(
        place[1] == 0, hidden_ref[:16, :].astype(F32), hidden_ref[16:, :].astype(F32)
    )
    wait(0)
    moe = keep_ref[...] + fetched[0][...].astype(F32)
    outs[0][...] = (hidden + moe).astype(BF16)


def extend(place, resident, fetched, outs, wait):
    residual_ref, ids_ref, gates_ref, gain_ref = resident
    lane = lax.broadcasted_iota(jnp.int32, (TOK_DEV, 128), 1)
    weights = jnp.zeros((TOK_DEV, 128), F32)
    for k in range(TOP):
        gate = gates_ref[:, k : k + 1].astype(F32)
        weights = weights + jnp.where(lane == ids_ref[:, k : k + 1], gate, 0.0)
    outs[0][:, :D] = residual_ref[...]
    outs[0][:, D:] = weights.astype(BF16)
    outs[1][...] = jnp.broadcast_to(gain_ref[...].astype(F32), outs[1].shape)


def by_core(step):
    route = []
    for c in range(16):
        way = step if c % 2 == 0 else -step
        for e in range(16):
            route.append((c * 16 + e, c * 16 + e // 8 * 8 + (e + way) % 8))
    return route


def on_both(block, route):
    return lax.ppermute(block, ("ctx", "exp"), route)


def two_swaps(ctx_bit, exp_bit):
    return [
        (c * 16 + e, (c ^ ctx_bit) * 16 + (e ^ exp_bit)) for c in range(16) for e in range(16)
    ]


def to_three(to_y, to_core, to_both):
    return (
        on_exp(to_y, Y_SWAP),
        on_ctx(to_core, CORE_SWAP),
        on_both(to_both, two_swaps(1, 8)),
    )


def shards(
    query,
    keys,
    values,
    out_proj,
    residual,
    norm_gain,
    expert_ids,
    gate_values,
    w_gate,
    w_up,
    w_down,
):
    ctx, exp = lax.axis_index("ctx"), lax.axis_index("exp")
    core, y, z = ctx % 2, exp // 8, exp % 8
    place = jnp.stack([core, y, z, ctx]).astype(jnp.int32)
    kv_index = exp // (HEADS // KV_HEADS)
    block = jnp.concatenate(
        [
            lax.dynamic_slice_in_dim(keys, kv_index * HEAD_DIM, HEAD_DIM, 1),
            lax.dynamic_slice_in_dim(values, kv_index * HEAD_DIM, HEAD_DIM, 1),
        ],
        axis=1,
    )

    other = on_ctx(block, ROW_SWAP)
    blocks = [block] + [on_ctx(block, x_shift(-d)) for _, d in PLACES[1:4]]
    blocks += [other] + [on_ctx(other, x_shift(-d)) for _, d in PLACES[5:]]

    by_holder = query.reshape(2, 8, TOK_DEV, HEAD_DIM)
    by_holder = jnp.concatenate([by_holder, by_holder], axis=1)

    def rows_of(first):
        return lax.dynamic_slice_in_dim(by_holder, first % 8, 4, 1).reshape(128, HEAD_DIM)

    first = z + 7 - core
    mine = jnp.concatenate([rows_of(first), on_exp(rows_of(first + 4), z_shift(4))], axis=0)
    theirs = on_ctx(mine, CORE_SWAP)

    w_out, blocks[4] = after(out_proj, blocks[4])
    w_half = lax.dynamic_slice_in_dim(w_out, core * (D // 2), D // 2, 1)
    w_near = on_exp(w_half, z_shift(4))
    w_far = on_ctx(w_near, CORE_SWAP)

    rows, *blocks[1:7] = after(residual, *blocks[1:7])
    extended, gain = kernel_call(
        extend,
        place,
        [rows, expert_ids, gate_values, norm_gain.reshape(1, D)],
        [],
        [struct((TOK_DEV, D + 128), BF16), struct((8, D), F32)],
        TOK_DEV * D,
    )
    extended_others = to_three(extended, extended, extended)
    mine, *extended_others = after(mine, *extended_others)

    own, swap = kernel_call(
        attend_all,
        place,
        [mine, theirs],
        blocks,
        [struct((256, 256), F32)] * 2,
        4 * 512 * 2048 * HEAD_DIM,
        512 * 2048,
    )
    joined = on_ctx(swap, CORE_SWAP)
    keep, *sends = kernel_call(
        project,
        place,
        [own],
        [joined, w_near, w_far, out_proj],
        [struct((32, D), F32)] + [struct((32, D), BF16)] * 3,
        2 * 128 * 256 * D,
        scratch=[pltpu.VMEM((256, HEAD_DIM), BF16)],
    )
    recvs = [
        on_exp(sends[0], z_shift(-1)),
        on_exp(sends[1], z_shift(1)),
        on_both(sends[2], by_core(2)),
    ]
    sums, send = kernel_call(
        add_up,
        place,
        [keep],
        recvs,
        [struct((32, D), F32), struct((32, D), BF16)],
        3 * 32 * D,
    )
    hidden, round_0 = kernel_call(
        normalise,
        place,
        [extended, sums, gain],
        [*extended_others, *to_three(send, send, send)],
        [struct((32, D), BF16), struct((64, D + 128), BF16)],
        16 * 32 * D,
    )

    half = struct((32, D), BF16)
    w = [w_gate[0], w_up[0], w_down[0]]
    round_1 = on_both(round_0, by_core(1))
    round_2 = on_both(round_0, by_core(2))
    (seen,) = kernel_call(
        early, place, [round_0], [], [struct((8, 128), BF16)], 8 * 128, idle=w
    )
    round_2, seen = after(round_2, seen)
    round_3 = on_both(round_2, by_core(1))
    round_4 = on_both(round_2[:32], by_core(2))
    keep, got = run_expert(place, [round_1, round_2, round_0[:32]], w, [seen])
    keep_far, got_far = run_expert(place, [round_3, round_4], w)
    sum_1, sum_2, own_sum = run_join(place, keep, got, [half, half, struct((16, D), F32)])
    back_1 = on_both(sum_1, by_core(-1))
    back_2 = on_both(sum_2, by_core(-2))
    got_far, back_1 = after(got_far, back_1)
    sum_3, sum_4 = run_join(place, keep_far, got_far, [half, struct((16, D), BF16)])
    back_3 = on_both(sum_3, by_core(-3))
    back_4 = on_exp(sum_4, z_shift(4))
    keep, to_core = kernel_call(
        gather_up,
        place,
        [own_sum, back_4, back_1, back_2, back_3],
        [],
        [struct((16, D), F32), struct((16, D), BF16)],
        8 * 16 * D,
    )
    return kernel_call(
        finish,
        place,
        [hidden, keep],
        [on_ctx(to_core, CORE_SWAP)],
        [struct((16, D), BF16)],
        3 * 16 * D,
    )[0]


def solution(mesh):
    return jax.shard_map(
        shards,
        mesh=mesh,
        in_specs=(
            P("ctx", "exp"),
            P("ctx", None),
            P("ctx", None),
            P("exp", None),
            P(("ctx", "exp"), None),
            P(),
            P(("ctx", "exp"), None),
            P(("ctx", "exp"), None),
            P("exp", None, None),
            P("exp", None, None),
            P("exp", None, None),
        ),
        out_specs=P(("ctx", "exp"), None),
        check_vma=False,
    )
```

```python
import math

import jax
import jax.numpy as jnp
from jax import lax
from jax.experimental import pallas as pl
from jax.experimental.pallas import tpu as pltpu
from jax.sharding import PartitionSpec as P

D = 2048
HEAD_DIM = 128
FF = 768
TOP = 8
HEADS = 16
KV_HEADS = 2
EXPERTS = 16
TOK_C = 256
TOK_DEV = 16
NEGATIVE = -1e30
SCALE = math.log2(math.e) / math.sqrt(HEAD_DIM)
F32 = jnp.float32
BF16 = jnp.bfloat16

CORE_SWAP = [(i, i ^ 1) for i in range(16)]
Y_SWAP = [(i, i ^ 8) for i in range(16)]


ROW_SWAP = [(i, i ^ 8) for i in range(16)]


def x_shift(step):
    return [(i, i // 8 * 8 + (i // 2 + step) % 4 * 2 + i % 2) for i in range(16)]


def z_shift(step):
    return [(y * 8 + z, y * 8 + (z + step) % 8) for y in range(2) for z in range(8)]


def on_ctx(block, route):
    return lax.ppermute(block, "ctx", route)


def on_exp(block, route):
    return lax.ppermute(block, "exp", route)


def kernel_call(
    body, scalars, resident, fetched, out_shapes, flops, transcendentals=0, limit=10, idle=(), scratch=()
):
    ins = [*resident, *fetched, *idle]
    n_res, n_fetch = len(resident), len(fetched)
    n_out = len(jax.tree.leaves(out_shapes))

    def whole(*refs):
        place, refs = refs[0], refs[1:]
        sources = refs[n_res : n_res + n_fetch]
        outs = refs[len(ins) : len(ins) + n_out]
        buffers = refs[len(ins) + n_out : len(ins) + n_out + n_fetch]
        copies = []
        for n in range(n_fetch):
            copies.append(
                pltpu.make_async_copy(sources[n], buffers[n], refs[len(ins) + n_out + n_fetch + n])
            )
        for copy in copies:
            copy.start()
        extra = refs[len(ins) + n_out + 2 * n_fetch :]
        body(place, refs[:n_res], buffers, (*outs, *extra), lambda n: copies[n].wait())

    size = sum(a.size * a.dtype.itemsize for a in [*resident, *fetched])
    vmem = pl.BlockSpec(memory_space=pltpu.VMEM)
    return pl.pallas_call(
        whole,
        out_shape=out_shapes,
        in_specs=[pl.BlockSpec(memory_space=pltpu.SMEM)]
        + [vmem] * n_res
        + [pl.BlockSpec(memory_space=pltpu.HBM)] * n_fetch
        + [vmem] * len(idle),
        out_specs=jax.tree.map(lambda _: vmem, out_shapes),
        scratch_shapes=[pltpu.VMEM(a.shape, a.dtype) for a in fetched]
        + [pltpu.SemaphoreType.DMA] * n_fetch
        + list(scratch),
        compiler_params=pltpu.CompilerParams(vmem_limit_bytes=limit * 1024 * 1024),
        cost_estimate=pl.CostEstimate(
            flops=flops, bytes_accessed=size, transcendentals=transcendentals
        ),
    )(scalars, *ins)


def after(value, *earlier):
    return lax.optimization_barrier((value, *earlier))


def struct(shape, dtype):
    return jax.ShapeDtypeStruct(shape, dtype)


ROWS_TILE = 256
DISTANCES = (0, -1, 1, 2)


def attend_all(place, resident, fetched, outs, wait):
    core, y, z, ctx = place[0], place[1], place[2], place[3]
    row, x = ctx // 8, lax.rem(ctx // 2, 4)
    sources = [(row ^ r) * 8 + lax.rem(x + d + 4, 4) * 2 + core for d in DISTANCES for r in (0, 1)]
    half = resident[0].shape[0]
    token = lax.broadcasted_iota(jnp.int32, (ROWS_TILE, 1), 0) & 127
    part = token >> 4
    key = lax.broadcasted_iota(jnp.int32, (1, TOK_C), 1)
    lane = lax.broadcasted_iota(jnp.int32, (ROWS_TILE, HEAD_DIM), 1)
    blocks = [ref.at[pl.ds(r * TOK_C, TOK_C)] for ref in resident[2:] for r in (0, 1)]
    for n, q_ref in enumerate(resident[:2]):
        q_ctx = ctx ^ n
        first = z + 7 - (core ^ n)
        local = (part >> 2) * 128 + (((part & 3) + first) & 7) * 16 + (token & 15)

        def rows(i, _, n=n, q_ref=q_ref, q_ctx=q_ctx, local=local):
            at = pl.ds(pl.multiple_of(i * ROWS_TILE, ROWS_TILE), ROWS_TILE)
            ahead = key - local
            queries = q_ref[at, :]
            parts = []
            for source, ref in zip(sources, blocks):
                scores = lax.dot_general(
                    queries,
                    ref[:, :HEAD_DIM],
                    (((1,), (1,)), ((), ())),
                    preferred_element_type=F32,
                )
                parts.append(
                    jnp.where(ahead <= (q_ctx - source) * TOK_C, scores, F32(NEGATIVE))
                )
            top = parts[0]
            for part in parts[1:]:
                top = jnp.maximum(top, part)
            top = jnp.max(top, axis=1, keepdims=True)
            total, mixed = 0.0, 0.0
            for part, ref in zip(parts, blocks):
                weights = jnp.exp2((part - top) * SCALE)
                total = total + weights
                mixed = mixed + jnp.dot(
                    weights.astype(BF16), ref[:, HEAD_DIM:], preferred_element_type=F32
                )
            total = jnp.sum(total, axis=1, keepdims=True)
            outs[n][at, :HEAD_DIM] = mixed
            outs[n][at, HEAD_DIM:] = jnp.where(lane < 64, top, total)
            return 0

        lax.fori_loop(0, half // ROWS_TILE, rows, 0)


def project(place, resident, fetched, outs, wait):
    own_ref, other_ref, *part_refs = resident
    (w_own_ref,) = fetched
    keep_ref, *send_refs, attn_ref = outs
    core, row = place[0], place[3] // 8
    own_top = own_ref[:, HEAD_DIM : HEAD_DIM + 1]
    other_top = other_ref[:, HEAD_DIM : HEAD_DIM + 1]
    top = jnp.maximum(own_top, other_top)
    own_factor = jnp.exp2((own_top - top) * SCALE)
    other_factor = jnp.exp2((other_top - top) * SCALE)
    total = own_ref[:, HEAD_DIM + 64 : HEAD_DIM + 65] * own_factor
    total = total + other_ref[:, HEAD_DIM + 64 : HEAD_DIM + 65] * other_factor
    mixed = own_ref[:, :HEAD_DIM] * own_factor + other_ref[:, :HEAD_DIM] * other_factor
    attn_ref[...] = (mixed / total).astype(BF16)

    def ordered(head):
        pieces = []
        for low, high in ((1, 2), (0, 1), (2, 3), (3, 0)):
            for half in range(2):
                start = head * 128 + half * 64 + jnp.where(core == 0, low, high) * 16
                pieces.append(attn_ref[pl.ds(pl.multiple_of(start, 16), 16), :])
        return jnp.concatenate(pieces, axis=0)

    heads = [ordered(0), ordered(1)]
    width = D // 4
    wait(0)
    for n, w_ref in enumerate(part_refs):
        column = ((core ^ (n // 2)) * 2 + (row ^ (n % 2))) * width
        at = pl.ds(pl.multiple_of(column, width), width)
        sums = jnp.dot(heads[0], w_own_ref[:, at], preferred_element_type=F32)
        sums = sums + jnp.dot(heads[1], w_ref[:, HEAD_DIM:], preferred_element_type=F32)
        keep_ref[:, at] = sums[:32]
        for s in range(3):
            send_refs[s][:, at] = sums[(s + 1) * 32 : (s + 2) * 32].astype(BF16)


def add_up(place, resident, fetched, outs, wait):
    sums = resident[0][...]
    for ref in resident[1:]:
        sums = sums + ref[...].astype(F32)
    outs[0][...] = sums
    outs[1][...] = sums.astype(BF16)


def normalise(place, resident, fetched, outs, wait):
    own_ref, sums_ref, gain_ref, y_ref, core_ref, both_ref = resident[:6]
    sums_y_ref, sums_core_ref, sums_both_ref = resident[6:]
    hidden_ref, normed_ref = outs
    y = place[1]
    for n in range(4):
        at = pl.ds(n % 2 * 16, 16)
        to = pl.ds(n * 16, 16)
        here, there = (own_ref, y_ref) if n < 2 else (core_ref, both_ref)
        extended = jnp.where(y == n % 2, here[...].astype(F32), there[...].astype(F32))
        if n < 2:
            projected = sums_ref[at, :] + sums_y_ref[at, :].astype(F32)
        else:
            projected = sums_core_ref[at, :].astype(F32) + sums_both_ref[at, :].astype(F32)
        hidden = (extended[:, :D] + projected).astype(BF16)
        wide = hidden.astype(F32)
        inverse = lax.rsqrt(jnp.mean(wide * wide, axis=-1, keepdims=True) + 1e-06)
        normed = (wide * inverse * gain_ref[...].astype(F32)).astype(BF16)
        if n < 2:
            hidden_ref[at, :] = hidden
        normed_ref[to, :D] = normed
        normed_ref[to, D:] = extended[:, D:].astype(BF16)


def early(place, resident, fetched, outs, wait):
    outs[0][...] = resident[0][:8, :128]


def expert(place, resident, fetched, outs, wait):
    gate_ref, up_ref, down_ref, *inputs = resident
    keep_ref, give_ref = outs
    y, z = place[1], place[2]
    rows = [ref[:, :D] for ref in inputs]
    weights = [ref[:, D:] for ref in inputs]
    rows = rows[0] if len(rows) == 1 else jnp.concatenate(rows, axis=0)
    weights = weights[0] if len(weights) == 1 else jnp.concatenate(weights, axis=0)
    lane = lax.broadcasted_iota(jnp.int32, weights.shape, 1)
    weight = jnp.where(lane == y * 8 + z, weights.astype(F32), 0.0)
    weight = jnp.sum(weight, axis=1, keepdims=True)
    gate_part = jnp.dot(rows, gate_ref[...], preferred_element_type=F32)
    up_part = jnp.dot(rows, up_ref[...], preferred_element_type=F32)
    inner = (gate_part * jax.nn.sigmoid(gate_part) * up_part).astype(BF16)
    result = jnp.dot(inner, down_ref[...], preferred_element_type=F32).astype(BF16)
    result = result.astype(F32) * weight
    for n in range(rows.shape[0] // 32):
        at = pl.ds(n * 16, 16)
        low, high = result[n * 32 : n * 32 + 16], result[n * 32 + 16 : n * 32 + 32]
        keep_ref[at, :] = jnp.where(y == 0, low, high)
        give_ref[at, :] = jnp.where(y == 0, high, low).astype(BF16)


def run_expert(place, rows, weights, idle=()):
    total = sum(r.shape[0] for r in rows)
    keep, give = kernel_call(
        expert,
        place,
        [*weights, *rows],
        [],
        [struct((total // 2, D), F32), struct((total // 2, D), BF16)],
        6 * total * D * FF,
        total * FF,
        idle=idle,
    )
    return keep, on_exp(give, Y_SWAP)


def join(place, resident, fetched, outs, wait):
    sums = resident[0][...] + resident[1][...].astype(F32)
    start = 0
    for out in outs:
        out[...] = sums[start : start + out.shape[0]].astype(out.dtype)
        start += out.shape[0]


def run_join(place, keep, got, outs):
    return kernel_call(join, place, [keep, got], [], outs, keep.size)


def gather_up(place, resident, fetched, outs, wait):
    own_ref, opposite_ref, *near_refs = resident
    mine = own_ref[...] + opposite_ref[...].astype(F32)
    theirs = 0.0
    for ref in near_refs:
        mine = mine + ref[:16, :].astype(F32)
        theirs = theirs + ref[16:, :].astype(F32)
    outs[0][...] = mine
    outs[1][...] = theirs.astype(BF16)


def finish(place, resident, fetched, outs, wait):
    hidden_ref, keep_ref, got_ref = resident
    hidden = jnp.where(
        place[1] == 0, hidden_ref[:16, :].astype(F32), hidden_ref[16:, :].astype(F32)
    )
    moe = keep_ref[...] + got_ref[...].astype(F32)
    outs[0][...] = (hidden + moe).astype(BF16)


def router_weights(ids, gates):
    name = jnp.arange(128, dtype=jnp.int32)[None, :]
    weights = jnp.zeros((ids.shape[0], 128), BF16)
    for k in range(TOP):
        weights = jnp.where(ids[:, k : k + 1] == name, gates[:, k : k + 1], weights)
    return weights


def by_core(step):
    route = []
    for c in range(16):
        way = step if c % 2 == 0 else -step
        for e in range(16):
            route.append((c * 16 + e, c * 16 + e // 8 * 8 + (e + way) % 8))
    return route


def on_both(block, route):
    return lax.ppermute(block, ("ctx", "exp"), route)


def two_swaps(ctx_bit, exp_bit):
    return [
        (c * 16 + e, (c ^ ctx_bit) * 16 + (e ^ exp_bit)) for c in range(16) for e in range(16)
    ]


def to_three(to_y, to_core, to_both):
    return (
        on_exp(to_y, Y_SWAP),
        on_ctx(to_core, CORE_SWAP),
        on_both(to_both, two_swaps(1, 8)),
    )


def shards(
    query,
    keys,
    values,
    out_proj,
    residual,
    norm_gain,
    expert_ids,
    gate_values,
    w_gate,
    w_up,
    w_down,
):
    ctx, exp = lax.axis_index("ctx"), lax.axis_index("exp")
    core, row, y, z = ctx % 2, ctx // 8, exp // 8, exp % 8
    place = jnp.stack([core, y, z, ctx]).astype(jnp.int32)
    kv_index = exp // (HEADS // KV_HEADS)
    block = jnp.concatenate(
        [
            lax.dynamic_slice_in_dim(keys, kv_index * HEAD_DIM, HEAD_DIM, 1),
            lax.dynamic_slice_in_dim(values, kv_index * HEAD_DIM, HEAD_DIM, 1),
        ],
        axis=1,
    )

    other = on_ctx(block, ROW_SWAP)
    rows, other = after(residual, other)
    pair = jnp.concatenate([block, other], axis=0)
    blocks = [pair] + [on_ctx(pair, x_shift(-d)) for d in DISTANCES[1:]]

    by_holder = query.reshape(2, 8, TOK_DEV, HEAD_DIM)
    by_holder = jnp.concatenate([by_holder, by_holder], axis=1)

    def rows_of(first):
        return lax.dynamic_slice_in_dim(by_holder, first % 8, 4, 1).reshape(128, HEAD_DIM)

    first = z + 7 - core
    quarter = D // 4
    w_part = lax.dynamic_slice_in_dim(out_proj, (core * 2 + row) * quarter, quarter, 1)
    part = on_exp(jnp.concatenate([rows_of(first + 4), w_part], axis=1), z_shift(4))
    mine = jnp.concatenate([rows_of(first), part[:, :HEAD_DIM]], axis=0)
    theirs = on_ctx(mine, CORE_SWAP)
    part_row = on_ctx(part, ROW_SWAP)
    w_parts = [part, part_row, on_ctx(part, CORE_SWAP), on_ctx(part_row, CORE_SWAP)]

    extended = jnp.concatenate([rows, router_weights(expert_ids, gate_values)], axis=1)
    extended_y = on_exp(extended, Y_SWAP)
    mine, extended_y = after(mine, extended_y)
    extended_others = [extended_y, on_ctx(extended, CORE_SWAP), on_ctx(extended_y, CORE_SWAP)]

    own, swap = kernel_call(
        attend_all,
        place,
        [mine, theirs, *blocks],
        [],
        [struct((256, 256), F32)] * 2,
        4 * 512 * 2048 * HEAD_DIM,
        512 * 2048,
    )
    joined = on_ctx(swap, CORE_SWAP)
    joined, *extended_others = after(joined, *extended_others)
    keep, *sends = kernel_call(
        project,
        place,
        [own, joined, *w_parts],
        [out_proj],
        [struct((32, D), F32)] + [struct((32, D), BF16)] * 3,
        2 * 128 * 256 * D,
        scratch=[pltpu.VMEM((256, HEAD_DIM), BF16)],
    )
    recvs = [
        on_exp(sends[0], z_shift(-1)),
        on_exp(sends[1], z_shift(1)),
        on_both(sends[2], by_core(2)),
    ]
    sums, send = kernel_call(
        add_up,
        place,
        [keep, *recvs],
        [],
        [struct((32, D), F32), struct((32, D), BF16)],
        3 * 32 * D,
    )
    hidden, round_0 = kernel_call(
        normalise,
        place,
        [extended, sums, norm_gain.reshape(1, D), *extended_others, *to_three(send, send, send)],
        [],
        [struct((32, D), BF16), struct((64, D + 128), BF16)],
        16 * 32 * D,
    )

    half = struct((32, D), BF16)
    w = [w_gate[0], w_up[0], w_down[0]]
    round_1 = on_both(round_0, by_core(1))
    round_2 = on_both(round_0, by_core(2))
    (seen,) = kernel_call(
        early, place, [round_0], [], [struct((8, 128), BF16)], 8 * 128, idle=w
    )
    round_2, seen = after(round_2, seen)
    round_3 = on_both(round_2, by_core(1))
    round_4 = on_both(round_2[:32], by_core(2))
    keep, got = run_expert(place, [round_1, round_2, round_0[:32]], w, [seen])
    keep_far, got_far = run_expert(place, [round_3, round_4], w)
    sum_1, sum_2, own_sum = run_join(place, keep, got, [half, half, struct((16, D), F32)])
    back_1 = on_both(sum_1, by_core(-1))
    back_2 = on_both(sum_2, by_core(-2))
    got_far, back_1 = after(got_far, back_1)
    sum_3, sum_4 = run_join(place, keep_far, got_far, [half, struct((16, D), BF16)])
    back_3 = on_both(sum_3, by_core(-3))
    back_4 = on_exp(sum_4, z_shift(4))
    keep, to_core = kernel_call(
        gather_up,
        place,
        [own_sum, back_4, back_1, back_2, back_3],
        [],
        [struct((16, D), F32), struct((16, D), BF16)],
        8 * 16 * D,
    )
    return kernel_call(
        finish,
        place,
        [hidden, keep, on_ctx(to_core, CORE_SWAP)],
        [],
        [struct((16, D), BF16)],
        3 * 16 * D,
    )[0]


def solution(mesh):
    return jax.shard_map(
        shards,
        mesh=mesh,
        in_specs=(
            P("ctx", "exp"),
            P("ctx", None),
            P("ctx", None),
            P("exp", None),
            P(("ctx", "exp"), None),
            P(),
            P(("ctx", "exp"), None),
            P(("ctx", "exp"), None),
            P("exp", None, None),
            P("exp", None, None),
            P("exp", None, None),
        ),
        out_specs=P(("ctx", "exp"), None),
        check_vma=False,
    )
```

```python
import math

import jax
import jax.numpy as jnp
from jax import lax
from jax.experimental import pallas as pl
from jax.experimental.pallas import tpu as pltpu
from jax.sharding import PartitionSpec as P

D = 2048
HEAD_DIM = 128
FF = 768
TOP = 8
HEADS = 16
KV_HEADS = 2
EXPERTS = 16
TOK_C = 256
TOK_DEV = 16
NEGATIVE = -1e30
SCALE = math.log2(math.e) / math.sqrt(HEAD_DIM)
F32 = jnp.float32
BF16 = jnp.bfloat16

CORE_SWAP = [(i, i ^ 1) for i in range(16)]
Y_SWAP = [(i, i ^ 8) for i in range(16)]


ROW_SWAP = [(i, i ^ 8) for i in range(16)]


def x_shift(step):
    return [(i, i // 8 * 8 + (i // 2 + step) % 4 * 2 + i % 2) for i in range(16)]


def z_shift(step):
    return [(y * 8 + z, y * 8 + (z + step) % 8) for y in range(2) for z in range(8)]


def on_ctx(block, route):
    return lax.ppermute(block, "ctx", route)


def on_exp(block, route):
    return lax.ppermute(block, "exp", route)


def kernel_call(
    body, scalars, resident, fetched, out_shapes, flops, transcendentals=0, limit=10, idle=(), scratch=()
):
    ins = [*resident, *fetched, *idle]
    n_res, n_fetch = len(resident), len(fetched)
    n_out = len(jax.tree.leaves(out_shapes))

    def whole(*refs):
        place, refs = refs[0], refs[1:]
        sources = refs[n_res : n_res + n_fetch]
        outs = refs[len(ins) : len(ins) + n_out]
        buffers = refs[len(ins) + n_out : len(ins) + n_out + n_fetch]
        copies = []
        for n in range(n_fetch):
            copies.append(
                pltpu.make_async_copy(sources[n], buffers[n], refs[len(ins) + n_out + n_fetch + n])
            )
        for copy in copies:
            copy.start()
        extra = refs[len(ins) + n_out + 2 * n_fetch :]
        body(place, refs[:n_res], buffers, (*outs, *extra), lambda n: copies[n].wait())

    size = sum(a.size * a.dtype.itemsize for a in [*resident, *fetched])
    vmem = pl.BlockSpec(memory_space=pltpu.VMEM)
    return pl.pallas_call(
        whole,
        out_shape=out_shapes,
        in_specs=[pl.BlockSpec(memory_space=pltpu.SMEM)]
        + [vmem] * n_res
        + [pl.BlockSpec(memory_space=pltpu.HBM)] * n_fetch
        + [vmem] * len(idle),
        out_specs=jax.tree.map(lambda _: vmem, out_shapes),
        scratch_shapes=[pltpu.VMEM(a.shape, a.dtype) for a in fetched]
        + [pltpu.SemaphoreType.DMA] * n_fetch
        + list(scratch),
        compiler_params=pltpu.CompilerParams(vmem_limit_bytes=limit * 1024 * 1024),
        cost_estimate=pl.CostEstimate(
            flops=flops, bytes_accessed=size, transcendentals=transcendentals
        ),
    )(scalars, *ins)


def after(value, *earlier):
    return lax.optimization_barrier((value, *earlier))


def struct(shape, dtype):
    return jax.ShapeDtypeStruct(shape, dtype)


ROWS_TILE = 256
DISTANCES = (0, -1, 1, 2)


def attend_all(place, resident, fetched, outs, wait):
    core, y, z, ctx = place[0], place[1], place[2], place[3]
    row, x = ctx // 8, lax.rem(ctx // 2, 4)
    sources = [(row ^ r) * 8 + lax.rem(x + d + 4, 4) * 2 + core for d in DISTANCES for r in (0, 1)]
    half = resident[0].shape[0]
    token = lax.broadcasted_iota(jnp.int32, (ROWS_TILE, 1), 0) & 127
    part = token >> 4
    key = lax.broadcasted_iota(jnp.int32, (1, TOK_C), 1)
    lane = lax.broadcasted_iota(jnp.int32, (ROWS_TILE, HEAD_DIM), 1)
    blocks = [ref.at[pl.ds(r * TOK_C, TOK_C)] for ref in resident[2:] for r in (0, 1)]
    for n, q_ref in enumerate(resident[:2]):
        q_ctx = ctx ^ n
        first = z + 7 - (core ^ n)
        local = (part >> 2) * 128 + (((part & 3) + first) & 7) * 16 + (token & 15)

        def rows(i, _, n=n, q_ref=q_ref, q_ctx=q_ctx, local=local):
            at = pl.ds(pl.multiple_of(i * ROWS_TILE, ROWS_TILE), ROWS_TILE)
            ahead = key - local
            queries = q_ref[at, :]
            parts = []
            for source, ref in zip(sources, blocks):
                scores = lax.dot_general(
                    queries,
                    ref[:, :HEAD_DIM],
                    (((1,), (1,)), ((), ())),
                    preferred_element_type=F32,
                )
                parts.append(
                    jnp.where(ahead <= (q_ctx - source) * TOK_C, scores, F32(NEGATIVE))
                )
            top = parts[0]
            for part in parts[1:]:
                top = jnp.maximum(top, part)
            top = jnp.max(top, axis=1, keepdims=True)
            total, mixed = 0.0, 0.0
            for part, ref in zip(parts, blocks):
                weights = jnp.exp2((part - top) * SCALE)
                total = total + weights
                mixed = mixed + jnp.dot(
                    weights.astype(BF16), ref[:, HEAD_DIM:], preferred_element_type=F32
                )
            total = jnp.sum(total, axis=1, keepdims=True)
            outs[n][at, :HEAD_DIM] = mixed
            outs[n][at, HEAD_DIM:] = jnp.where(lane < 64, top, total)
            return 0

        lax.fori_loop(0, half // ROWS_TILE, rows, 0)


def project(place, resident, fetched, outs, wait):
    own_ref, other_ref, *part_refs = resident
    (w_own_ref,) = fetched
    keep_ref, *send_refs, attn_ref = outs
    core, row = place[0], place[3] // 8
    own_top = own_ref[:, HEAD_DIM : HEAD_DIM + 1]
    other_top = other_ref[:, HEAD_DIM : HEAD_DIM + 1]
    top = jnp.maximum(own_top, other_top)
    own_factor = jnp.exp2((own_top - top) * SCALE)
    other_factor = jnp.exp2((other_top - top) * SCALE)
    total = own_ref[:, HEAD_DIM + 64 : HEAD_DIM + 65] * own_factor
    total = total + other_ref[:, HEAD_DIM + 64 : HEAD_DIM + 65] * other_factor
    mixed = own_ref[:, :HEAD_DIM] * own_factor + other_ref[:, :HEAD_DIM] * other_factor
    attn_ref[...] = (mixed / total).astype(BF16)

    def ordered(head):
        pieces = []
        for low, high in ((1, 2), (0, 1), (2, 3), (3, 0)):
            for half in range(2):
                start = head * 128 + half * 64 + jnp.where(core == 0, low, high) * 16
                pieces.append(attn_ref[pl.ds(pl.multiple_of(start, 16), 16), :])
        return jnp.concatenate(pieces, axis=0)

    heads = [ordered(0), ordered(1)]
    width = D // 4
    wait(0)
    for n, w_ref in enumerate(part_refs):
        column = ((core ^ (n // 2)) * 2 + (row ^ (n % 2))) * width
        at = pl.ds(pl.multiple_of(column, width), width)
        sums = jnp.dot(heads[0], w_own_ref[:, at], preferred_element_type=F32)
        sums = sums + jnp.dot(heads[1], w_ref[:, HEAD_DIM:], preferred_element_type=F32)
        keep_ref[:, at] = sums[:32]
        for s in range(3):
            send_refs[s][:, at] = sums[(s + 1) * 32 : (s + 2) * 32].astype(BF16)


def add_up(place, resident, fetched, outs, wait):
    sums = resident[0][...]
    for ref in resident[1:]:
        sums = sums + ref[...].astype(F32)
    outs[0][...] = sums
    outs[1][...] = sums.astype(BF16)


def normalise(place, resident, fetched, outs, wait):
    own_ref, sums_ref, gain_ref, y_ref, core_ref, both_ref = resident[:6]
    sums_y_ref, sums_core_ref, sums_both_ref = resident[6:]
    hidden_ref, normed_ref = outs
    y = place[1]
    for n in range(4):
        at = pl.ds(n % 2 * 16, 16)
        to = pl.ds(n * 16, 16)
        here, there = (own_ref, y_ref) if n < 2 else (core_ref, both_ref)
        extended = jnp.where(y == n % 2, here[...].astype(F32), there[...].astype(F32))
        if n < 2:
            projected = sums_ref[at, :] + sums_y_ref[at, :].astype(F32)
        else:
            projected = sums_core_ref[at, :].astype(F32) + sums_both_ref[at, :].astype(F32)
        hidden = (extended[:, :D] + projected).astype(BF16)
        wide = hidden.astype(F32)
        inverse = lax.rsqrt(jnp.mean(wide * wide, axis=-1, keepdims=True) + 1e-06)
        normed = (wide * inverse * gain_ref[...].astype(F32)).astype(BF16)
        if n < 2:
            hidden_ref[at, :] = hidden
        normed_ref[to, :D] = normed
        normed_ref[to, D:] = extended[:, D:].astype(BF16)


def early(place, resident, fetched, outs, wait):
    outs[0][...] = resident[0][:8, :128]


def expert(place, resident, fetched, outs, wait):
    gate_ref, up_ref, down_ref, *inputs = resident
    keep_ref, give_ref = outs
    y, z = place[1], place[2]
    rows = [ref[:, :D] for ref in inputs]
    weights = [ref[:, D:] for ref in inputs]
    rows = rows[0] if len(rows) == 1 else jnp.concatenate(rows, axis=0)
    weights = weights[0] if len(weights) == 1 else jnp.concatenate(weights, axis=0)
    lane = lax.broadcasted_iota(jnp.int32, weights.shape, 1)
    weight = jnp.where(lane == y * 8 + z, weights.astype(F32), 0.0)
    weight = jnp.sum(weight, axis=1, keepdims=True)
    gate_part = jnp.dot(rows, gate_ref[...], preferred_element_type=F32)
    up_part = jnp.dot(rows, up_ref[...], preferred_element_type=F32)
    inner = (gate_part * jax.nn.sigmoid(gate_part) * up_part).astype(BF16)
    result = jnp.dot(inner, down_ref[...], preferred_element_type=F32).astype(BF16)
    result = result.astype(F32) * weight
    for n in range(rows.shape[0] // 32):
        at = pl.ds(n * 16, 16)
        low, high = result[n * 32 : n * 32 + 16], result[n * 32 + 16 : n * 32 + 32]
        keep_ref[at, :] = jnp.where(y == 0, low, high)
        give_ref[at, :] = jnp.where(y == 0, high, low).astype(BF16)


def run_expert(place, rows, weights, idle=()):
    total = sum(r.shape[0] for r in rows)
    keep, give = kernel_call(
        expert,
        place,
        [*weights, *rows],
        [],
        [struct((total // 2, D), F32), struct((total // 2, D), BF16)],
        6 * total * D * FF,
        total * FF,
        idle=idle,
    )
    return keep, on_exp(give, Y_SWAP)


def join(place, resident, fetched, outs, wait):
    sums = resident[0][...] + resident[1][...].astype(F32)
    start = 0
    for out in outs:
        out[...] = sums[start : start + out.shape[0]].astype(out.dtype)
        start += out.shape[0]


def run_join(place, keep, got, outs):
    return kernel_call(join, place, [keep, got], [], outs, keep.size)


def gather_up(place, resident, fetched, outs, wait):
    own_ref, opposite_ref, *near_refs = resident
    mine = own_ref[...] + opposite_ref[...].astype(F32)
    theirs = 0.0
    for ref in near_refs:
        mine = mine + ref[:16, :].astype(F32)
        theirs = theirs + ref[16:, :].astype(F32)
    outs[0][...] = mine
    outs[1][...] = theirs.astype(BF16)


def finish(place, resident, fetched, outs, wait):
    hidden_ref, keep_ref, got_ref = resident
    hidden = jnp.where(
        place[1] == 0, hidden_ref[:16, :].astype(F32), hidden_ref[16:, :].astype(F32)
    )
    moe = keep_ref[...] + got_ref[...].astype(F32)
    outs[0][...] = (hidden + moe).astype(BF16)


def router_weights(ids, gates):
    name = jnp.arange(128, dtype=jnp.int32)[None, :]
    weights = jnp.zeros((ids.shape[0], 128), BF16)
    for k in range(TOP):
        weights = jnp.where(ids[:, k : k + 1] == name, gates[:, k : k + 1], weights)
    return weights


def by_core(step):
    route = []
    for c in range(16):
        way = step if c % 2 == 0 else -step
        for e in range(16):
            route.append((c * 16 + e, c * 16 + e // 8 * 8 + (e + way) % 8))
    return route


def on_both(block, route):
    return lax.ppermute(block, ("ctx", "exp"), route)


def two_swaps(ctx_bit, exp_bit):
    return [
        (c * 16 + e, (c ^ ctx_bit) * 16 + (e ^ exp_bit)) for c in range(16) for e in range(16)
    ]


def to_three(to_y, to_core, to_both):
    return (
        on_exp(to_y, Y_SWAP),
        on_ctx(to_core, CORE_SWAP),
        on_both(to_both, two_swaps(1, 8)),
    )


def shards(
    query,
    keys,
    values,
    out_proj,
    residual,
    norm_gain,
    expert_ids,
    gate_values,
    w_gate,
    w_up,
    w_down,
):
    ctx, exp = lax.axis_index("ctx"), lax.axis_index("exp")
    core, row, y, z = ctx % 2, ctx // 8, exp // 8, exp % 8
    place = jnp.stack([core, y, z, ctx]).astype(jnp.int32)
    kv_index = exp // (HEADS // KV_HEADS)
    block = jnp.concatenate(
        [
            lax.dynamic_slice_in_dim(keys, kv_index * HEAD_DIM, HEAD_DIM, 1),
            lax.dynamic_slice_in_dim(values, kv_index * HEAD_DIM, HEAD_DIM, 1),
        ],
        axis=1,
    )

    other = on_ctx(block, ROW_SWAP)
    rows, other = after(residual, other)
    pair = jnp.concatenate([block, other], axis=0)
    blocks = [pair] + [on_ctx(pair, x_shift(-d)) for d in DISTANCES[1:]]

    by_holder = query.reshape(2, 8, TOK_DEV, HEAD_DIM)
    by_holder = jnp.concatenate([by_holder, by_holder], axis=1)

    def rows_of(first):
        return lax.dynamic_slice_in_dim(by_holder, first % 8, 4, 1).reshape(128, HEAD_DIM)

    first = z + 7 - core
    quarter = D // 4
    w_part = lax.dynamic_slice_in_dim(out_proj, (core * 2 + row) * quarter, quarter, 1)
    part = on_exp(jnp.concatenate([rows_of(first + 4), w_part], axis=1), z_shift(4))
    mine = jnp.concatenate([rows_of(first), part[:, :HEAD_DIM]], axis=0)
    theirs = on_ctx(mine, CORE_SWAP)
    part_row = on_ctx(part, ROW_SWAP)
    w_parts = [part, part_row, on_ctx(part, CORE_SWAP), on_ctx(part_row, CORE_SWAP)]

    extended = jnp.concatenate([rows, router_weights(expert_ids, gate_values)], axis=1)
    extended_y = on_exp(extended, Y_SWAP)
    mine, extended_y = after(mine, extended_y)
    extended_others = [extended_y, on_ctx(extended, CORE_SWAP), on_ctx(extended_y, CORE_SWAP)]

    own, swap = kernel_call(
        attend_all,
        place,
        [mine, theirs, *blocks],
        [],
        [struct((256, 256), F32)] * 2,
        4 * 512 * 2048 * HEAD_DIM,
        512 * 2048,
    )
    joined = on_ctx(swap, CORE_SWAP)
    joined, *extended_others = after(joined, *extended_others)
    keep, *sends = kernel_call(
        project,
        place,
        [own, joined, *w_parts],
        [out_proj],
        [struct((32, D), F32)] + [struct((32, D), BF16)] * 3,
        2 * 128 * 256 * D,
        scratch=[pltpu.VMEM((256, HEAD_DIM), BF16)],
    )
    recvs = [
        on_exp(sends[0], z_shift(-1)),
        on_exp(sends[1], z_shift(1)),
        on_both(sends[2], by_core(2)),
    ]
    sums, send = kernel_call(
        add_up,
        place,
        [keep, *recvs],
        [],
        [struct((32, D), F32), struct((32, D), BF16)],
        3 * 32 * D,
    )
    hidden, round_0 = kernel_call(
        normalise,
        place,
        [extended, sums, norm_gain.reshape(1, D), *extended_others, *to_three(send, send, send)],
        [],
        [struct((32, D), BF16), struct((64, D + 128), BF16)],
        16 * 32 * D,
    )

    half = struct((32, D), BF16)
    w = [w_gate[0], w_up[0], w_down[0]]
    round_1 = on_both(round_0, by_core(1))
    round_2 = on_both(round_0, by_core(2))
    (seen,) = kernel_call(
        early, place, [round_0], [], [struct((8, 128), BF16)], 8 * 128, idle=w
    )
    round_2, seen = after(round_2, seen)
    round_3 = on_both(round_2, by_core(1))
    round_4 = on_both(round_2[:32], by_core(2))
    keep, got = run_expert(place, [round_1, round_2, round_0[:32]], w, [seen])
    keep_far, got_far = run_expert(place, [round_3, round_4], w)
    sum_1, sum_2, own_sum = run_join(place, keep, got, [half, half, struct((16, D), F32)])
    back_1 = on_both(sum_1, by_core(-1))
    back_2 = on_both(sum_2, by_core(-2))
    sum_3, sum_4 = run_join(place, keep_far, got_far, [half, struct((16, D), BF16)])
    back_3 = on_both(sum_3, by_core(-3))
    back_4 = on_exp(sum_4, z_shift(4))
    keep, to_core = kernel_call(
        gather_up,
        place,
        [own_sum, back_4, back_1, back_2, back_3],
        [],
        [struct((16, D), F32), struct((16, D), BF16)],
        8 * 16 * D,
    )
    return kernel_call(
        finish,
        place,
        [hidden, keep, on_ctx(to_core, CORE_SWAP)],
        [],
        [struct((16, D), BF16)],
        3 * 16 * D,
    )[0]


def solution(mesh):
    return jax.shard_map(
        shards,
        mesh=mesh,
        in_specs=(
            P("ctx", "exp"),
            P("ctx", None),
            P("ctx", None),
            P("exp", None),
            P(("ctx", "exp"), None),
            P(),
            P(("ctx", "exp"), None),
            P(("ctx", "exp"), None),
            P("exp", None, None),
            P("exp", None, None),
            P("exp", None, None),
        ),
        out_specs=P(("ctx", "exp"), None),
        check_vma=False,
    )
```

```python
import math

import jax
import jax.numpy as jnp
from jax import lax
from jax.experimental import pallas as pl
from jax.experimental.pallas import tpu as pltpu
from jax.sharding import PartitionSpec as P

D = 2048
HEAD_DIM = 128
FF = 768
TOP = 8
HEADS = 16
KV_HEADS = 2
EXPERTS = 16
TOK_C = 256
TOK_DEV = 16
NEGATIVE = -1e30
SCALE = math.log2(math.e) / math.sqrt(HEAD_DIM)
F32 = jnp.float32
BF16 = jnp.bfloat16

CORE_SWAP = [(i, i ^ 1) for i in range(16)]
Y_SWAP = [(i, i ^ 8) for i in range(16)]


ROW_SWAP = [(i, i ^ 8) for i in range(16)]


def x_shift(step):
    return [(i, i // 8 * 8 + (i // 2 + step) % 4 * 2 + i % 2) for i in range(16)]


def z_shift(step):
    return [(y * 8 + z, y * 8 + (z + step) % 8) for y in range(2) for z in range(8)]


def on_ctx(block, route):
    return lax.ppermute(block, "ctx", route)


def on_exp(block, route):
    return lax.ppermute(block, "exp", route)


def kernel_call(
    body, scalars, resident, fetched, out_shapes, flops, transcendentals=0, limit=10, idle=(), scratch=()
):
    ins = [*resident, *fetched, *idle]
    n_res, n_fetch = len(resident), len(fetched)
    n_out = len(jax.tree.leaves(out_shapes))

    def whole(*refs):
        place, refs = refs[0], refs[1:]
        sources = refs[n_res : n_res + n_fetch]
        outs = refs[len(ins) : len(ins) + n_out]
        buffers = refs[len(ins) + n_out : len(ins) + n_out + n_fetch]
        copies = []
        for n in range(n_fetch):
            copies.append(
                pltpu.make_async_copy(sources[n], buffers[n], refs[len(ins) + n_out + n_fetch + n])
            )
        for copy in copies:
            copy.start()
        extra = refs[len(ins) + n_out + 2 * n_fetch :]
        body(place, refs[:n_res], buffers, (*outs, *extra), lambda n: copies[n].wait())

    size = sum(a.size * a.dtype.itemsize for a in [*resident, *fetched])
    vmem = pl.BlockSpec(memory_space=pltpu.VMEM)
    return pl.pallas_call(
        whole,
        out_shape=out_shapes,
        in_specs=[pl.BlockSpec(memory_space=pltpu.SMEM)]
        + [vmem] * n_res
        + [pl.BlockSpec(memory_space=pltpu.HBM)] * n_fetch
        + [vmem] * len(idle),
        out_specs=jax.tree.map(lambda _: vmem, out_shapes),
        scratch_shapes=[pltpu.VMEM(a.shape, a.dtype) for a in fetched]
        + [pltpu.SemaphoreType.DMA] * n_fetch
        + list(scratch),
        compiler_params=pltpu.CompilerParams(vmem_limit_bytes=limit * 1024 * 1024),
        cost_estimate=pl.CostEstimate(
            flops=flops, bytes_accessed=size, transcendentals=transcendentals
        ),
    )(scalars, *ins)


def after(value, *earlier):
    return lax.optimization_barrier((value, *earlier))


def struct(shape, dtype):
    return jax.ShapeDtypeStruct(shape, dtype)


ROWS_TILE = 256
DISTANCES = (0, -1, 1, 2)


def attend_all(place, resident, fetched, outs, wait):
    core, y, z, ctx = place[0], place[1], place[2], place[3]
    row, x = ctx // 8, lax.rem(ctx // 2, 4)
    sources = [(row ^ r) * 8 + lax.rem(x + d + 4, 4) * 2 + core for d in DISTANCES for r in (0, 1)]
    half = resident[0].shape[0]
    token = lax.broadcasted_iota(jnp.int32, (ROWS_TILE, 1), 0) & 127
    part = token >> 4
    key = lax.broadcasted_iota(jnp.int32, (1, TOK_C), 1)
    lane = lax.broadcasted_iota(jnp.int32, (ROWS_TILE, HEAD_DIM), 1)
    blocks = [ref.at[pl.ds(r * TOK_C, TOK_C)] for ref in resident[2:] for r in (0, 1)]
    for n, q_ref in enumerate(resident[:2]):
        q_ctx = ctx ^ n
        first = z + 7 - (core ^ n)
        local = (part >> 2) * 128 + (((part & 3) + first) & 7) * 16 + (token & 15)

        def rows(i, _, n=n, q_ref=q_ref, q_ctx=q_ctx, local=local):
            at = pl.ds(pl.multiple_of(i * ROWS_TILE, ROWS_TILE), ROWS_TILE)
            ahead = key - local
            queries = q_ref[at, :]
            parts = []
            for source, ref in zip(sources, blocks):
                scores = lax.dot_general(
                    queries,
                    ref[:, :HEAD_DIM],
                    (((1,), (1,)), ((), ())),
                    preferred_element_type=F32,
                )
                parts.append(
                    jnp.where(ahead <= (q_ctx - source) * TOK_C, scores, F32(NEGATIVE))
                )
            top = parts[0]
            for part in parts[1:]:
                top = jnp.maximum(top, part)
            top = jnp.max(top, axis=1, keepdims=True)
            total, mixed = 0.0, 0.0
            for part, ref in zip(parts, blocks):
                weights = jnp.exp2((part - top) * SCALE)
                total = total + weights
                mixed = mixed + jnp.dot(
                    weights.astype(BF16), ref[:, HEAD_DIM:], preferred_element_type=F32
                )
            total = jnp.sum(total, axis=1, keepdims=True)
            outs[n][at, :HEAD_DIM] = mixed
            outs[n][at, HEAD_DIM:] = jnp.where(lane < 64, top, total)
            return 0

        lax.fori_loop(0, half // ROWS_TILE, rows, 0)


def project(place, resident, fetched, outs, wait):
    own_ref, other_ref, *part_refs = resident
    (w_own_ref,) = fetched
    keep_ref, *send_refs, attn_ref = outs
    core, row = place[0], place[3] // 8
    own_top = own_ref[:, HEAD_DIM : HEAD_DIM + 1]
    other_top = other_ref[:, HEAD_DIM : HEAD_DIM + 1]
    top = jnp.maximum(own_top, other_top)
    own_factor = jnp.exp2((own_top - top) * SCALE)
    other_factor = jnp.exp2((other_top - top) * SCALE)
    total = own_ref[:, HEAD_DIM + 64 : HEAD_DIM + 65] * own_factor
    total = total + other_ref[:, HEAD_DIM + 64 : HEAD_DIM + 65] * other_factor
    mixed = own_ref[:, :HEAD_DIM] * own_factor + other_ref[:, :HEAD_DIM] * other_factor
    attn_ref[...] = (mixed / total).astype(BF16)

    def ordered(head):
        pieces = []
        for low, high in ((1, 2), (0, 1), (2, 3), (3, 0)):
            for half in range(2):
                start = head * 128 + half * 64 + jnp.where(core == 0, low, high) * 16
                pieces.append(attn_ref[pl.ds(pl.multiple_of(start, 16), 16), :])
        return jnp.concatenate(pieces, axis=0)

    heads = [ordered(0), ordered(1)]
    width = D // 4
    wait(0)
    for n, w_ref in enumerate(part_refs):
        column = ((core ^ (n // 2)) * 2 + (row ^ (n % 2))) * width
        at = pl.ds(pl.multiple_of(column, width), width)
        sums = jnp.dot(heads[0], w_own_ref[:, at], preferred_element_type=F32)
        sums = sums + jnp.dot(heads[1], w_ref[:, HEAD_DIM:], preferred_element_type=F32)
        keep_ref[:, at] = sums[:32]
        for s in range(3):
            send_refs[s][:, at] = sums[(s + 1) * 32 : (s + 2) * 32].astype(BF16)


def add_up(place, resident, fetched, outs, wait):
    sums = resident[0][...]
    for ref in resident[1:]:
        sums = sums + ref[...].astype(F32)
    outs[0][...] = sums
    outs[1][...] = sums.astype(BF16)


def normalise(place, resident, fetched, outs, wait):
    own_ref, sums_ref, gain_ref, y_ref, core_ref, both_ref = resident[:6]
    sums_y_ref, sums_core_ref, sums_both_ref = resident[6:]
    hidden_ref, normed_ref = outs
    y = place[1]
    for n in range(4):
        at = pl.ds(n % 2 * 16, 16)
        to = pl.ds(n * 16, 16)
        here, there = (own_ref, y_ref) if n < 2 else (core_ref, both_ref)
        extended = jnp.where(y == n % 2, here[...].astype(F32), there[...].astype(F32))
        if n < 2:
            projected = sums_ref[at, :] + sums_y_ref[at, :].astype(F32)
        else:
            projected = sums_core_ref[at, :].astype(F32) + sums_both_ref[at, :].astype(F32)
        hidden = (extended[:, :D] + projected).astype(BF16)
        wide = hidden.astype(F32)
        inverse = lax.rsqrt(jnp.mean(wide * wide, axis=-1, keepdims=True) + 1e-06)
        normed = (wide * inverse * gain_ref[...].astype(F32)).astype(BF16)
        if n < 2:
            hidden_ref[at, :] = hidden
        normed_ref[to, :D] = normed
        normed_ref[to, D:] = extended[:, D:].astype(BF16)


def early(place, resident, fetched, outs, wait):
    outs[0][...] = resident[0][:8, :128]


def expert(place, resident, fetched, outs, wait):
    gate_ref, up_ref, down_ref, *inputs = resident
    keep_ref, give_ref = outs
    y, z = place[1], place[2]
    rows = [ref[:, :D] for ref in inputs]
    weights = [ref[:, D:] for ref in inputs]
    rows = rows[0] if len(rows) == 1 else jnp.concatenate(rows, axis=0)
    weights = weights[0] if len(weights) == 1 else jnp.concatenate(weights, axis=0)
    lane = lax.broadcasted_iota(jnp.int32, weights.shape, 1)
    weight = jnp.where(lane == y * 8 + z, weights.astype(F32), 0.0)
    weight = jnp.sum(weight, axis=1, keepdims=True)
    gate_part = jnp.dot(rows, gate_ref[...], preferred_element_type=F32)
    up_part = jnp.dot(rows, up_ref[...], preferred_element_type=F32)
    inner = (gate_part * jax.nn.sigmoid(gate_part) * up_part).astype(BF16)
    result = jnp.dot(inner, down_ref[...], preferred_element_type=F32).astype(BF16)
    result = result.astype(F32) * weight
    for n in range(rows.shape[0] // 32):
        at = pl.ds(n * 16, 16)
        low, high = result[n * 32 : n * 32 + 16], result[n * 32 + 16 : n * 32 + 32]
        keep_ref[at, :] = jnp.where(y == 0, low, high)
        give_ref[at, :] = jnp.where(y == 0, high, low).astype(BF16)


def run_expert(place, rows, weights, idle=()):
    total = sum(r.shape[0] for r in rows)
    keep, give = kernel_call(
        expert,
        place,
        [*weights, *rows],
        [],
        [struct((total // 2, D), F32), struct((total // 2, D), BF16)],
        6 * total * D * FF,
        total * FF,
        idle=idle,
    )
    return keep, on_exp(give, Y_SWAP)


def join(place, resident, fetched, outs, wait):
    sums = resident[0][...] + resident[1][...].astype(F32)
    start = 0
    for out in outs:
        out[...] = sums[start : start + out.shape[0]].astype(out.dtype)
        start += out.shape[0]


def run_join(place, keep, got, outs):
    return kernel_call(join, place, [keep, got], [], outs, keep.size)


def gather_up(place, resident, fetched, outs, wait):
    own_ref, opposite_ref, *near_refs = resident
    mine = own_ref[...] + opposite_ref[...].astype(F32)
    theirs = 0.0
    for ref in near_refs:
        mine = mine + ref[:16, :].astype(F32)
        theirs = theirs + ref[16:, :].astype(F32)
    outs[0][...] = mine
    outs[1][...] = theirs.astype(BF16)


def finish(place, resident, fetched, outs, wait):
    hidden_ref, keep_ref, got_ref = resident
    hidden = jnp.where(
        place[1] == 0, hidden_ref[:16, :].astype(F32), hidden_ref[16:, :].astype(F32)
    )
    moe = keep_ref[...] + got_ref[...].astype(F32)
    outs[0][...] = (hidden + moe).astype(BF16)


def router_weights(ids, gates):
    name = jnp.arange(128, dtype=jnp.int32)[None, :]
    weights = jnp.zeros((ids.shape[0], 128), BF16)
    for k in range(TOP):
        weights = jnp.where(ids[:, k : k + 1] == name, gates[:, k : k + 1], weights)
    return weights


def by_core(step):
    route = []
    for c in range(16):
        way = step if c % 2 == 0 else -step
        for e in range(16):
            route.append((c * 16 + e, c * 16 + e // 8 * 8 + (e + way) % 8))
    return route


def on_both(block, route):
    return lax.ppermute(block, ("ctx", "exp"), route)


def two_swaps(ctx_bit, exp_bit):
    return [
        (c * 16 + e, (c ^ ctx_bit) * 16 + (e ^ exp_bit)) for c in range(16) for e in range(16)
    ]


def to_three(to_y, to_core, to_both):
    return (
        on_exp(to_y, Y_SWAP),
        on_ctx(to_core, CORE_SWAP),
        on_both(to_both, two_swaps(1, 8)),
    )


def shards(
    query,
    keys,
    values,
    out_proj,
    residual,
    norm_gain,
    expert_ids,
    gate_values,
    w_gate,
    w_up,
    w_down,
):
    ctx, exp = lax.axis_index("ctx"), lax.axis_index("exp")
    core, row, y, z = ctx % 2, ctx // 8, exp // 8, exp % 8
    place = jnp.stack([core, y, z, ctx]).astype(jnp.int32)
    kv_index = exp // (HEADS // KV_HEADS)
    block = jnp.concatenate(
        [
            lax.dynamic_slice_in_dim(keys, kv_index * HEAD_DIM, HEAD_DIM, 1),
            lax.dynamic_slice_in_dim(values, kv_index * HEAD_DIM, HEAD_DIM, 1),
        ],
        axis=1,
    )

    other = on_ctx(block, ROW_SWAP)
    rows, other = after(residual, other)
    pair = jnp.concatenate([block, other], axis=0)
    blocks = [pair] + [on_ctx(pair, x_shift(-d)) for d in DISTANCES[1:]]

    by_holder = query.reshape(2, 8, TOK_DEV, HEAD_DIM)
    by_holder = jnp.concatenate([by_holder, by_holder], axis=1)

    def rows_of(first):
        return lax.dynamic_slice_in_dim(by_holder, first % 8, 4, 1).reshape(128, HEAD_DIM)

    first = z + 7 - core
    quarter = D // 4
    w_part = lax.dynamic_slice_in_dim(out_proj, (core * 2 + row) * quarter, quarter, 1)
    part = on_exp(jnp.concatenate([rows_of(first + 4), w_part], axis=1), z_shift(4))
    mine = jnp.concatenate([rows_of(first), part[:, :HEAD_DIM]], axis=0)
    theirs = on_ctx(mine, CORE_SWAP)
    part_row = on_ctx(part, ROW_SWAP)
    w_parts = [part, part_row, on_ctx(part, CORE_SWAP), on_ctx(part_row, CORE_SWAP)]

    extended = jnp.concatenate([rows, router_weights(expert_ids, gate_values)], axis=1)
    extended_y = on_exp(extended, Y_SWAP)
    mine, extended_y = after(mine, extended_y)
    extended_others = [extended_y, on_ctx(extended, CORE_SWAP), on_ctx(extended_y, CORE_SWAP)]

    own, swap = kernel_call(
        attend_all,
        place,
        [mine, theirs, *blocks],
        [],
        [struct((256, 256), F32)] * 2,
        4 * 512 * 2048 * HEAD_DIM,
        512 * 2048,
    )
    joined = on_ctx(swap, CORE_SWAP)
    joined, *extended_others = after(joined, *extended_others)
    keep, *sends = kernel_call(
        project,
        place,
        [own, joined, *w_parts],
        [out_proj],
        [struct((32, D), F32)] + [struct((32, D), BF16)] * 3,
        2 * 128 * 256 * D,
        scratch=[pltpu.VMEM((256, HEAD_DIM), BF16)],
    )
    recvs = [
        on_exp(sends[0], z_shift(-1)),
        on_exp(sends[1], z_shift(1)),
        on_both(sends[2], by_core(2)),
    ]
    sums, send = kernel_call(
        add_up,
        place,
        [keep, *recvs],
        [],
        [struct((32, D), F32), struct((32, D), BF16)],
        3 * 32 * D,
    )
    sums_y = on_exp(send, Y_SWAP)
    sums_others = [sums_y, on_ctx(send, CORE_SWAP), on_ctx(sums_y, CORE_SWAP)]
    hidden, round_0 = kernel_call(
        normalise,
        place,
        [extended, sums, norm_gain.reshape(1, D), *extended_others, *sums_others],
        [],
        [struct((32, D), BF16), struct((64, D + 128), BF16)],
        16 * 32 * D,
    )

    half = struct((32, D), BF16)
    w = [w_gate[0], w_up[0], w_down[0]]
    round_2 = on_both(round_0, by_core(2))
    round_1 = on_both(round_0, by_core(1))
    (seen,) = kernel_call(
        early, place, [round_0], [], [struct((8, 128), BF16)], 8 * 128, idle=w
    )
    round_2, seen = after(round_2, seen)
    round_3 = on_both(round_2, by_core(1))
    round_4 = on_both(round_2[:32], by_core(2))
    keep, got = run_expert(place, [round_1, round_2, round_0[:32]], w, [seen])
    keep_far, got_far = run_expert(place, [round_3, round_4], w)
    sum_1, sum_2, own_sum = run_join(place, keep, got, [half, half, struct((16, D), F32)])
    back_1 = on_both(sum_1, by_core(-1))
    back_2 = on_both(sum_2, by_core(-2))
    sum_3, sum_4 = run_join(place, keep_far, got_far, [half, struct((16, D), BF16)])
    back_3 = on_both(sum_3, by_core(-3))
    back_4 = on_exp(sum_4, z_shift(4))
    keep, to_core = kernel_call(
        gather_up,
        place,
        [own_sum, back_4, back_1, back_2, back_3],
        [],
        [struct((16, D), F32), struct((16, D), BF16)],
        8 * 16 * D,
    )
    return kernel_call(
        finish,
        place,
        [hidden, keep, on_ctx(to_core, CORE_SWAP)],
        [],
        [struct((16, D), BF16)],
        3 * 16 * D,
    )[0]


def solution(mesh):
    return jax.shard_map(
        shards,
        mesh=mesh,
        in_specs=(
            P("ctx", "exp"),
            P("ctx", None),
            P("ctx", None),
            P("exp", None),
            P(("ctx", "exp"), None),
            P(),
            P(("ctx", "exp"), None),
            P(("ctx", "exp"), None),
            P("exp", None, None),
            P("exp", None, None),
            P("exp", None, None),
        ),
        out_specs=P(("ctx", "exp"), None),
        check_vma=False,
    )
```

```python
import math

import jax
import jax.numpy as jnp
from jax import lax
from jax.experimental import pallas as pl
from jax.experimental.pallas import tpu as pltpu
from jax.sharding import PartitionSpec as P

D = 2048
HEAD_DIM = 128
FF = 768
TOP = 8
HEADS = 16
KV_HEADS = 2
EXPERTS = 16
TOK_C = 256
TOK_DEV = 16
NEGATIVE = -1e30
SCALE = math.log2(math.e) / math.sqrt(HEAD_DIM)
F32 = jnp.float32
BF16 = jnp.bfloat16

CORE_SWAP = [(i, i ^ 1) for i in range(16)]
Y_SWAP = [(i, i ^ 8) for i in range(16)]


ROW_SWAP = [(i, i ^ 8) for i in range(16)]


def x_shift(step):
    return [(i, i // 8 * 8 + (i // 2 + step) % 4 * 2 + i % 2) for i in range(16)]


def z_shift(step):
    return [(y * 8 + z, y * 8 + (z + step) % 8) for y in range(2) for z in range(8)]


def on_ctx(block, route):
    return lax.ppermute(block, "ctx", route)


def on_exp(block, route):
    return lax.ppermute(block, "exp", route)


def kernel_call(
    body, scalars, resident, fetched, out_shapes, flops, transcendentals=0, limit=10, idle=(), scratch=()
):
    ins = [*resident, *fetched, *idle]
    n_res, n_fetch = len(resident), len(fetched)
    n_out = len(jax.tree.leaves(out_shapes))

    def whole(*refs):
        place, refs = refs[0], refs[1:]
        sources = refs[n_res : n_res + n_fetch]
        outs = refs[len(ins) : len(ins) + n_out]
        buffers = refs[len(ins) + n_out : len(ins) + n_out + n_fetch]
        copies = []
        for n in range(n_fetch):
            copies.append(
                pltpu.make_async_copy(sources[n], buffers[n], refs[len(ins) + n_out + n_fetch + n])
            )
        for copy in copies:
            copy.start()
        extra = refs[len(ins) + n_out + 2 * n_fetch :]
        body(place, refs[:n_res], buffers, (*outs, *extra), lambda n: copies[n].wait())

    size = sum(a.size * a.dtype.itemsize for a in [*resident, *fetched])
    vmem = pl.BlockSpec(memory_space=pltpu.VMEM)
    return pl.pallas_call(
        whole,
        out_shape=out_shapes,
        in_specs=[pl.BlockSpec(memory_space=pltpu.SMEM)]
        + [vmem] * n_res
        + [pl.BlockSpec(memory_space=pltpu.HBM)] * n_fetch
        + [vmem] * len(idle),
        out_specs=jax.tree.map(lambda _: vmem, out_shapes),
        scratch_shapes=[pltpu.VMEM(a.shape, a.dtype) for a in fetched]
        + [pltpu.SemaphoreType.DMA] * n_fetch
        + list(scratch),
        compiler_params=pltpu.CompilerParams(vmem_limit_bytes=limit * 1024 * 1024),
        cost_estimate=pl.CostEstimate(
            flops=flops, bytes_accessed=size, transcendentals=transcendentals
        ),
    )(scalars, *ins)


def after(value, *earlier):
    return lax.optimization_barrier((value, *earlier))


def struct(shape, dtype):
    return jax.ShapeDtypeStruct(shape, dtype)


ROWS_TILE = 256
DISTANCES = (0, -1, 1, 2)


def attend_all(place, resident, fetched, outs, wait):
    core, y, z, ctx = place[0], place[1], place[2], place[3]
    row, x = ctx // 8, lax.rem(ctx // 2, 4)
    sources = [(row ^ r) * 8 + lax.rem(x + d + 4, 4) * 2 + core for d in DISTANCES for r in (0, 1)]
    half = resident[0].shape[0]
    token = lax.broadcasted_iota(jnp.int32, (ROWS_TILE, 1), 0) & 127
    part = token >> 4
    key = lax.broadcasted_iota(jnp.int32, (1, TOK_C), 1)
    lane = lax.broadcasted_iota(jnp.int32, (ROWS_TILE, HEAD_DIM), 1)
    blocks = [ref.at[pl.ds(r * TOK_C, TOK_C)] for ref in resident[2:] for r in (0, 1)]
    for n, q_ref in enumerate(resident[:2]):
        q_ctx = ctx ^ n
        first = z + 7 - (core ^ n)
        local = (part >> 2) * 128 + (((part & 3) + first) & 7) * 16 + (token & 15)

        def rows(i, _, n=n, q_ref=q_ref, q_ctx=q_ctx, local=local):
            at = pl.ds(pl.multiple_of(i * ROWS_TILE, ROWS_TILE), ROWS_TILE)
            ahead = key - local
            queries = q_ref[at, :]
            parts = []
            for source, ref in zip(sources, blocks):
                scores = lax.dot_general(
                    queries,
                    ref[:, :HEAD_DIM],
                    (((1,), (1,)), ((), ())),
                    preferred_element_type=F32,
                )
                parts.append(
                    jnp.where(ahead <= (q_ctx - source) * TOK_C, scores, F32(NEGATIVE))
                )
            top = parts[0]
            for part in parts[1:]:
                top = jnp.maximum(top, part)
            top = jnp.max(top, axis=1, keepdims=True)
            total, mixed = 0.0, 0.0
            for part, ref in zip(parts, blocks):
                weights = jnp.exp2((part - top) * SCALE)
                total = total + weights
                mixed = mixed + jnp.dot(
                    weights.astype(BF16), ref[:, HEAD_DIM:], preferred_element_type=F32
                )
            total = jnp.sum(total, axis=1, keepdims=True)
            outs[n][at, :HEAD_DIM] = mixed
            outs[n][at, HEAD_DIM:] = jnp.where(lane < 64, top, total)
            return 0

        lax.fori_loop(0, half // ROWS_TILE, rows, 0)


def project(place, resident, fetched, outs, wait):
    own_ref, other_ref, *part_refs = resident
    (w_own_ref,) = fetched
    keep_ref, *send_refs, attn_ref = outs
    core, row = place[0], place[3] // 8
    own_top = own_ref[:, HEAD_DIM : HEAD_DIM + 1]
    other_top = other_ref[:, HEAD_DIM : HEAD_DIM + 1]
    top = jnp.maximum(own_top, other_top)
    own_factor = jnp.exp2((own_top - top) * SCALE)
    other_factor = jnp.exp2((other_top - top) * SCALE)
    total = own_ref[:, HEAD_DIM + 64 : HEAD_DIM + 65] * own_factor
    total = total + other_ref[:, HEAD_DIM + 64 : HEAD_DIM + 65] * other_factor
    mixed = own_ref[:, :HEAD_DIM] * own_factor + other_ref[:, :HEAD_DIM] * other_factor
    attn_ref[...] = (mixed / total).astype(BF16)

    def ordered(head):
        pieces = []
        for low, high in ((1, 2), (0, 1), (2, 3), (3, 0)):
            for half in range(2):
                start = head * 128 + half * 64 + jnp.where(core == 0, low, high) * 16
                pieces.append(attn_ref[pl.ds(pl.multiple_of(start, 16), 16), :])
        return jnp.concatenate(pieces, axis=0)

    heads = [ordered(0), ordered(1)]
    width = D // 4
    wait(0)
    for n, w_ref in enumerate(part_refs):
        column = ((core ^ (n // 2)) * 2 + (row ^ (n % 2))) * width
        at = pl.ds(pl.multiple_of(column, width), width)
        sums = jnp.dot(heads[0], w_own_ref[:, at], preferred_element_type=F32)
        sums = sums + jnp.dot(heads[1], w_ref[:, HEAD_DIM:], preferred_element_type=F32)
        keep_ref[:, at] = sums[:32]
        for s in range(3):
            send_refs[s][:, at] = sums[(s + 1) * 32 : (s + 2) * 32].astype(BF16)


def add_up(place, resident, fetched, outs, wait):
    sums = resident[0][...]
    for ref in resident[1:]:
        sums = sums + ref[...].astype(F32)
    outs[0][...] = sums
    outs[1][...] = sums.astype(BF16)


def normalise(place, resident, fetched, outs, wait):
    own_ref, sums_ref, gain_ref, y_ref, core_ref, both_ref = resident[:6]
    sums_y_ref, sums_core_ref, sums_both_ref = resident[6:]
    hidden_ref, normed_ref = outs
    y = place[1]
    for n in range(4):
        at = pl.ds(n % 2 * 16, 16)
        to = pl.ds(n * 16, 16)
        here, there = (own_ref, y_ref) if n < 2 else (core_ref, both_ref)
        extended = jnp.where(y == n % 2, here[...].astype(F32), there[...].astype(F32))
        if n < 2:
            projected = sums_ref[at, :] + sums_y_ref[at, :].astype(F32)
        else:
            projected = sums_core_ref[at, :].astype(F32) + sums_both_ref[at, :].astype(F32)
        hidden = (extended[:, :D] + projected).astype(BF16)
        wide = hidden.astype(F32)
        inverse = lax.rsqrt(jnp.mean(wide * wide, axis=-1, keepdims=True) + 1e-06)
        normed = (wide * inverse * gain_ref[...].astype(F32)).astype(BF16)
        if n < 2:
            hidden_ref[at, :] = hidden
        normed_ref[to, :D] = normed
        normed_ref[to, D:] = extended[:, D:].astype(BF16)


def early(place, resident, fetched, outs, wait):
    outs[0][...] = resident[0][:16, :128]


def expert(place, resident, fetched, outs, wait):
    gate_ref, up_ref, down_ref, *inputs = resident
    keep_ref, give_ref = outs
    y, z = place[1], place[2]
    rows = [ref[:, :D] for ref in inputs]
    weights = [ref[:, D:] for ref in inputs]
    rows = rows[0] if len(rows) == 1 else jnp.concatenate(rows, axis=0)
    weights = weights[0] if len(weights) == 1 else jnp.concatenate(weights, axis=0)
    lane = lax.broadcasted_iota(jnp.int32, weights.shape, 1)
    weight = jnp.where(lane == y * 8 + z, weights.astype(F32), 0.0)
    weight = jnp.sum(weight, axis=1, keepdims=True)
    gate_part = jnp.dot(rows, gate_ref[...], preferred_element_type=F32)
    up_part = jnp.dot(rows, up_ref[...], preferred_element_type=F32)
    inner = (gate_part * jax.nn.sigmoid(gate_part) * up_part).astype(BF16)
    result = jnp.dot(inner, down_ref[...], preferred_element_type=F32).astype(BF16)
    result = result.astype(F32) * weight
    for n in range(rows.shape[0] // 32):
        at = pl.ds(n * 16, 16)
        low, high = result[n * 32 : n * 32 + 16], result[n * 32 + 16 : n * 32 + 32]
        keep_ref[at, :] = jnp.where(y == 0, low, high)
        give_ref[at, :] = jnp.where(y == 0, high, low).astype(BF16)


def run_expert(place, rows, weights, idle=()):
    total = sum(r.shape[0] for r in rows)
    keep, give = kernel_call(
        expert,
        place,
        [*weights, *rows],
        [],
        [struct((total // 2, D), F32), struct((total // 2, D), BF16)],
        6 * total * D * FF,
        total * FF,
        idle=idle,
    )
    return keep, on_exp(give, Y_SWAP)


def join(place, resident, fetched, outs, wait):
    sums = resident[0][...] + resident[1][...].astype(F32)
    start = 0
    for out in outs:
        out[...] = sums[start : start + out.shape[0]].astype(out.dtype)
        start += out.shape[0]


def run_join(place, keep, got, outs):
    return kernel_call(join, place, [keep, got], [], outs, keep.size)


def gather_up(place, resident, fetched, outs, wait):
    own_ref, opposite_ref, *near_refs = resident
    mine = own_ref[...] + opposite_ref[...].astype(F32)
    theirs = 0.0
    for ref in near_refs:
        mine = mine + ref[:16, :].astype(F32)
        theirs = theirs + ref[16:, :].astype(F32)
    outs[0][...] = mine
    outs[1][...] = theirs.astype(BF16)


def finish(place, resident, fetched, outs, wait):
    hidden_ref, keep_ref, got_ref = resident
    hidden = jnp.where(
        place[1] == 0, hidden_ref[:16, :].astype(F32), hidden_ref[16:, :].astype(F32)
    )
    moe = keep_ref[...] + got_ref[...].astype(F32)
    outs[0][...] = (hidden + moe).astype(BF16)


def router_weights(ids, gates):
    name = jnp.arange(128, dtype=jnp.int32)[None, :]
    weights = jnp.zeros((ids.shape[0], 128), BF16)
    for k in range(TOP):
        weights = jnp.where(ids[:, k : k + 1] == name, gates[:, k : k + 1], weights)
    return weights


def by_core(step):
    route = []
    for c in range(16):
        way = step if c % 2 == 0 else -step
        for e in range(16):
            route.append((c * 16 + e, c * 16 + e // 8 * 8 + (e + way) % 8))
    return route


def on_both(block, route):
    return lax.ppermute(block, ("ctx", "exp"), route)


def two_swaps(ctx_bit, exp_bit):
    return [
        (c * 16 + e, (c ^ ctx_bit) * 16 + (e ^ exp_bit)) for c in range(16) for e in range(16)
    ]


def to_three(to_y, to_core, to_both):
    return (
        on_exp(to_y, Y_SWAP),
        on_ctx(to_core, CORE_SWAP),
        on_both(to_both, two_swaps(1, 8)),
    )


def shards(
    query,
    keys,
    values,
    out_proj,
    residual,
    norm_gain,
    expert_ids,
    gate_values,
    w_gate,
    w_up,
    w_down,
):
    ctx, exp = lax.axis_index("ctx"), lax.axis_index("exp")
    core, row, y, z = ctx % 2, ctx // 8, exp // 8, exp % 8
    place = jnp.stack([core, y, z, ctx]).astype(jnp.int32)
    kv_index = exp // (HEADS // KV_HEADS)
    block = jnp.concatenate(
        [
            lax.dynamic_slice_in_dim(keys, kv_index * HEAD_DIM, HEAD_DIM, 1),
            lax.dynamic_slice_in_dim(values, kv_index * HEAD_DIM, HEAD_DIM, 1),
        ],
        axis=1,
    )

    other = on_ctx(block, ROW_SWAP)
    rows, other = after(residual, other)
    pair = jnp.concatenate([block, other], axis=0)
    blocks = [pair] + [on_ctx(pair, x_shift(-d)) for d in DISTANCES[1:]]

    by_holder = query.reshape(2, 8, TOK_DEV, HEAD_DIM)
    by_holder = jnp.concatenate([by_holder, by_holder], axis=1)

    def rows_of(first):
        return lax.dynamic_slice_in_dim(by_holder, first % 8, 4, 1).reshape(128, HEAD_DIM)

    first = z + 7 - core
    quarter = D // 4
    w_part = lax.dynamic_slice_in_dim(out_proj, (core * 2 + row) * quarter, quarter, 1)
    part = on_exp(jnp.concatenate([rows_of(first + 4), w_part], axis=1), z_shift(4))
    mine = jnp.concatenate([rows_of(first), part[:, :HEAD_DIM]], axis=0)
    theirs = on_ctx(mine, CORE_SWAP)
    part_row = on_ctx(part, ROW_SWAP)
    w_parts = [part, part_row, on_ctx(part, CORE_SWAP), on_ctx(part_row, CORE_SWAP)]

    extended = jnp.concatenate([rows, router_weights(expert_ids, gate_values)], axis=1)
    extended_y = on_exp(extended, Y_SWAP)
    mine, extended_y = after(mine, extended_y)
    extended_others = [extended_y, on_ctx(extended, CORE_SWAP), on_ctx(extended_y, CORE_SWAP)]

    own, swap = kernel_call(
        attend_all,
        place,
        [mine, theirs, *blocks],
        [],
        [struct((256, 256), F32)] * 2,
        4 * 512 * 2048 * HEAD_DIM,
        512 * 2048,
    )
    joined = on_ctx(swap, CORE_SWAP)
    joined, *extended_others = after(joined, *extended_others)
    keep, *sends = kernel_call(
        project,
        place,
        [own, joined, *w_parts],
        [out_proj],
        [struct((32, D), F32)] + [struct((32, D), BF16)] * 3,
        2 * 128 * 256 * D,
        scratch=[pltpu.VMEM((256, HEAD_DIM), BF16)],
    )
    recvs = [
        on_exp(sends[0], z_shift(-1)),
        on_exp(sends[1], z_shift(1)),
        on_both(sends[2], by_core(2)),
    ]
    sums, send = kernel_call(
        add_up,
        place,
        [keep, *recvs],
        [],
        [struct((32, D), F32), struct((32, D), BF16)],
        3 * 32 * D,
    )
    sums_y = on_exp(send, Y_SWAP)
    sums_others = [sums_y, on_ctx(send, CORE_SWAP), on_ctx(sums_y, CORE_SWAP)]
    hidden, round_0 = kernel_call(
        normalise,
        place,
        [extended, sums, norm_gain.reshape(1, D), *extended_others, *sums_others],
        [],
        [struct((32, D), BF16), struct((64, D + 128), BF16)],
        16 * 32 * D,
    )

    half = struct((32, D), BF16)
    w = [w_gate[0], w_up[0], w_down[0]]
    round_2 = on_both(round_0, by_core(2))
    round_1 = on_both(round_0, by_core(1))
    (seen,) = kernel_call(
        early, place, [round_0], [], [struct((16, 128), BF16)], 16 * 128, idle=w
    )
    round_2, seen = after(round_2, seen)
    round_3 = on_both(round_2, by_core(1))
    round_4 = on_both(round_2[:32], by_core(2))
    keep, got = run_expert(place, [round_1, round_2, round_0[:32]], w, [seen])
    keep_far, got_far = run_expert(place, [round_3, round_4], w)
    sum_1, sum_2, own_sum = run_join(place, keep, got, [half, half, struct((16, D), F32)])
    back_1 = on_both(sum_1, by_core(-1))
    back_2 = on_both(sum_2, by_core(-2))
    sum_3, sum_4 = run_join(place, keep_far, got_far, [half, struct((16, D), BF16)])
    back_3 = on_both(sum_3, by_core(-3))
    back_4 = on_exp(sum_4, z_shift(4))
    keep, to_core = kernel_call(
        gather_up,
        place,
        [own_sum, back_4, back_1, back_2, back_3],
        [],
        [struct((16, D), F32), struct((16, D), BF16)],
        8 * 16 * D,
    )
    return kernel_call(
        finish,
        place,
        [hidden, keep, on_ctx(to_core, CORE_SWAP)],
        [],
        [struct((16, D), BF16)],
        3 * 16 * D,
    )[0]


def solution(mesh):
    return jax.shard_map(
        shards,
        mesh=mesh,
        in_specs=(
            P("ctx", "exp"),
            P("ctx", None),
            P("ctx", None),
            P("exp", None),
            P(("ctx", "exp"), None),
            P(),
            P(("ctx", "exp"), None),
            P(("ctx", "exp"), None),
            P("exp", None, None),
            P("exp", None, None),
            P("exp", None, None),
        ),
        out_specs=P(("ctx", "exp"), None),
        check_vma=False,
    )
```

```python
import math

import jax
import jax.numpy as jnp
from jax import lax
from jax.experimental import pallas as pl
from jax.experimental.pallas import tpu as pltpu
from jax.sharding import PartitionSpec as P

D = 2048
HEAD_DIM = 128
FF = 768
TOP = 8
HEADS = 16
KV_HEADS = 2
EXPERTS = 16
TOK_C = 256
TOK_DEV = 16
NEGATIVE = -1e30
SCALE = math.log2(math.e) / math.sqrt(HEAD_DIM)
F32 = jnp.float32
BF16 = jnp.bfloat16

CORE_SWAP = [(i, i ^ 1) for i in range(16)]
Y_SWAP = [(i, i ^ 8) for i in range(16)]


ROW_SWAP = [(i, i ^ 8) for i in range(16)]


def x_shift(step):
    return [(i, i // 8 * 8 + (i // 2 + step) % 4 * 2 + i % 2) for i in range(16)]


def z_shift(step):
    return [(y * 8 + z, y * 8 + (z + step) % 8) for y in range(2) for z in range(8)]


def on_ctx(block, route):
    return lax.ppermute(block, "ctx", route)


def on_exp(block, route):
    return lax.ppermute(block, "exp", route)


def kernel_call(
    body, scalars, resident, fetched, out_shapes, flops, transcendentals=0, limit=10, idle=(), scratch=()
):
    ins = [*resident, *fetched, *idle]
    n_res, n_fetch = len(resident), len(fetched)
    n_out = len(jax.tree.leaves(out_shapes))

    def whole(*refs):
        place, refs = refs[0], refs[1:]
        sources = refs[n_res : n_res + n_fetch]
        outs = refs[len(ins) : len(ins) + n_out]
        buffers = refs[len(ins) + n_out : len(ins) + n_out + n_fetch]
        copies = []
        for n in range(n_fetch):
            copies.append(
                pltpu.make_async_copy(sources[n], buffers[n], refs[len(ins) + n_out + n_fetch + n])
            )
        for copy in copies:
            copy.start()
        extra = refs[len(ins) + n_out + 2 * n_fetch :]
        body(place, refs[:n_res], buffers, (*outs, *extra), lambda n: copies[n].wait())

    size = sum(a.size * a.dtype.itemsize for a in [*resident, *fetched])
    vmem = pl.BlockSpec(memory_space=pltpu.VMEM)
    return pl.pallas_call(
        whole,
        out_shape=out_shapes,
        in_specs=[pl.BlockSpec(memory_space=pltpu.SMEM)]
        + [vmem] * n_res
        + [pl.BlockSpec(memory_space=pltpu.HBM)] * n_fetch
        + [vmem] * len(idle),
        out_specs=jax.tree.map(lambda _: vmem, out_shapes),
        scratch_shapes=[pltpu.VMEM(a.shape, a.dtype) for a in fetched]
        + [pltpu.SemaphoreType.DMA] * n_fetch
        + list(scratch),
        compiler_params=pltpu.CompilerParams(vmem_limit_bytes=limit * 1024 * 1024),
        cost_estimate=pl.CostEstimate(
            flops=flops, bytes_accessed=size, transcendentals=transcendentals
        ),
    )(scalars, *ins)


def after(value, *earlier):
    return lax.optimization_barrier((value, *earlier))


def struct(shape, dtype):
    return jax.ShapeDtypeStruct(shape, dtype)


ROWS_TILE = 256
DISTANCES = (0, -1, 1, 2)


def attend_all(place, resident, fetched, outs, wait):
    core, y, z, ctx = place[0], place[1], place[2], place[3]
    row, x = ctx // 8, lax.rem(ctx // 2, 4)
    sources = [(row ^ r) * 8 + lax.rem(x + d + 4, 4) * 2 + core for d in DISTANCES for r in (0, 1)]
    half = resident[0].shape[0]
    token = lax.broadcasted_iota(jnp.int32, (ROWS_TILE, 1), 0) & 127
    part = token >> 4
    key = lax.broadcasted_iota(jnp.int32, (1, TOK_C), 1)
    lane = lax.broadcasted_iota(jnp.int32, (ROWS_TILE, HEAD_DIM), 1)
    blocks = [ref.at[pl.ds(r * TOK_C, TOK_C)] for ref in resident[2:] for r in (0, 1)]
    for n, q_ref in enumerate(resident[:2]):
        q_ctx = ctx ^ n
        first = z + 7 - (core ^ n)
        local = (part >> 2) * 128 + (((part & 3) + first) & 7) * 16 + (token & 15)

        def rows(i, _, n=n, q_ref=q_ref, q_ctx=q_ctx, local=local):
            at = pl.ds(pl.multiple_of(i * ROWS_TILE, ROWS_TILE), ROWS_TILE)
            ahead = key - local
            queries = q_ref[at, :]
            parts = []
            for source, ref in zip(sources, blocks):
                scores = lax.dot_general(
                    queries,
                    ref[:, :HEAD_DIM],
                    (((1,), (1,)), ((), ())),
                    preferred_element_type=F32,
                )
                parts.append(
                    jnp.where(ahead <= (q_ctx - source) * TOK_C, scores, F32(NEGATIVE))
                )
            top = parts[0]
            for part in parts[1:]:
                top = jnp.maximum(top, part)
            top = jnp.max(top, axis=1, keepdims=True)
            total, mixed = 0.0, 0.0
            for part, ref in zip(parts, blocks):
                weights = jnp.exp2((part - top) * SCALE)
                total = total + weights
                mixed = mixed + jnp.dot(
                    weights.astype(BF16), ref[:, HEAD_DIM:], preferred_element_type=F32
                )
            total = jnp.sum(total, axis=1, keepdims=True)
            outs[n][at, :HEAD_DIM] = mixed
            outs[n][at, HEAD_DIM:] = jnp.where(lane < 64, top, total)
            return 0

        lax.fori_loop(0, half // ROWS_TILE, rows, 0)


def project(place, resident, fetched, outs, wait):
    own_ref, other_ref, *part_refs = resident
    (w_own_ref,) = fetched
    keep_ref, *send_refs, attn_ref = outs
    core, row = place[0], place[3] // 8
    own_top = own_ref[:, HEAD_DIM : HEAD_DIM + 1]
    other_top = other_ref[:, HEAD_DIM : HEAD_DIM + 1]
    top = jnp.maximum(own_top, other_top)
    own_factor = jnp.exp2((own_top - top) * SCALE)
    other_factor = jnp.exp2((other_top - top) * SCALE)
    total = own_ref[:, HEAD_DIM + 64 : HEAD_DIM + 65] * own_factor
    total = total + other_ref[:, HEAD_DIM + 64 : HEAD_DIM + 65] * other_factor
    mixed = own_ref[:, :HEAD_DIM] * own_factor + other_ref[:, :HEAD_DIM] * other_factor
    attn_ref[...] = (mixed / total).astype(BF16)

    def ordered(head):
        pieces = []
        for low, high in ((1, 2), (0, 1), (2, 3), (3, 0)):
            for half in range(2):
                start = head * 128 + half * 64 + jnp.where(core == 0, low, high) * 16
                pieces.append(attn_ref[pl.ds(pl.multiple_of(start, 16), 16), :])
        return jnp.concatenate(pieces, axis=0)

    heads = [ordered(0), ordered(1)]
    width = D // 4
    wait(0)
    for n, w_ref in enumerate(part_refs):
        column = ((core ^ (n // 2)) * 2 + (row ^ (n % 2))) * width
        at = pl.ds(pl.multiple_of(column, width), width)
        sums = jnp.dot(heads[0], w_own_ref[:, at], preferred_element_type=F32)
        sums = sums + jnp.dot(heads[1], w_ref[:, HEAD_DIM:], preferred_element_type=F32)
        keep_ref[:, at] = sums[:32]
        for s in range(3):
            send_refs[s][:, at] = sums[(s + 1) * 32 : (s + 2) * 32].astype(BF16)


def add_up(place, resident, fetched, outs, wait):
    sums = resident[0][...]
    for ref in resident[1:]:
        sums = sums + ref[...].astype(F32)
    outs[0][...] = sums
    outs[1][...] = sums.astype(BF16)


def normalise(place, resident, fetched, outs, wait):
    own_ref, sums_ref, gain_ref, y_ref, core_ref, both_ref = resident[:6]
    sums_y_ref, sums_core_ref, sums_both_ref = resident[6:]
    hidden_ref, normed_ref = outs
    y = place[1]
    for n in range(4):
        at = pl.ds(n % 2 * 16, 16)
        to = pl.ds(n * 16, 16)
        here, there = (own_ref, y_ref) if n < 2 else (core_ref, both_ref)
        extended = jnp.where(y == n % 2, here[...].astype(F32), there[...].astype(F32))
        if n < 2:
            projected = sums_ref[at, :] + sums_y_ref[at, :].astype(F32)
        else:
            projected = sums_core_ref[at, :].astype(F32) + sums_both_ref[at, :].astype(F32)
        hidden = (extended[:, :D] + projected).astype(BF16)
        wide = hidden.astype(F32)
        inverse = lax.rsqrt(jnp.mean(wide * wide, axis=-1, keepdims=True) + 1e-06)
        normed = (wide * inverse * gain_ref[...].astype(F32)).astype(BF16)
        if n < 2:
            hidden_ref[at, :] = hidden
        normed_ref[to, :D] = normed
        normed_ref[to, D:] = extended[:, D:].astype(BF16)


def early(place, resident, fetched, outs, wait):
    outs[0][...] = resident[0][:16, :128]


def expert(place, resident, fetched, outs, wait):
    gate_ref, up_ref, down_ref, *inputs = resident
    keep_ref, give_ref = outs
    y, z = place[1], place[2]
    rows = [ref[:, :D] for ref in inputs]
    weights = [ref[:, D:] for ref in inputs]
    rows = rows[0] if len(rows) == 1 else jnp.concatenate(rows, axis=0)
    weights = weights[0] if len(weights) == 1 else jnp.concatenate(weights, axis=0)
    lane = lax.broadcasted_iota(jnp.int32, weights.shape, 1)
    weight = jnp.where(lane == y * 8 + z, weights.astype(F32), 0.0)
    weight = jnp.sum(weight, axis=1, keepdims=True)
    gate_part = jnp.dot(rows, gate_ref[...], preferred_element_type=F32)
    up_part = jnp.dot(rows, up_ref[...], preferred_element_type=F32)
    inner = (gate_part * jax.nn.sigmoid(gate_part) * up_part).astype(BF16)
    result = jnp.dot(inner, down_ref[...], preferred_element_type=F32).astype(BF16)
    result = result.astype(F32) * weight
    for n in range(rows.shape[0] // 32):
        at = pl.ds(n * 16, 16)
        low, high = result[n * 32 : n * 32 + 16], result[n * 32 + 16 : n * 32 + 32]
        keep_ref[at, :] = jnp.where(y == 0, low, high)
        give_ref[at, :] = jnp.where(y == 0, high, low).astype(BF16)


def run_expert(place, rows, weights, idle=()):
    total = sum(r.shape[0] for r in rows)
    keep, give = kernel_call(
        expert,
        place,
        [*weights, *rows],
        [],
        [struct((total // 2, D), F32), struct((total // 2, D), BF16)],
        6 * total * D * FF,
        total * FF,
        idle=idle,
    )
    return keep, on_exp(give, Y_SWAP)


def join(place, resident, fetched, outs, wait):
    sums = resident[0][...] + resident[1][...].astype(F32)
    start = 0
    for out in outs:
        out[...] = sums[start : start + out.shape[0]].astype(out.dtype)
        start += out.shape[0]


def run_join(place, keep, got, outs):
    return kernel_call(join, place, [keep, got], [], outs, keep.size)


def gather_theirs(place, resident, fetched, outs, wait):
    theirs = 0.0
    for ref in resident:
        theirs = theirs + ref[16:, :].astype(F32)
    outs[0][...] = theirs.astype(BF16)


def finish(place, resident, fetched, outs, wait):
    hidden_ref, own_ref, got_ref, opposite_ref, *near_refs = resident
    hidden = jnp.where(
        place[1] == 0, hidden_ref[:16, :].astype(F32), hidden_ref[16:, :].astype(F32)
    )
    moe = own_ref[...] + got_ref[...].astype(F32) + opposite_ref[...].astype(F32)
    for ref in near_refs:
        moe = moe + ref[:16, :].astype(F32)
    outs[0][...] = (hidden + moe).astype(BF16)


def router_weights(ids, gates):
    name = jnp.arange(128, dtype=jnp.int32)[None, :]
    weights = jnp.zeros((ids.shape[0], 128), BF16)
    for k in range(TOP):
        weights = jnp.where(ids[:, k : k + 1] == name, gates[:, k : k + 1], weights)
    return weights


def by_core(step):
    route = []
    for c in range(16):
        way = step if c % 2 == 0 else -step
        for e in range(16):
            route.append((c * 16 + e, c * 16 + e // 8 * 8 + (e + way) % 8))
    return route


def on_both(block, route):
    return lax.ppermute(block, ("ctx", "exp"), route)


def two_swaps(ctx_bit, exp_bit):
    return [
        (c * 16 + e, (c ^ ctx_bit) * 16 + (e ^ exp_bit)) for c in range(16) for e in range(16)
    ]


def to_three(to_y, to_core, to_both):
    return (
        on_exp(to_y, Y_SWAP),
        on_ctx(to_core, CORE_SWAP),
        on_both(to_both, two_swaps(1, 8)),
    )


def shards(
    query,
    keys,
    values,
    out_proj,
    residual,
    norm_gain,
    expert_ids,
    gate_values,
    w_gate,
    w_up,
    w_down,
):
    ctx, exp = lax.axis_index("ctx"), lax.axis_index("exp")
    core, row, y, z = ctx % 2, ctx // 8, exp // 8, exp % 8
    place = jnp.stack([core, y, z, ctx]).astype(jnp.int32)
    kv_index = exp // (HEADS // KV_HEADS)
    block = jnp.concatenate(
        [
            lax.dynamic_slice_in_dim(keys, kv_index * HEAD_DIM, HEAD_DIM, 1),
            lax.dynamic_slice_in_dim(values, kv_index * HEAD_DIM, HEAD_DIM, 1),
        ],
        axis=1,
    )

    other = on_ctx(block, ROW_SWAP)
    rows, other = after(residual, other)
    pair = jnp.concatenate([block, other], axis=0)
    blocks = [pair] + [on_ctx(pair, x_shift(-d)) for d in DISTANCES[1:]]

    by_holder = query.reshape(2, 8, TOK_DEV, HEAD_DIM)
    by_holder = jnp.concatenate([by_holder, by_holder], axis=1)

    def rows_of(first):
        return lax.dynamic_slice_in_dim(by_holder, first % 8, 4, 1).reshape(128, HEAD_DIM)

    first = z + 7 - core
    quarter = D // 4
    w_part = lax.dynamic_slice_in_dim(out_proj, (core * 2 + row) * quarter, quarter, 1)
    part = on_exp(jnp.concatenate([rows_of(first + 4), w_part], axis=1), z_shift(4))
    mine = jnp.concatenate([rows_of(first), part[:, :HEAD_DIM]], axis=0)
    theirs = on_ctx(mine, CORE_SWAP)
    part_row = on_ctx(part, ROW_SWAP)
    w_parts = [part, part_row, on_ctx(part, CORE_SWAP), on_ctx(part_row, CORE_SWAP)]

    extended = jnp.concatenate([rows, router_weights(expert_ids, gate_values)], axis=1)
    extended_y = on_exp(extended, Y_SWAP)
    mine, extended_y = after(mine, extended_y)
    extended_others = [extended_y, on_ctx(extended, CORE_SWAP), on_ctx(extended_y, CORE_SWAP)]

    own, swap = kernel_call(
        attend_all,
        place,
        [mine, theirs, *blocks],
        [],
        [struct((256, 256), F32)] * 2,
        4 * 512 * 2048 * HEAD_DIM,
        512 * 2048,
    )
    joined = on_ctx(swap, CORE_SWAP)
    joined, *extended_others = after(joined, *extended_others)
    keep, *sends = kernel_call(
        project,
        place,
        [own, joined, *w_parts],
        [out_proj],
        [struct((32, D), F32)] + [struct((32, D), BF16)] * 3,
        2 * 128 * 256 * D,
        scratch=[pltpu.VMEM((256, HEAD_DIM), BF16)],
    )
    recvs = [
        on_exp(sends[0], z_shift(-1)),
        on_exp(sends[1], z_shift(1)),
        on_both(sends[2], by_core(2)),
    ]
    sums, send = kernel_call(
        add_up,
        place,
        [keep, *recvs],
        [],
        [struct((32, D), F32), struct((32, D), BF16)],
        3 * 32 * D,
    )
    sums_y = on_exp(send, Y_SWAP)
    sums_others = [sums_y, on_ctx(send, CORE_SWAP), on_ctx(sums_y, CORE_SWAP)]
    hidden, round_0 = kernel_call(
        normalise,
        place,
        [extended, sums, norm_gain.reshape(1, D), *extended_others, *sums_others],
        [],
        [struct((32, D), BF16), struct((64, D + 128), BF16)],
        16 * 32 * D,
    )

    half = struct((32, D), BF16)
    w = [w_gate[0], w_up[0], w_down[0]]
    round_2 = on_both(round_0, by_core(2))
    round_1 = on_both(round_0, by_core(1))
    (seen,) = kernel_call(
        early, place, [round_0], [], [struct((16, 128), BF16)], 16 * 128, idle=w
    )
    round_2, seen = after(round_2, seen)
    round_3 = on_both(round_2, by_core(1))
    round_4 = on_both(round_2[:32], by_core(2))
    keep, got = run_expert(place, [round_1, round_2, round_0[:32]], w, [seen])
    keep_far, got_far = run_expert(place, [round_3, round_4], w)
    sum_1, sum_2, own_sum = run_join(place, keep, got, [half, half, struct((16, D), F32)])
    back_1 = on_both(sum_1, by_core(-1))
    back_2 = on_both(sum_2, by_core(-2))
    sum_3, sum_4 = run_join(place, keep_far, got_far, [half, struct((16, D), BF16)])
    back_3 = on_both(sum_3, by_core(-3))
    back_4 = on_exp(sum_4, z_shift(4))
    near = [back_1, back_2, back_3]
    (theirs,) = kernel_call(
        gather_theirs, place, near, [], [struct((16, D), BF16)], 3 * 16 * D
    )
    return kernel_call(
        finish,
        place,
        [hidden, own_sum, on_ctx(theirs, CORE_SWAP), back_4, *near],
        [],
        [struct((16, D), BF16)],
        7 * 16 * D,
    )[0]


def solution(mesh):
    return jax.shard_map(
        shards,
        mesh=mesh,
        in_specs=(
            P("ctx", "exp"),
            P("ctx", None),
            P("ctx", None),
            P("exp", None),
            P(("ctx", "exp"), None),
            P(),
            P(("ctx", "exp"), None),
            P(("ctx", "exp"), None),
            P("exp", None, None),
            P("exp", None, None),
            P("exp", None, None),
        ),
        out_specs=P(("ctx", "exp"), None),
        check_vma=False,
    )
```

```python
import math

import jax
import jax.numpy as jnp
from jax import lax
from jax.experimental import pallas as pl
from jax.experimental.pallas import tpu as pltpu
from jax.sharding import PartitionSpec as P

D = 2048
HEAD_DIM = 128
FF = 768
TOP = 8
HEADS = 16
KV_HEADS = 2
EXPERTS = 16
TOK_C = 256
TOK_DEV = 16
NEGATIVE = -1e30
SCALE = math.log2(math.e) / math.sqrt(HEAD_DIM)
F32 = jnp.float32
BF16 = jnp.bfloat16

CORE_SWAP = [(i, i ^ 1) for i in range(16)]
Y_SWAP = [(i, i ^ 8) for i in range(16)]


ROW_SWAP = [(i, i ^ 8) for i in range(16)]


def x_shift(step):
    return [(i, i // 8 * 8 + (i // 2 + step) % 4 * 2 + i % 2) for i in range(16)]


def z_shift(step):
    return [(y * 8 + z, y * 8 + (z + step) % 8) for y in range(2) for z in range(8)]


def on_ctx(block, route):
    return lax.ppermute(block, "ctx", route)


def on_exp(block, route):
    return lax.ppermute(block, "exp", route)


def kernel_call(
    body, scalars, resident, fetched, out_shapes, flops, transcendentals=0, limit=10, idle=(), scratch=()
):
    ins = [*resident, *fetched, *idle]
    n_res, n_fetch = len(resident), len(fetched)
    n_out = len(jax.tree.leaves(out_shapes))

    def whole(*refs):
        place, refs = refs[0], refs[1:]
        sources = refs[n_res : n_res + n_fetch]
        outs = refs[len(ins) : len(ins) + n_out]
        buffers = refs[len(ins) + n_out : len(ins) + n_out + n_fetch]
        copies = []
        for n in range(n_fetch):
            copies.append(
                pltpu.make_async_copy(sources[n], buffers[n], refs[len(ins) + n_out + n_fetch + n])
            )
        for copy in copies:
            copy.start()
        extra = refs[len(ins) + n_out + 2 * n_fetch :]
        body(place, refs[:n_res], buffers, (*outs, *extra), lambda n: copies[n].wait())

    size = sum(a.size * a.dtype.itemsize for a in [*resident, *fetched])
    vmem = pl.BlockSpec(memory_space=pltpu.VMEM)
    return pl.pallas_call(
        whole,
        out_shape=out_shapes,
        in_specs=[pl.BlockSpec(memory_space=pltpu.SMEM)]
        + [vmem] * n_res
        + [pl.BlockSpec(memory_space=pltpu.HBM)] * n_fetch
        + [vmem] * len(idle),
        out_specs=jax.tree.map(lambda _: vmem, out_shapes),
        scratch_shapes=[pltpu.VMEM(a.shape, a.dtype) for a in fetched]
        + [pltpu.SemaphoreType.DMA] * n_fetch
        + list(scratch),
        compiler_params=pltpu.CompilerParams(vmem_limit_bytes=limit * 1024 * 1024),
        cost_estimate=pl.CostEstimate(
            flops=flops, bytes_accessed=size, transcendentals=transcendentals
        ),
    )(scalars, *ins)


def after(value, *earlier):
    return lax.optimization_barrier((value, *earlier))


def struct(shape, dtype):
    return jax.ShapeDtypeStruct(shape, dtype)


ROWS_TILE = 256
DISTANCES = (0, -1, 1, 2)


def attend_all(place, resident, fetched, outs, wait):
    core, y, z, ctx = place[0], place[1], place[2], place[3]
    row, x = ctx // 8, lax.rem(ctx // 2, 4)
    sources = [(row ^ r) * 8 + lax.rem(x + d + 4, 4) * 2 + core for d in DISTANCES for r in (0, 1)]
    half = resident[0].shape[0]
    token = lax.broadcasted_iota(jnp.int32, (ROWS_TILE, 1), 0) & 127
    part = token >> 4
    key = lax.broadcasted_iota(jnp.int32, (1, TOK_C), 1)
    lane = lax.broadcasted_iota(jnp.int32, (ROWS_TILE, HEAD_DIM), 1)
    blocks = [ref.at[pl.ds(r * TOK_C, TOK_C)] for ref in resident[2:] for r in (0, 1)]
    for n, q_ref in enumerate(resident[:2]):
        q_ctx = ctx ^ n
        first = z + 7 - (core ^ n)
        local = (part >> 2) * 128 + (((part & 3) + first) & 7) * 16 + (token & 15)

        def rows(i, _, n=n, q_ref=q_ref, q_ctx=q_ctx, local=local):
            at = pl.ds(pl.multiple_of(i * ROWS_TILE, ROWS_TILE), ROWS_TILE)
            ahead = key - local
            queries = q_ref[at, :]
            parts = []
            for source, ref in zip(sources, blocks):
                scores = lax.dot_general(
                    queries,
                    ref[:, :HEAD_DIM],
                    (((1,), (1,)), ((), ())),
                    preferred_element_type=F32,
                )
                parts.append(
                    jnp.where(ahead <= (q_ctx - source) * TOK_C, scores, F32(NEGATIVE))
                )
            top = parts[0]
            for part in parts[1:]:
                top = jnp.maximum(top, part)
            top = jnp.max(top, axis=1, keepdims=True)
            total, mixed = 0.0, 0.0
            for part, ref in zip(parts, blocks):
                weights = jnp.exp2((part - top) * SCALE)
                total = total + weights
                mixed = mixed + jnp.dot(
                    weights.astype(BF16), ref[:, HEAD_DIM:], preferred_element_type=F32
                )
            total = jnp.sum(total, axis=1, keepdims=True)
            outs[n][at, :HEAD_DIM] = mixed
            outs[n][at, HEAD_DIM:] = jnp.where(lane < 64, top, total)
            return 0

        lax.fori_loop(0, half // ROWS_TILE, rows, 0)


def project(place, resident, fetched, outs, wait):
    own_ref, other_ref, *part_refs = resident
    (w_own_ref,) = fetched
    keep_ref, *send_refs, attn_ref = outs
    core, row = place[0], place[3] // 8
    own_top = own_ref[:, HEAD_DIM : HEAD_DIM + 1]
    other_top = other_ref[:, HEAD_DIM : HEAD_DIM + 1]
    top = jnp.maximum(own_top, other_top)
    own_factor = jnp.exp2((own_top - top) * SCALE)
    other_factor = jnp.exp2((other_top - top) * SCALE)
    total = own_ref[:, HEAD_DIM + 64 : HEAD_DIM + 65] * own_factor
    total = total + other_ref[:, HEAD_DIM + 64 : HEAD_DIM + 65] * other_factor
    mixed = own_ref[:, :HEAD_DIM] * own_factor + other_ref[:, :HEAD_DIM] * other_factor
    attn_ref[...] = (mixed / total).astype(BF16)

    def ordered(head):
        pieces = []
        for low, high in ((1, 2), (0, 1), (2, 3), (3, 0)):
            for half in range(2):
                start = head * 128 + half * 64 + jnp.where(core == 0, low, high) * 16
                pieces.append(attn_ref[pl.ds(pl.multiple_of(start, 16), 16), :])
        return jnp.concatenate(pieces, axis=0)

    heads = [ordered(0), ordered(1)]
    width = D // 4
    wait(0)
    for n, w_ref in enumerate(part_refs):
        column = ((core ^ (n // 2)) * 2 + (row ^ (n % 2))) * width
        at = pl.ds(pl.multiple_of(column, width), width)
        sums = jnp.dot(heads[0], w_own_ref[:, at], preferred_element_type=F32)
        sums = sums + jnp.dot(heads[1], w_ref[:, HEAD_DIM:], preferred_element_type=F32)
        keep_ref[:, at] = sums[:32]
        for s in range(3):
            send_refs[s][:, at] = sums[(s + 1) * 32 : (s + 2) * 32].astype(BF16)


def add_up(place, resident, fetched, outs, wait):
    sums = resident[0][...]
    for ref in resident[1:]:
        sums = sums + ref[...].astype(F32)
    outs[0][...] = sums
    outs[1][...] = sums.astype(BF16)


def normalise(place, resident, fetched, outs, wait):
    own_ref, sums_ref, gain_ref, y_ref, core_ref, both_ref = resident[:6]
    sums_y_ref, sums_core_ref, sums_both_ref = resident[6:]
    hidden_ref, normed_ref = outs
    y = place[1]
    for n in range(4):
        at = pl.ds(n % 2 * 16, 16)
        to = pl.ds(n * 16, 16)
        here, there = (own_ref, y_ref) if n < 2 else (core_ref, both_ref)
        extended = jnp.where(y == n % 2, here[...].astype(F32), there[...].astype(F32))
        if n < 2:
            projected = sums_ref[at, :] + sums_y_ref[at, :].astype(F32)
        else:
            projected = sums_core_ref[at, :].astype(F32) + sums_both_ref[at, :].astype(F32)
        hidden = (extended[:, :D] + projected).astype(BF16)
        wide = hidden.astype(F32)
        inverse = lax.rsqrt(jnp.mean(wide * wide, axis=-1, keepdims=True) + 1e-06)
        normed = (wide * inverse * gain_ref[...].astype(F32)).astype(BF16)
        if n < 2:
            hidden_ref[at, :] = hidden
        normed_ref[to, :D] = normed
        normed_ref[to, D:] = extended[:, D:].astype(BF16)


def early(place, resident, fetched, outs, wait):
    outs[0][...] = resident[0][:16, :128]


def expert(place, resident, fetched, outs, wait):
    gate_ref, up_ref, down_ref, *inputs = resident
    keep_ref, give_ref = outs
    y, z = place[1], place[2]
    rows = [ref[:, :D] for ref in inputs]
    weights = [ref[:, D:] for ref in inputs]
    rows = rows[0] if len(rows) == 1 else jnp.concatenate(rows, axis=0)
    weights = weights[0] if len(weights) == 1 else jnp.concatenate(weights, axis=0)
    lane = lax.broadcasted_iota(jnp.int32, weights.shape, 1)
    weight = jnp.where(lane == y * 8 + z, weights.astype(F32), 0.0)
    weight = jnp.sum(weight, axis=1, keepdims=True)
    gate_part = jnp.dot(rows, gate_ref[...], preferred_element_type=F32)
    up_part = jnp.dot(rows, up_ref[...], preferred_element_type=F32)
    inner = (gate_part * jax.nn.sigmoid(gate_part) * up_part).astype(BF16)
    result = jnp.dot(inner, down_ref[...], preferred_element_type=F32).astype(BF16)
    result = result.astype(F32) * weight
    for n in range(rows.shape[0] // 32):
        at = pl.ds(n * 16, 16)
        low, high = result[n * 32 : n * 32 + 16], result[n * 32 + 16 : n * 32 + 32]
        keep_ref[at, :] = jnp.where(y == 0, low, high)
        give_ref[at, :] = jnp.where(y == 0, high, low).astype(BF16)


def run_expert(place, rows, weights, idle=()):
    total = sum(r.shape[0] for r in rows)
    keep, give = kernel_call(
        expert,
        place,
        [*weights, *rows],
        [],
        [struct((total // 2, D), F32), struct((total // 2, D), BF16)],
        6 * total * D * FF,
        total * FF,
        idle=idle,
    )
    return keep, on_exp(give, Y_SWAP)


def join(place, resident, fetched, outs, wait):
    sums = resident[0][...] + resident[1][...].astype(F32)
    start = 0
    for out in outs:
        out[...] = sums[start : start + out.shape[0]].astype(out.dtype)
        start += out.shape[0]


def run_join(place, keep, got, outs):
    return kernel_call(join, place, [keep, got], [], outs, keep.size)


def gather_theirs(place, resident, fetched, outs, wait):
    theirs = 0.0
    for ref in resident:
        theirs = theirs + ref[16:, :].astype(F32)
    outs[0][...] = theirs.astype(BF16)


def finish(place, resident, fetched, outs, wait):
    hidden_ref, own_ref, got_ref, opposite_ref, *near_refs = resident
    hidden = jnp.where(
        place[1] == 0, hidden_ref[:16, :].astype(F32), hidden_ref[16:, :].astype(F32)
    )
    moe = own_ref[...] + got_ref[...].astype(F32) + opposite_ref[...].astype(F32)
    for ref in near_refs:
        moe = moe + ref[:16, :].astype(F32)
    outs[0][...] = (hidden + moe).astype(BF16)


def router_weights(ids, gates):
    name = jnp.arange(128, dtype=jnp.int32)[None, :]
    weights = jnp.zeros((ids.shape[0], 128), BF16)
    for k in range(TOP):
        weights = jnp.where(ids[:, k : k + 1] == name, gates[:, k : k + 1], weights)
    return weights


def by_core(step):
    route = []
    for c in range(16):
        way = step if c % 2 == 0 else -step
        for e in range(16):
            route.append((c * 16 + e, c * 16 + e // 8 * 8 + (e + way) % 8))
    return route


def on_both(block, route):
    return lax.ppermute(block, ("ctx", "exp"), route)


def two_swaps(ctx_bit, exp_bit):
    return [
        (c * 16 + e, (c ^ ctx_bit) * 16 + (e ^ exp_bit)) for c in range(16) for e in range(16)
    ]


def to_three(to_y, to_core, to_both):
    return (
        on_exp(to_y, Y_SWAP),
        on_ctx(to_core, CORE_SWAP),
        on_both(to_both, two_swaps(1, 8)),
    )


def shards(
    query,
    keys,
    values,
    out_proj,
    residual,
    norm_gain,
    expert_ids,
    gate_values,
    w_gate,
    w_up,
    w_down,
):
    ctx, exp = lax.axis_index("ctx"), lax.axis_index("exp")
    core, row, y, z = ctx % 2, ctx // 8, exp // 8, exp % 8
    place = jnp.stack([core, y, z, ctx]).astype(jnp.int32)
    kv_index = exp // (HEADS // KV_HEADS)
    block = jnp.concatenate(
        [
            lax.dynamic_slice_in_dim(keys, kv_index * HEAD_DIM, HEAD_DIM, 1),
            lax.dynamic_slice_in_dim(values, kv_index * HEAD_DIM, HEAD_DIM, 1),
        ],
        axis=1,
    )

    other = on_ctx(block, ROW_SWAP)
    rows, other = after(residual, other)
    pair = jnp.concatenate([block, other], axis=0)
    blocks = [pair] + [on_ctx(pair, x_shift(-d)) for d in DISTANCES[1:]]

    by_holder = query.reshape(2, 8, TOK_DEV, HEAD_DIM)
    by_holder = jnp.concatenate([by_holder, by_holder], axis=1)

    def rows_of(first):
        return lax.dynamic_slice_in_dim(by_holder, first % 8, 4, 1).reshape(128, HEAD_DIM)

    first = z + 7 - core
    quarter = D // 4
    w_part = lax.dynamic_slice_in_dim(out_proj, (core * 2 + row) * quarter, quarter, 1)
    part = on_exp(jnp.concatenate([rows_of(first + 4), w_part], axis=1), z_shift(4))
    mine = jnp.concatenate([rows_of(first), part[:, :HEAD_DIM]], axis=0)
    theirs = on_ctx(mine, CORE_SWAP)
    part_row = on_ctx(part, ROW_SWAP)
    w_parts = [part, part_row, on_ctx(part, CORE_SWAP), on_ctx(part_row, CORE_SWAP)]

    extended = jnp.concatenate([rows, router_weights(expert_ids, gate_values)], axis=1)
    extended_y = on_exp(extended, Y_SWAP)
    mine, extended_y = after(mine, extended_y)
    extended_others = [extended_y, on_ctx(extended, CORE_SWAP), on_ctx(extended_y, CORE_SWAP)]

    own, swap = kernel_call(
        attend_all,
        place,
        [mine, theirs, *blocks],
        [],
        [struct((256, 256), F32)] * 2,
        4 * 512 * 2048 * HEAD_DIM,
        512 * 2048,
    )
    joined = on_ctx(swap, CORE_SWAP)
    keep, *sends = kernel_call(
        project,
        place,
        [own, joined, *w_parts],
        [out_proj],
        [struct((32, D), F32)] + [struct((32, D), BF16)] * 3,
        2 * 128 * 256 * D,
        scratch=[pltpu.VMEM((256, HEAD_DIM), BF16)],
    )
    recvs = [
        on_exp(sends[0], z_shift(-1)),
        on_exp(sends[1], z_shift(1)),
        on_both(sends[2], by_core(2)),
    ]
    sums, send = kernel_call(
        add_up,
        place,
        [keep, *recvs],
        [],
        [struct((32, D), F32), struct((32, D), BF16)],
        3 * 32 * D,
    )
    sums_y = on_exp(send, Y_SWAP)
    sums_others = [sums_y, on_ctx(send, CORE_SWAP), on_ctx(sums_y, CORE_SWAP)]
    hidden, round_0 = kernel_call(
        normalise,
        place,
        [extended, sums, norm_gain.reshape(1, D), *extended_others, *sums_others],
        [],
        [struct((32, D), BF16), struct((64, D + 128), BF16)],
        16 * 32 * D,
    )

    half = struct((32, D), BF16)
    w = [w_gate[0], w_up[0], w_down[0]]
    round_2 = on_both(round_0, by_core(2))
    round_1 = on_both(round_0, by_core(1))
    (seen,) = kernel_call(
        early, place, [round_0], [], [struct((16, 128), BF16)], 16 * 128, idle=w
    )
    round_2, seen = after(round_2, seen)
    round_3 = on_both(round_2, by_core(1))
    round_4 = on_both(round_2[:32], by_core(2))
    keep, got = run_expert(place, [round_1, round_2, round_0[:32]], w, [seen])
    keep_far, got_far = run_expert(place, [round_3, round_4], w)
    sum_1, sum_2, own_sum = run_join(place, keep, got, [half, half, struct((16, D), F32)])
    back_1 = on_both(sum_1, by_core(-1))
    back_2 = on_both(sum_2, by_core(-2))
    sum_3, sum_4 = run_join(place, keep_far, got_far, [half, struct((16, D), BF16)])
    back_3 = on_both(sum_3, by_core(-3))
    back_4 = on_exp(sum_4, z_shift(4))
    near = [back_1, back_2, back_3]
    (theirs,) = kernel_call(
        gather_theirs, place, near, [], [struct((16, D), BF16)], 3 * 16 * D
    )
    return kernel_call(
        finish,
        place,
        [hidden, own_sum, on_ctx(theirs, CORE_SWAP), back_4, *near],
        [],
        [struct((16, D), BF16)],
        7 * 16 * D,
    )[0]


def solution(mesh):
    return jax.shard_map(
        shards,
        mesh=mesh,
        in_specs=(
            P("ctx", "exp"),
            P("ctx", None),
            P("ctx", None),
            P("exp", None),
            P(("ctx", "exp"), None),
            P(),
            P(("ctx", "exp"), None),
            P(("ctx", "exp"), None),
            P("exp", None, None),
            P("exp", None, None),
            P("exp", None, None),
        ),
        out_specs=P(("ctx", "exp"), None),
        check_vma=False,
    )
```
